32 devices in a mesh: dp: 4 (over x, core), row: 4 (over z), col: 2 (over y).
Axes of the slice: x: 2, y: 2, z: 4, core: 2. Of those that a mesh axis runs over, the one named last changes fastest.
Arguments:
- token_ids: int32 [4, 1024], P('dp'), may hold values from 0 to 50303
- target_ids: int32 [4, 1024], P('dp'), may hold values from 0 to 50303
- included: int32 [4], P('dp'), may hold values 0 or 1
- tok_table: float32 [50304, 768], P(('col', 'row')), may hold values from -0.4330127 to 0.4330127, as said below
- pos_table: float32 [1024, 768], P('col', 'row'), may hold values from -3 to 3
- qkv_weight: float32 [768, 2304], P('row', 'col'), may hold values from -0.21875 to 0.21875
- attn_weight: float32 [768, 768], P('row', 'col'), may hold values from -1.25 to 1.25
- up_weight: float32 [768, 3072], P('row', 'col'), may hold values from -0.21875 to 0.21875
- down_weight: float32 [768, 3072], P('col', 'row'), may hold values from -0.109375 to 0.109375
- small_params: float32 [14, 768], replicated, may hold values from -3 to 3, as said below
- table_rows: float32 [50304], P(('col', 'row')), may hold values from 1.9204263e-07 to 7.6817054e-07
- table_cols: float32 [768], replicated, may hold values from 1.9204263e-07 to 7.6817054e-07
- pos_rows: float32 [1024], P('col'), may hold values from 1.9204263e-07 to 7.6817054e-07
- pos_cols: float32 [768], P('row'), may hold values from 1.9204263e-07 to 7.6817054e-07
- qkv_rows: float32 [768], P('row'), may hold values from 1.9204263e-07 to 7.6817054e-07
- qkv_cols: float32 [2304], P('col'), may hold values from 1.9204263e-07 to 7.6817054e-07
- attn_rows: float32 [768], P('row'), may hold values from 1.9204263e-07 to 7.6817054e-07
- attn_cols: float32 [768], P('col'), may hold values from 1.9204263e-07 to 7.6817054e-07
- up_rows: float32 [768], P('row'), may hold values from 1.9204263e-07 to 7.6817054e-07
- up_cols: float32 [3072], P('col'), may hold values from 1.9204263e-07 to 7.6817054e-07
- down_rows: float32 [768], P('col'), may hold values from 1.9204263e-07 to 7.6817054e-07
- down_cols: float32 [3072], P('row'), may hold values from 1.9204263e-07 to 7.6817054e-07
- small_second: float32 [14, 768], replicated, may hold values from 3.0322522e-06 to 1.2129009e-05
- table_noise: float32 [50304, 768], P(('col', 'row')), may hold values from -6 to 6
- pos_noise: float32 [1024, 768], P('col', 'row'), may hold values from -6 to 6
- qkv_noise: float32 [768, 2304], P('row', 'col'), may hold values from -6 to 6
- attn_noise: float32 [768, 768], P('row', 'col'), may hold values from -6 to 6
- up_noise: float32 [768, 3072], P('row', 'col'), may hold values from -6 to 6
- down_noise: float32 [768, 3072], P('col', 'row'), may hold values from -6 to 6
- small_noise: float32 [14, 768], replicated, may hold values from -6 to 6
Outputs:
- table_grad: float32 [50304, 768], P(('col', 'row'))
- table_rows_new: float32 [50304], P(('col', 'row'))
- table_cols_new: float32 [768], replicated
- table_new: float32 [50304, 768], P(('col', 'row'))
- pos_grad: float32 [1024, 768], P('col', 'row')
- pos_rows_new: float32 [1024], P('col')
- pos_cols_new: float32 [768], P('row')
- pos_new: float32 [1024, 768], P('col', 'row')
- qkv_grad: float32 [768, 2304], P('row', 'col')
- qkv_rows_new: float32 [768], P('row')
- qkv_cols_new: float32 [2304], P('col')
- qkv_new: float32 [768, 2304], P('row', 'col')
- attn_grad: float32 [768, 768], P('row', 'col')
- attn_rows_new: float32 [768], P('row')
- attn_cols_new: float32 [768], P('col')
- attn_new: float32 [768, 768], P('row', 'col')
- up_grad: float32 [768, 3072], P('row', 'col')
- up_rows_new: float32 [768], P('row')
- up_cols_new: float32 [3072], P('col')
- up_new: float32 [768, 3072], P('row', 'col')
- down_grad: float32 [768, 3072], P('col', 'row')
- down_rows_new: float32 [768], P('col')
- down_cols_new: float32 [3072], P('row')
- down_new: float32 [768, 3072], P('col', 'row')
- small_grad: float32 [14, 768], replicated
- small_second_new: float32 [14, 768], replicated
- small_new: float32 [14, 768], replicated
- loss_sum: float32 [], replicated
- token_count: float32 [], replicated
- example_norms: float32 [4], P('dp')
The draws below stay inside these ranges and needn't reach their ends.
Inputs may be any that keep to these rules, and one draw needn't show every extreme that they name: `tok_table`: rows scaled by factors that differ over the vocabulary. `small_params`: gains near one, biases of both signs.
All inputs are finite; a program needn't handle non-finite values. No bound on the sum of `included` on one device may be relied on, other than what follows from the above.
Results may differ from the reference program's by a relative error of at most 0.012.
Values may be sent and summed in bfloat16 or wider, within the bound.
A program may use at most 640 MiB of HBM per device.

```python
import math
from functools import partial
import jax
import jax.numpy as jnp
import numpy as np
from jax import lax

D = 768
HEADS = 12
HEAD = 64
FF = 3072
V = 50304
LEN = 1024
STEP = 10
EXAMPLES = 4


def draw_tok_table(key, part):
    key = jax.random.fold_in(key, 11)
    ramp = jnp.arange(V, dtype=jnp.float32)[:, None] / (V - 1)
    base = jax.random.truncated_normal(key, -4.0, 4.0, (V, D), jnp.float32)
    factor = 1.0 + 2.0 * ramp
    return base * factor * D ** (-0.5)


def draw_small_params(key, part):
    key = jax.random.fold_in(key, 23)
    ramp = jnp.arange(D, dtype=jnp.float32)[None, :] / (D - 1)
    gain_rows = (jnp.arange(14)[:, None] == 0) | (jnp.arange(14)[:, None] == 5) | (jnp.arange(14)[:, None] == 12)
    rough = jax.random.truncated_normal(key, -4.0, 4.0, (14, D), jnp.float32)
    gains = (0.6 + 1.2 * ramp) * (1.0 + 0.1 * rough)
    return jnp.where(gain_rows, gains, 0.3 * rough)


def with_ends(entries, rng, least, largest):
    longest = entries.shape.index(max(entries.shape))
    spots = []
    for shift in (0, 1):
        where = [jax.random.randint(jax.random.fold_in(rng, axis), (), 0, length) for axis, length in enumerate(entries.shape)]
        where[longest] = (where[longest] + shift) % entries.shape[longest]
        spots.append(tuple(where))
    return entries.at[spots[0]].set(least).at[spots[1]].set(largest)


def level_of(stream_key, shape, shards, least, high):
    def one(axis_at, shards_of):
        steps = jax.random.uniform(jax.random.fold_in(jax.random.fold_in(stream_key, 6), axis_at), (shards_of,), jnp.float32, least / len(shards), high / len(shards))
        return jnp.repeat(jnp.exp(steps), shape[axis_at] // shards_of).reshape((-1,) + (1,) * (len(shape) - axis_at - 1))

    level = one(*shards[0])
    for cut in shards[1:]:
        level = level * one(*cut)
    return level


def rank_table(count, skew):
    portions = [(1 << 20) // math.isqrt(rank ** skew) + 1 for rank in range(1, count + 1)]
    width = 1 + sum(portions) // (1 << 30)
    return np.cumsum(np.array([max(1, weight // width) for weight in portions]))


def ranked(rng, shape, count, skew):
    grid = rank_table(count, skew)
    pick = jax.random.randint(jax.random.fold_in(rng, 1), shape, 0, int(grid[count - 1]))
    grade = jnp.searchsorted(jnp.asarray(grid, jnp.int32), pick, side="right")
    return jax.random.permutation(jax.random.fold_in(rng, 2), count)[grade].astype(jnp.int32)


def bell_draw(rng, dims, width, reach, pieces=(), kind=jnp.bfloat16):
    values = jax.random.normal(rng, dims, jnp.float32) * width
    if len(pieces) > 0:
        values = level_of(rng, dims, pieces, -0.22, 0.18) * values
    return jnp.clip(values, min=-reach, max=reach).astype(kind)


def setup_inputs(seed: int = 0) -> dict:
    keys = jax.random.split(jax.random.key(seed), 31)
    return {
        "token_ids": with_ends(ranked(keys[0], (EXAMPLES, LEN), V, 2), jax.random.fold_in(keys[0], 3), 0, V - 1).astype(jnp.int32),
        "target_ids": with_ends(ranked(keys[1], (EXAMPLES, LEN), V, 2), jax.random.fold_in(keys[1], 3), 0, V - 1).astype(jnp.int32),
        "included": with_ends((jax.random.randint(keys[2], (EXAMPLES,), 0, 2) < 1).astype(jnp.int32), jax.random.fold_in(keys[2], 1), 0, 1),
        "tok_table": draw_tok_table(jax.random.fold_in(keys[30], 71), 0),
        "pos_table": bell_draw(keys[4], (LEN, D), 0.5, 3.0, ((0, 2), (1, 4)), jnp.float32),
        "qkv_weight": bell_draw(keys[5], (D, 3 * D), D ** -0.5, 0.21875, ((0, 4), (1, 2)), jnp.float32),
        "attn_weight": bell_draw(keys[6], (D, D), (max(1, D * 32 // LEN)) ** -0.5, 1.25, ((0, 4), (1, 2)), jnp.float32),
        "up_weight": bell_draw(keys[7], (D, FF), D ** -0.5, 0.21875, ((0, 4), (1, 2)), jnp.float32),
        "down_weight": bell_draw(keys[8], (D, FF), FF ** -0.5, 0.109375, ((0, 2), (1, 4)), jnp.float32),
        "small_params": draw_small_params(jax.random.fold_in(keys[30], 71), 0),
        "table_rows": jnp.clip(jnp.exp(math.log(7.681705369577685e-07) - 1.3862944 * jax.random.uniform(keys[10], (V,), jnp.float32) ** level_of(keys[10], (V,), ((0, 8),), -0.2, 0.2)), 1.9204263423944212e-07, 7.681705369577685e-07),
        "table_cols": jnp.clip(jnp.exp(jax.random.uniform(keys[11], (D,), jnp.float32, math.log(1.9204263423944212e-07), math.log(7.681705369577685e-07))), 1.9204263423944212e-07, 7.681705369577685e-07),
        "pos_rows": jnp.clip(jnp.exp(math.log(7.681705369577685e-07) - 1.3862944 * jax.random.uniform(keys[12], (LEN,), jnp.float32) ** level_of(keys[12], (LEN,), ((0, 2),), -0.2, 0.2)), 1.9204263423944212e-07, 7.681705369577685e-07),
        "pos_cols": jnp.clip(jnp.exp(math.log(7.681705369577685e-07) - 1.3862944 * jax.random.uniform(keys[13], (D,), jnp.float32) ** level_of(keys[13], (D,), ((0, 4),), -0.2, 0.2)), 1.9204263423944212e-07, 7.681705369577685e-07),
        "qkv_rows": jnp.clip(jnp.exp(math.log(7.681705369577685e-07) - 1.3862944 * jax.random.uniform(keys[14], (D,), jnp.float32) ** level_of(keys[14], (D,), ((0, 4),), -0.2, 0.2)), 1.9204263423944212e-07, 7.681705369577685e-07),
        "qkv_cols": jnp.clip(jnp.exp(math.log(7.681705369577685e-07) - 1.3862944 * jax.random.uniform(keys[15], (3 * D,), jnp.float32) ** level_of(keys[15], (3 * D,), ((0, 2),), -0.2, 0.2)), 1.9204263423944212e-07, 7.681705369577685e-07),
        "attn_rows": jnp.clip(jnp.exp(math.log(7.681705369577685e-07) - 1.3862944 * jax.random.uniform(keys[16], (D,), jnp.float32) ** level_of(keys[16], (D,), ((0, 4),), -0.2, 0.2)), 1.9204263423944212e-07, 7.681705369577685e-07),
        "attn_cols": jnp.clip(jnp.exp(math.log(7.681705369577685e-07) - 1.3862944 * jax.random.uniform(keys[17], (D,), jnp.float32) ** level_of(keys[17], (D,), ((0, 2),), -0.2, 0.2)), 1.9204263423944212e-07, 7.681705369577685e-07),
        "up_rows": jnp.clip(jnp.exp(math.log(7.681705369577685e-07) - 1.3862944 * jax.random.uniform(keys[18], (D,), jnp.float32) ** level_of(keys[18], (D,), ((0, 4),), -0.2, 0.2)), 1.9204263423944212e-07, 7.681705369577685e-07),
        "up_cols": jnp.clip(jnp.exp(math.log(7.681705369577685e-07) - 1.3862944 * jax.random.uniform(keys[19], (FF,), jnp.float32) ** level_of(keys[19], (FF,), ((0, 2),), -0.2, 0.2)), 1.9204263423944212e-07, 7.681705369577685e-07),
        "down_rows": jnp.clip(jnp.exp(math.log(7.681705369577685e-07) - 1.3862944 * jax.random.uniform(keys[20], (D,), jnp.float32) ** level_of(keys[20], (D,), ((0, 2),), -0.2, 0.2)), 1.9204263423944212e-07, 7.681705369577685e-07),
        "down_cols": jnp.clip(jnp.exp(math.log(7.681705369577685e-07) - 1.3862944 * jax.random.uniform(keys[21], (FF,), jnp.float32) ** level_of(keys[21], (FF,), ((0, 4),), -0.2, 0.2)), 1.9204263423944212e-07, 7.681705369577685e-07),
        "small_second": jnp.clip(jnp.exp(jax.random.uniform(keys[22], (14, D), jnp.float32, math.log(3.0322521524794865e-06), math.log(1.2129008609917946e-05))), 3.0322521524794865e-06, 1.2129008609917946e-05),
        "table_noise": bell_draw(keys[23], (V, D), 1.0, 6.0, ((0, 8),), jnp.float32),
        "pos_noise": bell_draw(keys[24], (LEN, D), 1.0, 6.0, ((0, 2), (1, 4)), jnp.float32),
        "qkv_noise": bell_draw(keys[25], (D, 3 * D), 1.0, 6.0, ((0, 4), (1, 2)), jnp.float32),
        "attn_noise": bell_draw(keys[26], (D, D), 1.0, 6.0, ((0, 4), (1, 2)), jnp.float32),
        "up_noise": bell_draw(keys[27], (D, FF), 1.0, 6.0, ((0, 4), (1, 2)), jnp.float32),
        "down_noise": bell_draw(keys[28], (D, FF), 1.0, 6.0, ((0, 2), (1, 4)), jnp.float32),
        "small_noise": bell_draw(keys[29], (14, D), 1.0, 6.0, (), jnp.float32),
    }


clip_bound = 1.0
noise_mult = 0.002
sample_rate = 0.5
step_rate = 0.5
highest = lax.Precision.HIGHEST

@jax.custom_vjp
def low(v):
    return lax.optimization_barrier(v.astype(jnp.bfloat16)).astype(jnp.float32)

@jax.custom_vjp
def low_back(v):
    return v

def low_keep(v):
    return (low(v), None)

def low_pass(kept, grad):
    return (grad,)

def back_keep(v):
    return (v, None)

def back_low(kept, grad):
    return (low(grad),)
low.defvjp(low_keep, low_pass)
low_back.defvjp(back_keep, back_low)

def matmul(left, right):
    return jnp.dot(left, right, precision=highest)

def layer_norm(inputs, gain, shift):
    center = lax.optimization_barrier(jnp.mean(inputs, -1, keepdims=True))
    spread_var = lax.optimization_barrier(jnp.mean(inputs * inputs, -1, keepdims=True)) - center * center
    return (inputs - center) * lax.rsqrt(spread_var + 1e-05) * gain + shift

def example_loss(params, ids, targets):
    tok_table, pos_table, qkv_weight, attn_weight, up_weight, down_weight, small = params
    table = low(tok_table)
    start = low_back(table[ids]) + pos_table
    normed = low(layer_norm(start, small[0], small[1]))
    bias = jnp.concatenate([small[2], jnp.zeros_like(small[2]), small[3]])
    packed = low_back(low(matmul(normed, low(qkv_weight)) + bias)).reshape(LEN, 3, HEADS, HEAD)
    scores = low_back(jnp.einsum('qhe,khe->hqk', packed[:, 0], packed[:, 1], precision=highest) * HEAD ** (-0.5))
    causal = jnp.arange(LEN)[None, :] <= jnp.arange(LEN)[:, None]
    scores = jnp.where(causal[None], scores, -1e+30)
    soft_probs = low(jax.nn.softmax(scores, -1))
    mixed = jnp.einsum('hqk,khe->qhe', soft_probs, packed[:, 2], precision=highest).reshape(LEN, D)
    mixed = low_back(low(mixed))
    middle = start + low_back(matmul(mixed, low(attn_weight)) + small[4])
    inner = low(layer_norm(middle, small[5], small[6]))
    up_pre = low_back(matmul(inner, low(up_weight)) + small[7:11].reshape(FF))
    hidden = low(jax.nn.gelu(up_pre, approximate=True))
    final = middle + low_back(matmul(hidden, low(down_weight).T) + small[11])
    topped = low(layer_norm(final, small[12], small[13]))
    logits = low_back(jnp.dot(topped, table.T, precision=highest))
    picked = jnp.take_along_axis(logits, targets[:, None], 1)[:, 0]
    return jnp.sum(jax.nn.logsumexp(logits, -1) - picked)

def gradients(params, ids, targets):
    loss, pull = jax.vjp(partial(example_loss, ids=ids, targets=targets), params)
    return (loss, pull(jnp.ones((), loss.dtype))[0])

def factored(weight, grad, rows_old, cols_old, decay_rate):
    squares = grad * grad + 1e-30
    rows_new = decay_rate * rows_old + (1.0 - decay_rate) * lax.optimization_barrier(jnp.mean(squares, 1))
    cols_new = decay_rate * cols_old + (1.0 - decay_rate) * lax.optimization_barrier(jnp.mean(squares, 0))
    update = grad * lax.rsqrt(rows_new[:, None] * cols_new[None, :] / jnp.mean(rows_new))
    update = update / jnp.maximum(1.0, jnp.sqrt(jnp.mean(update * update)))
    size = step_rate * jnp.maximum(0.001, jnp.sqrt(jnp.mean(weight * weight)))
    return (grad, rows_new, cols_new, weight - size * update)

def reference(token_ids, target_ids, included, tok_table, pos_table, qkv_weight, attn_weight, up_weight, down_weight, small_params, table_rows, table_cols, pos_rows, pos_cols, qkv_rows, qkv_cols, attn_rows, attn_cols, up_rows, up_cols, down_rows, down_cols, small_second, table_noise, pos_noise, qkv_noise, attn_noise, up_noise, down_noise, small_noise):
    params = (tok_table, pos_table, qkv_weight, attn_weight, up_weight, down_weight, small_params)

    def measure(pair):
        loss, grads = gradients(params, pair[0], pair[1])
        return (loss, sum((jnp.sum(item * item) for item in grads)))
    losses, squares = lax.map(measure, (token_ids, target_ids))
    example_norms = jnp.sqrt(squares)
    taken = included.astype(jnp.float32)
    share = taken * jnp.minimum(1.0, clip_bound * lax.rsqrt(squares + 1e-12))

    def accumulate(carry, item):
        grads = gradients(params, item[0], item[1])[1]
        return (tuple((total + item[2] * piece for total, piece in zip(carry, grads))), None)
    start = tuple((jnp.zeros_like(item) for item in params))
    summed, unused = lax.scan(accumulate, start, (token_ids, target_ids, share))
    noises = (table_noise, pos_noise, qkv_noise, attn_noise, up_noise, down_noise, small_noise)
    grads = [(total + noise_mult * clip_bound * noise) / (sample_rate * EXAMPLES) for total, noise in zip(summed, noises)]
    decay_rate = 1.0 - STEP ** (-0.8)
    states = ((table_rows, table_cols), (pos_rows, pos_cols), (qkv_rows, qkv_cols), (attn_rows, attn_cols), (up_rows, up_cols), (down_rows, down_cols))
    outputs = []
    for index in range(6):
        outputs.extend(factored(params[index], grads[index], states[index][0], states[index][1], decay_rate))
    small_grad = grads[6]
    second_new = decay_rate * small_second + (1.0 - decay_rate) * (small_grad * small_grad + 1e-30)
    update = small_grad * lax.rsqrt(second_new)
    update = update / jnp.maximum(1.0, jnp.sqrt(jnp.mean(update * update)))
    small_new = small_params - step_rate * jnp.maximum(0.001, jnp.sqrt(jnp.mean(small_params * small_params))) * update
    loss_sum = jnp.sum(taken * losses)
    token_count = jnp.sum(taken) * LEN
    return (outputs[0], outputs[1], outputs[2], outputs[3], outputs[4], outputs[5], outputs[6], outputs[7], outputs[8], outputs[9], outputs[10], outputs[11], outputs[12], outputs[13], outputs[14], outputs[15], outputs[16], outputs[17], outputs[18], outputs[19], outputs[20], outputs[21], outputs[22], outputs[23], small_grad, second_new, small_new, loss_sum, token_count, example_norms)
```

```python
import functools

import jax
import jax.numpy as jnp
from jax import lax
from jax.experimental import pallas as pl
from jax.experimental.pallas import tpu as pltpu
from jax.sharding import PartitionSpec as P

HEADS = 12
HEAD = 64
STEP = 10
CLIP = 1.0
NOISE = 0.002
SAMPLE = 0.5
RATE = 0.5
DECAY = 1.0 - STEP ** (-0.8)

F32 = jnp.float32
BF16 = jnp.bfloat16
PLANE = ("row", "col")
MESH = pl.DeviceIdType.MESH


def dot_f32(left, right, dims):
    return lax.dot_general(left, right, (dims, ((), ())), preferred_element_type=F32)


def mm(left, right):
    return dot_f32(left, right, ((1,), (0,)))


def mm_nt(left, right):
    return dot_f32(left, right, ((1,), (1,)))


def mm_tn(left, right):
    return dot_f32(left, right, ((0,), (0,)))


def gather_matrix(block, row_dim):
    part = lax.all_gather(block, "row", axis=row_dim, tiled=True)
    return lax.all_gather(part, "col", axis=1 - row_dim, tiled=True)


def plane_sum(array):
    return lax.psum(array, PLANE)


def example_sum(array):
    return lax.psum(array, "dp")


class Link:
    def __init__(self, send_sems, recv_sems):
        self.dp, self.row, self.col = (lax.axis_index(axis) for axis in ("dp", "row", "col"))
        self.x, self.core = self.dp // 2, self.dp % 2
        self.beside = 2 * (1 - self.x) + self.core
        self.sibling = 2 * self.x + 1 - self.core
        self.send_sems, self.recv_sems = send_sems, recv_sems
        self.n_send = 0
        self.open = []

    def device(self, **moved):
        return {"dp": self.dp, "row": self.row, "col": self.col, **moved}

    def send(self, src, dst, recv, device, when=None):
        sem = self.send_sems.at[self.n_send]
        self.n_send += 1
        copy = pltpu.make_async_remote_copy(
            src_ref=src,
            dst_ref=dst,
            send_sem=sem,
            recv_sem=self.recv_sems.at[recv],
            device_id=device,
            device_id_type=MESH,
        )
        self.open.append((copy, when))
        copy.start() if when is None else pl.when(when)(copy.start)

    def landed(self, dst, recv):
        pltpu.make_async_remote_copy(
            src_ref=dst,
            dst_ref=dst,
            send_sem=self.send_sems.at[0],
            recv_sem=self.recv_sems.at[recv],
            device_id=self.device(col=1 - self.col),
            device_id_type=MESH,
        ).wait_recv()

    def finish(self):
        for copy, when in self.open:
            copy.wait_send() if when is None else pl.when(when)(copy.wait_send)
        self.open = []

    def greet(self, devices):
        barrier = pltpu.get_barrier_semaphore()
        count = 0
        for device, when in devices:

            def signal(device=device):
                pl.semaphore_signal(barrier, inc=1, device_id=device, device_id_type=MESH)

            if when is None:
                signal()
                count = count + 1
            else:
                pl.when(when)(signal)
                count = count + when.astype(jnp.int32)
        pl.semaphore_wait(barrier, count)

    def plane_neighbours(self, n_row):
        return [
            (self.device(row=self.row + 1), self.row < n_row - 1),
            (self.device(row=self.row - 1), self.row > 0),
            (self.device(col=1 - self.col), None),
        ]


def run_together(*steps):
    steps = list(steps)
    while steps:
        for step in list(steps):
            try:
                next(step)
            except StopIteration:
                steps.remove(step)


def scatter_sum(link, base, n_row, part, from_col, ins, outs, own):
    row, col = link.row, link.col
    (up_in, down_in), (up_out, down_out) = ins, outs
    y_base, up_base, down_base = base, base + n_row, base + 2 * n_row
    order = [at for k in range(n_row // 2) for at in (n_row - 1 - k, k)]
    for at in order:
        link.send(part.at[1 - col, at], from_col.at[at], y_base + at, link.device(col=1 - col))
    yield
    for at in order:
        link.landed(from_col.at[at], y_base + at)

    def mine(at):
        return part[col, at].astype(F32) + from_col[at].astype(F32)

    for k in range(n_row - 1):
        for at, going, more, source, target, base_at, device in (
            (n_row - 1 - k, row < n_row - 1 - k, row > 0, up_in, up_out, up_base, link.device(row=row + 1)),
            (k, row > k, row < n_row - 1, down_in, down_out, down_base, link.device(row=row - 1)),
        ):

            @pl.when(going & more)
            def _():
                link.landed(source.at[at], base_at + at)
                target[at] = (mine(at) + source[at].astype(F32)).astype(BF16)

            @pl.when(going & jnp.logical_not(more))
            def _():
                target[at] = mine(at).astype(BF16)

            link.send(target.at[at], source.at[at], base_at + at, device, going)
        yield
    own[...] = mine(row)

    for more, source, base_at in ((row > 0, up_in, up_base), (row < n_row - 1, down_in, down_base)):

        @pl.when(more)
        def _():
            link.landed(source.at[row], base_at + row)
            own[...] += source[row].astype(F32)


def spread(link, base, n_row, own, place, onward=None):
    row, col = link.row, link.col
    up, down, side = (device for device, _ in link.plane_neighbours(n_row))
    here = place(row, col)
    link.send(own, here, base + row, up, row < n_row - 1)
    link.send(own, here, base + row, down, row > 0)
    link.send(own, here, base + n_row + row, side)
    yield
    for k in range(1, n_row):
        for at, there, device, further in (
            (row - k, row >= k, up, row < n_row - 1),
            (row + k, row + k < n_row, down, row > 0),
        ):
            block = place(at, col)
            pl.when(there)(functools.partial(link.landed, block, base + at))
            if k < n_row - 1:
                link.send(block, block, base + at, device, there & further)
            link.send(block, block, base + n_row + at, side, there)
            if onward is not None:
                onward(at, col, there)
        yield
    for k in range(n_row):
        for at, there in [(row - k, row >= k), (row + k, row + k < n_row)][: 2 if k else 1]:
            block = place(at, 1 - col)
            pl.when(there)(functools.partial(link.landed, block, base + n_row + at))
            if onward is not None:
                onward(at, 1 - col, there)
        if k % 2:
            yield


def spread_matrix(link, base, n_row, shard, whole, by_row, local_sems):
    row, col, at_x, at_core = link.row, link.col, link.x, link.core
    columns = shard.shape[-1]

    def block(at_row, at_col, x, core):
        lead, side = (at_row, at_col) if by_row else (at_col, at_row)
        return whole.at[lead, x, core, :, pl.ds(pl.multiple_of(side * columns, 128), columns)]

    local = []
    for index, x in enumerate((at_x, 1 - at_x)):
        copy = pltpu.make_async_copy(
            shard.at[2 * x + at_core], block(row, col, x, at_core), local_sems.at[index]
        )
        copy.start()
        local.append(copy)
    x_base, core_base = base + 2 * n_row, base + 4 * n_row
    beside, sibling = link.device(dp=link.beside), link.device(dp=link.sibling)

    def to_x(at_row, at_col, when):
        ref = block(at_row, at_col, at_x, at_core)
        link.send(ref, ref, x_base + at_col * n_row + at_row, beside, when)

    yield from spread(link, base, n_row, shard.at[link.dp], lambda r, c: block(r, c, at_x, at_core), to_x)
    for copy in local:
        copy.wait()
    ref = whole.at[:, at_x, at_core]
    link.send(ref, ref, core_base, sibling)
    yield
    for k in range(2 * n_row):
        at_row, at_col = lax.rem(row + k // 2, n_row), 1 - col if k % 2 else col
        if k:
            link.landed(block(at_row, at_col, 1 - at_x, at_core), x_base + at_col * n_row + at_row)
        if k % 2:
            yield
    ref = whole.at[:, 1 - at_x, at_core]
    link.send(ref, ref, core_base + 1, sibling)
    yield
    link.landed(whole.at[:, at_x, 1 - at_core], core_base)
    link.landed(whole.at[:, 1 - at_x, 1 - at_core], core_base + 1)


N_MATRIX = 4 * 4 + 2


def front_kernel(n_row, looked, pos, *refs):
    shards, (start, own_rows), wholes = refs[:4], refs[4:6], refs[6:10]
    from_col, up_in, down_in, up_out, down_out, own, own_low, send_sems, recv_sems, local_sems = refs[10:]
    link = Link(send_sems, recv_sems)
    link.greet(
        link.plane_neighbours(n_row)
        + [(link.device(dp=link.beside), None), (link.device(dp=link.sibling), None)]
    )

    def tokens():
        yield from scatter_sum(link, 0, n_row, looked, from_col, (up_in, down_in), (up_out, down_out), own)
        own_rows[...] = own[...].astype(BF16)
        own_low[...] = (own[...] + pos[...]).astype(BF16)
        start[link.col, link.row] = own_low[...]
        yield from spread(link, 3 * n_row, n_row, own_low, lambda r, c: start.at[c, r])

    matrices = [
        spread_matrix(
            link, 5 * n_row + index * N_MATRIX, n_row, shards[index], wholes[index], index < 3, local_sems.at[index]
        )
        for index in range(4)
    ]
    run_together(tokens(), *matrices)
    link.finish()


def front(looked, pos, shards, n_row):
    block, width = looked.shape[2:]
    wholes = [(n_row, 2, 2) + shard.shape[1:2] + (2 * shard.shape[2],) for shard in shards[:3]]
    wholes.append((2, 2, 2) + shards[3].shape[1:2] + (n_row * shards[3].shape[2],))
    rows = pltpu.VMEM((n_row, block, width), BF16)
    vmem, hbm = pl.BlockSpec(memory_space=pltpu.VMEM), pl.BlockSpec(memory_space=pl.ANY)
    return pl.pallas_call(
        functools.partial(front_kernel, n_row),
        out_shape=[jax.ShapeDtypeStruct(looked.shape, BF16), jax.ShapeDtypeStruct((block, width), BF16)]
        + [jax.ShapeDtypeStruct(shape, BF16) for shape in wholes],
        in_specs=[vmem, vmem] + [hbm] * 4,
        out_specs=[vmem, vmem] + [hbm] * 4,
        scratch_shapes=[rows] * 5
        + [pltpu.VMEM((block, width), F32), pltpu.VMEM((block, width), BF16)]
        + [
            pltpu.SemaphoreType.DMA((220,)),
            pltpu.SemaphoreType.DMA((5 * n_row + 4 * N_MATRIX,)),
            pltpu.SemaphoreType.DMA((4, 2)),
        ],
        compiler_params=pltpu.CompilerParams(
            collective_id=1, has_side_effects=True, vmem_limit_bytes=40 * 1024 * 1024
        ),
    )(looked, pos, *shards)


def total_kernel(n_row, part, total, *refs):
    from_col, up_in, down_in, up_out, down_out, own, own_low, send_sems, recv_sems = refs
    link = Link(send_sems, recv_sems)
    link.greet(link.plane_neighbours(n_row))

    def steps():
        yield from scatter_sum(link, 0, n_row, part, from_col, (up_in, down_in), (up_out, down_out), own)
        own_low[...] = own[...].astype(BF16)
        total[link.col, link.row] = own_low[...]
        yield from spread(link, 3 * n_row, n_row, own_low, lambda r, c: total.at[c, r])

    run_together(steps())
    link.finish()


def plane_total(part, collective_id):
    n_row, block, width = part.shape[1:]
    rows = pltpu.VMEM((n_row, block, width), BF16)
    vmem = pl.BlockSpec(memory_space=pltpu.VMEM)
    return pl.pallas_call(
        functools.partial(total_kernel, n_row),
        out_shape=jax.ShapeDtypeStruct(part.shape, BF16),
        in_specs=[vmem],
        out_specs=vmem,
        scratch_shapes=[rows] * 5
        + [pltpu.VMEM((block, width), F32), pltpu.VMEM((block, width), BF16)]
        + [pltpu.SemaphoreType.DMA((40,)), pltpu.SemaphoreType.DMA((5 * n_row,))],
        compiler_params=pltpu.CompilerParams(
            collective_id=collective_id, has_side_effects=True, vmem_limit_bytes=40 * 1024 * 1024
        ),
    )(part)


QUERIES = 256


def causal(scores):
    keys = lax.broadcasted_iota(jnp.int32, scores.shape, 0)
    queries = lax.broadcasted_iota(jnp.int32, scores.shape, 1)
    return jnp.where(keys <= queries, scores, -1e30)


def attend_kernel(q_ref, k_ref, v_ref, o_ref, log_ref):
    length = q_ref.shape[0]
    for head in range(2):
        lanes = slice(head * HEAD, (head + 1) * HEAD)
        keys, values = k_ref[:, lanes], v_ref[:, lanes].T
        for at in range(0, length, QUERIES):
            here = slice(at, at + QUERIES)
            queries = q_ref[here, lanes] * HEAD ** (-0.5)
            edge = causal(mm_nt(keys[here], queries))
            top = jnp.max(edge, 0, keepdims=True)
            if at:
                before = mm_nt(keys[:at], queries)
                top = jnp.maximum(top, jnp.max(before, 0, keepdims=True))
            edge = jnp.exp(edge - top)
            count = jnp.sum(edge, 0, keepdims=True)
            mixed = mm(values[:, here], edge.astype(BF16))
            if at:
                before = jnp.exp(before - top)
                count = count + jnp.sum(before, 0, keepdims=True)
                mixed = mixed + mm(values[:, :at], before.astype(BF16))
            o_ref[here, lanes] = (mixed / count).T.astype(BF16)
            log_ref[0, head : head + 1, here] = top + jnp.log(count)


def attend(packed):
    length, width = packed.shape[0], packed.shape[1] // 3
    pairs = HEADS // 2
    lanes = 2 * HEAD
    column = lambda first: pl.BlockSpec((length, lanes), lambda i: (0, first + i))
    return pl.pallas_call(
        attend_kernel,
        grid=(pairs,),
        out_shape=[
            jax.ShapeDtypeStruct((length, width), BF16),
            jax.ShapeDtypeStruct((pairs, 2, length), F32),
        ],
        in_specs=[column(0), column(pairs), column(2 * pairs)],
        out_specs=[column(0), pl.BlockSpec((1, 2, length), lambda i: (i, 0, 0))],
        compiler_params=pltpu.CompilerParams(vmem_limit_bytes=40 * 1024 * 1024),
    )(packed, packed, packed)


def attend_back_kernel(q_ref, k_ref, v_ref, g_ref, log_ref, out_ref, key_sum, value_sum):
    length = q_ref.shape[0]
    for head in range(2):
        lanes = slice(head * HEAD, (head + 1) * HEAD)
        keys, values = k_ref[:, lanes], v_ref[:, lanes]
        keys_turned = keys.T
        key_sum[...] = jnp.zeros_like(key_sum)
        value_sum[...] = jnp.zeros_like(value_sum)
        for at in range(0, length, QUERIES):
            here, seen = slice(at, at + QUERIES), slice(0, at + QUERIES)
            queries, grads = q_ref[here, lanes] * HEAD ** (-0.5), g_ref[here, lanes]
            log_norm = log_ref[0, head : head + 1, here]
            probs = jnp.exp(causal(mm_nt(keys[here], queries)) - log_norm)
            if at:
                probs = jnp.concatenate([jnp.exp(mm_nt(keys[:at], queries) - log_norm), probs], 0)
            prob_grad = mm_nt(values[seen], grads)
            level = jnp.sum(probs * prob_grad, 0, keepdims=True)
            score_grad = (probs * (prob_grad - level)).astype(BF16)
            value_sum[seen] += mm(probs.astype(BF16), grads)
            key_sum[seen] += mm(score_grad, queries)
            query_grad = mm(keys_turned[:, seen], score_grad) * HEAD ** (-0.5)
            out_ref[0, here, lanes] = query_grad.T.astype(BF16)
        out_ref[1, :, lanes] = key_sum[...].astype(BF16)
        out_ref[2, :, lanes] = value_sum[...].astype(BF16)


def attend_back(packed, mixed_grad, log_norm):
    length, width = mixed_grad.shape
    pairs = HEADS // 2
    lanes = 2 * HEAD
    column = lambda first: pl.BlockSpec((length, lanes), lambda i: (0, first + i))
    return pl.pallas_call(
        attend_back_kernel,
        grid=(pairs,),
        out_shape=jax.ShapeDtypeStruct((3, length, width), BF16),
        in_specs=[column(0), column(pairs), column(2 * pairs), column(0)]
        + [pl.BlockSpec((1, 2, length), lambda i: (i, 0, 0))],
        out_specs=pl.BlockSpec((3, length, lanes), lambda i: (0, 0, i)),
        scratch_shapes=[pltpu.VMEM((length, HEAD), F32)] * 2,
        compiler_params=pltpu.CompilerParams(vmem_limit_bytes=48 * 1024 * 1024),
    )(packed, packed, packed, mixed_grad, log_norm)


def norm_forward(inputs, gain, shift):
    center = jnp.mean(inputs, -1, keepdims=True)
    var = jnp.mean(inputs * inputs, -1, keepdims=True) - center * center
    inv = lax.rsqrt(var + 1e-05)
    normed = (inputs - center) * inv
    return (normed * gain + shift).astype(BF16), normed, inv


def norm_backward(upstream, normed, inv, gain):
    scaled = upstream * gain
    first = jnp.mean(scaled, -1, keepdims=True)
    second = jnp.mean(scaled * normed, -1, keepdims=True)
    result = inv * (scaled - first - normed * second)
    return result, jnp.sum(upstream * normed, 0), jnp.sum(upstream, 0)


def gelu_tanh(inputs):
    return jax.nn.gelu(inputs, approximate=True)


def body(
    token_ids,
    target_ids,
    included,
    tok_table,
    pos_table,
    qkv_weight,
    attn_weight,
    up_weight,
    down_weight,
    small_params,
    table_rows,
    table_cols,
    pos_rows,
    pos_cols,
    qkv_rows,
    qkv_cols,
    attn_rows,
    attn_cols,
    up_rows,
    up_cols,
    down_rows,
    down_cols,
    small_second,
    table_noise,
    pos_noise,
    qkv_noise,
    attn_noise,
    up_noise,
    down_noise,
    small_noise,
):
    n_row = lax.axis_size("row")
    n_col = lax.axis_size("col")
    n_data = lax.axis_size("dp")
    row_at = lax.axis_index("row")
    col_at = lax.axis_index("col")
    ids, targets = token_ids[0], target_ids[0]
    length = ids.shape[0]
    width = small_params.shape[1]
    vocab_here = tok_table.shape[0]
    vocab_start = (col_at * n_row + row_at) * vocab_here
    small = small_params

    weights_in = [tok_table, pos_table, qkv_weight, attn_weight, up_weight, down_weight]
    noises = [table_noise, pos_noise, qkv_noise, attn_noise, up_noise, down_noise]
    weight_sq = jnp.stack([jnp.sum(item * item) for item in weights_in])
    table_low = tok_table.astype(BF16)

    local_ids = ids - vocab_start
    inside = (local_ids >= 0) & (local_ids < vocab_here)
    safe_ids = jnp.clip(local_ids, 0, vocab_here - 1)
    looked = jnp.where(inside[:, None], jnp.take(table_low, safe_ids, axis=0), jnp.zeros((), BF16))
    tuned = (n_data, n_row, n_col) == (4, 4, 2)
    block = length // (n_row * n_col)
    lows = [item.astype(BF16) for item in weights_in[2:]]
    if tuned:
        pos_blocks = pos_table.reshape(n_row, block, -1)
        pieces = []
        for k in range(n_row):
            piece = lax.dynamic_index_in_dim(pos_blocks, row_at ^ k, 0, False)
            if k:
                piece = lax.ppermute(piece, "row", [(at, at ^ k) for at in range(n_row)])
            pieces.append(piece)
        pieces = jnp.stack(pieces)
        pos_own = jnp.concatenate([pieces[row_at ^ at] for at in range(n_row)], 1)
        shards = [item.reshape(n_data, -1, item.shape[1]) for item in lows]
        start, own_rows, qkv_full, attn_full, up_full, down_full = front(
            looked.reshape(n_col, n_row, block, width), pos_own, shards, n_row
        )
        stream_in = start.reshape(length, width).astype(F32)
        qkv_full, attn_full, up_full, down_full = (
            item.reshape(width, -1) for item in (qkv_full, attn_full, up_full, down_full)
        )
    else:
        stream_in = plane_sum(looked).astype(F32) + gather_matrix(pos_table, 1)
        qkv_full, attn_full, up_full = (gather_matrix(item, 0) for item in lows[:3])
        down_full = gather_matrix(lows[3], 1)

    ln_one, norm_one, inv_one = norm_forward(stream_in, small[0], small[1])
    bias = jnp.concatenate([small[2], jnp.zeros_like(small[2]), small[3]])
    packed = (mm(ln_one, qkv_full) + bias).astype(BF16)
    mixed, log_norm = attend(packed)
    stream_mid = stream_in + mm(mixed, attn_full) + small[4]
    ln_two, norm_two, inv_two = norm_forward(stream_mid, small[5], small[6])
    up_pre = mm(ln_two, up_full) + small[7:11].reshape(-1)
    up_act = gelu_tanh(up_pre).astype(BF16)
    stream_out = stream_mid + mm_nt(up_act, down_full) + small[11]
    ln_fin, norm_fin, inv_fin = norm_forward(stream_out, small[12], small[13])

    logits = mm_nt(table_low, ln_fin)
    top = jnp.max(logits, 0)
    hits = jnp.arange(vocab_here)[:, None] == (targets - vocab_start)[None, :]
    picked_here = jnp.sum(jnp.where(hits, logits, 0.0), 0)
    all_top = lax.pmax(top, PLANE)
    exp_logits = jnp.exp(logits - all_top[None, :])
    exp_total, picked = plane_sum((jnp.sum(exp_logits, 0), picked_here))
    loss = jnp.sum(all_top + jnp.log(exp_total) - picked)
    logit_grad = (exp_logits / exp_total[None, :] - hits.astype(F32)).astype(BF16)
    final_part = mm_tn(logit_grad, table_low).astype(BF16)
    if tuned:
        final_part = plane_total(final_part.reshape(n_col, n_row, block, width), 2)
        final_grad = final_part.reshape(length, width).astype(F32)
    else:
        final_grad = plane_sum(final_part).astype(F32)
    table_ex = mm(logit_grad, ln_fin)

    grad_out, gain_fin, shift_fin = norm_backward(final_grad, norm_fin, inv_fin, small[12])
    down_grad = grad_out.astype(BF16)
    act_grad = mm(down_grad, down_full)
    pre_grad = jax.vjp(gelu_tanh, up_pre)[1](act_grad)[0].astype(BF16)
    mid_part, gain_two, shift_two = norm_backward(mm_nt(pre_grad, up_full), norm_two, inv_two, small[5])
    mid_grad = grad_out + mid_part
    branch_grad = mid_grad.astype(BF16)
    mixed_grad = mm_nt(branch_grad, attn_full).astype(BF16)
    packed_grad = attend_back(packed, mixed_grad, log_norm)
    packed_grad = packed_grad.transpose(1, 0, 2).reshape(length, -1)
    in_part, gain_one, shift_one = norm_backward(mm_nt(packed_grad, qkv_full), norm_one, inv_one, small[0])
    grad_in = mid_grad + in_part

    def columns_of(array, at, parts):
        size = array.shape[1] // parts
        return lax.dynamic_slice_in_dim(array, at * size, size, 1)

    layer_ex = [
        mm_tn(columns_of(left, at_left, n_left), columns_of(right, at_right, n_right))
        for left, at_left, n_left, right, at_right, n_right in (
            (ln_one, row_at, n_row, packed_grad, col_at, n_col),
            (mixed, row_at, n_row, branch_grad, col_at, n_col),
            (ln_two, row_at, n_row, pre_grad, col_at, n_col),
            (down_grad, col_at, n_col, up_act, row_at, n_row),
        )
    ]
    tok_here, dim_here = pos_table.shape
    pos_ex = lax.dynamic_slice(grad_in, (col_at * tok_here, row_at * dim_here), (tok_here, dim_here))
    column = lambda item: jnp.sum(item.astype(F32), 0)
    packed_sums = column(packed_grad).reshape(3, width)
    small_ex = jnp.stack(
        [gain_one, shift_one, packed_sums[0], packed_sums[2], column(branch_grad), gain_two, shift_two]
        + list(column(pre_grad).reshape(-1, width))
        + [column(down_grad), gain_fin, shift_fin]
    )
    emb_grad = jnp.where(inside[:, None], grad_in.astype(BF16).astype(F32), 0.0)
    table_ex = table_ex + jnp.zeros_like(table_ex).at[safe_ids].add(emb_grad)

    own_sq = sum(jnp.sum(item * item) for item in [table_ex] + layer_ex)
    total = plane_sum(jnp.concatenate([weight_sq, own_sq[None]]))
    weight_total = total[:6]
    norm_sq = total[6] + jnp.sum(grad_in * grad_in) + jnp.sum(small_ex * small_ex)
    example_norm = jnp.sqrt(norm_sq)
    taken = included[0].astype(F32)
    share = taken * jnp.minimum(1.0, CLIP * lax.rsqrt(norm_sq + 1e-12))

    sums = [
        example_sum((share * item).astype(BF16)).astype(F32)
        for item in [table_ex, pos_ex] + layer_ex + [small_ex]
    ]
    loss_sum, taken_sum = example_sum(jnp.stack([taken * loss, taken]))
    divisor = SAMPLE * n_data
    grads = [(sums[index] + NOISE * CLIP * noises[index]) / divisor for index in range(6)]

    olds = [
        (table_rows, table_cols),
        (pos_rows, pos_cols),
        (qkv_rows, qkv_cols),
        (attn_rows, attn_cols),
        (up_rows, up_cols),
        (down_rows, down_cols),
    ]
    axes = [(PLANE, None), ("col", "row"), ("row", "col"), ("row", "col"), ("row", "col"), ("col", "row")]
    outputs = []
    for index in range(6):
        grad, (old_rows, old_cols), (rows_over, cols_over) = grads[index], olds[index], axes[index]
        squares = grad * grad + 1e-30
        row_sum, col_sum = jnp.sum(squares, 1), jnp.sum(squares, 0)
        n_rows, n_cols = grad.shape[0] * lax.axis_size(rows_over), grad.shape[1]
        if cols_over is not None:
            n_cols = n_cols * lax.axis_size(cols_over)
            row_sum = lax.psum(row_sum, cols_over)
        col_sum = lax.psum(col_sum, rows_over)
        rows_new = DECAY * old_rows + (1.0 - DECAY) * (row_sum / n_cols)
        cols_new = DECAY * old_cols + (1.0 - DECAY) * (col_sum / n_rows)
        row_mean = lax.psum(jnp.sum(rows_new), rows_over) / n_rows
        update = grad * lax.rsqrt(rows_new[:, None] * cols_new[None, :] / row_mean)
        update_total = lax.psum(jnp.sum(update * update), PLANE)
        entries = n_rows * n_cols
        size = RATE * jnp.maximum(1e-3, jnp.sqrt(weight_total[index] / entries))
        size = size / jnp.maximum(1.0, jnp.sqrt(update_total / entries))
        outputs.extend([grad, rows_new, cols_new, weights_in[index] - size * update])
    small_grad = (sums[6] + NOISE * CLIP * small_noise) / divisor
    second_new = DECAY * small_second + (1.0 - DECAY) * (small_grad * small_grad + 1e-30)
    small_update = small_grad * lax.rsqrt(second_new)
    small_update = small_update / jnp.maximum(1.0, jnp.sqrt(jnp.mean(small_update * small_update)))
    small_size = RATE * jnp.maximum(1e-3, jnp.sqrt(jnp.mean(small_params * small_params)))
    small_new = small_params - small_size * small_update
    return tuple(outputs) + (
        small_grad,
        second_new,
        small_new,
        loss_sum,
        taken_sum * length,
        example_norm[None],
    )


def solution(mesh):
    table, by_col, by_row = P(("col", "row"), None), P("col", "row"), P("row", "col")
    return jax.shard_map(
        body,
        mesh=mesh,
        in_specs=(P("dp", None), P("dp", None), P("dp"))
        + (table, by_col, by_row, by_row, by_row, by_col, P())
        + (P(("col", "row")), P(), P("col"), P("row"))
        + (P("row"), P("col")) * 3
        + (P("col"), P("row"), P())
        + (table, by_col, by_row, by_row, by_row, by_col, P()),
        out_specs=(table, P(("col", "row")), P(), table)
        + (by_col, P("col"), P("row"), by_col)
        + (by_row, P("row"), P("col"), by_row) * 3
        + (by_col, P("col"), P("row"), by_col)
        + (P(), P(), P(), P(), P(), P("dp")),
        check_vma=False,
    )
```

```python
import functools

import jax
import jax.numpy as jnp
from jax import lax
from jax.experimental import pallas as pl
from jax.experimental.pallas import tpu as pltpu
from jax.sharding import PartitionSpec as P

HEADS = 12
HEAD = 64
STEP = 10
CLIP = 1.0
NOISE = 0.002
SAMPLE = 0.5
RATE = 0.5
DECAY = 1.0 - STEP ** (-0.8)

F32 = jnp.float32
BF16 = jnp.bfloat16
PLANE = ("row", "col")
MESH = pl.DeviceIdType.MESH


def dot_f32(left, right, dims):
    return lax.dot_general(left, right, (dims, ((), ())), preferred_element_type=F32)


def mm(left, right):
    return dot_f32(left, right, ((1,), (0,)))


def mm_nt(left, right):
    return dot_f32(left, right, ((1,), (1,)))


def mm_tn(left, right):
    return dot_f32(left, right, ((0,), (0,)))


def gather_matrix(block, row_dim):
    part = lax.all_gather(block, "row", axis=row_dim, tiled=True)
    return lax.all_gather(part, "col", axis=1 - row_dim, tiled=True)


def plane_sum(array):
    return lax.psum(array, PLANE)


def example_sum(array):
    return lax.psum(array, "dp")


class Link:
    def __init__(self, send_sems, recv_sems):
        self.dp, self.row, self.col = (lax.axis_index(axis) for axis in ("dp", "row", "col"))
        self.x, self.core = self.dp // 2, self.dp % 2
        self.beside = 2 * (1 - self.x) + self.core
        self.sibling = 2 * self.x + 1 - self.core
        self.send_sems, self.recv_sems = send_sems, recv_sems
        self.n_send = 0
        self.open = []

    def device(self, **moved):
        return {"dp": self.dp, "row": self.row, "col": self.col, **moved}

    def send(self, src, dst, recv, device, when=None):
        sem = self.send_sems.at[self.n_send]
        self.n_send += 1
        copy = pltpu.make_async_remote_copy(
            src_ref=src,
            dst_ref=dst,
            send_sem=sem,
            recv_sem=self.recv_sems.at[recv],
            device_id=device,
            device_id_type=MESH,
        )
        self.open.append((copy, when))
        copy.start() if when is None else pl.when(when)(copy.start)

    def landed(self, dst, recv):
        pltpu.make_async_remote_copy(
            src_ref=dst,
            dst_ref=dst,
            send_sem=self.send_sems.at[0],
            recv_sem=self.recv_sems.at[recv],
            device_id=self.device(col=1 - self.col),
            device_id_type=MESH,
        ).wait_recv()

    def finish(self):
        for copy, when in self.open:
            copy.wait_send() if when is None else pl.when(when)(copy.wait_send)
        self.open = []

    def greet(self, devices):
        barrier = pltpu.get_barrier_semaphore()
        count = 0
        for device, when in devices:

            def signal(device=device):
                pl.semaphore_signal(barrier, inc=1, device_id=device, device_id_type=MESH)

            if when is None:
                signal()
                count = count + 1
            else:
                pl.when(when)(signal)
                count = count + when.astype(jnp.int32)
        pl.semaphore_wait(barrier, count)

    def plane_peers(self, n_row):
        me, peers = self.col * n_row + self.row, []
        for k in range(1, 2 * n_row):
            index = (me + k) % (2 * n_row)
            peers.append((index, self.device(row=index % n_row, col=index // n_row)))
        return me, peers

    def example_peers(self):
        return [((self.dp + k) % 4, self.device(dp=(self.dp + k) % 4)) for k in range(1, 4)]

    def plane_neighbours(self, n_row):
        return [
            (self.device(row=self.row + 1), self.row < n_row - 1),
            (self.device(row=self.row - 1), self.row > 0),
            (self.device(col=1 - self.col), None),
        ]


def run_together(*steps):
    steps = list(steps)
    while steps:
        for step in list(steps):
            try:
                next(step)
            except StopIteration:
                steps.remove(step)


def scatter_sum(link, base, n_row, part, from_col, ins, outs, own):
    row, col = link.row, link.col
    (up_in, down_in), (up_out, down_out) = ins, outs
    y_base, up_base, down_base = base, base + n_row, base + 2 * n_row
    order = [at for k in range(n_row // 2) for at in (n_row - 1 - k, k)]
    for at in order:
        link.send(part.at[1 - col, at], from_col.at[at], y_base + at, link.device(col=1 - col))
    yield
    waiting = list(order)

    def mine(at):
        return part[col, at].astype(F32) + from_col[at].astype(F32)

    for k in range(n_row - 1):
        for at in (n_row - 1 - k, k):
            if at in waiting:
                waiting.remove(at)
                link.landed(from_col.at[at], y_base + at)
        for at, going, more, source, target, base_at, device in (
            (n_row - 1 - k, row < n_row - 1 - k, row > 0, up_in, up_out, up_base, link.device(row=row + 1)),
            (k, row > k, row < n_row - 1, down_in, down_out, down_base, link.device(row=row - 1)),
        ):

            @pl.when(going & more)
            def _():
                link.landed(source.at[at], base_at + at)
                target[at] = (mine(at) + source[at].astype(F32)).astype(BF16)

            @pl.when(going & jnp.logical_not(more))
            def _():
                target[at] = mine(at).astype(BF16)

            link.send(target.at[at], source.at[at], base_at + at, device, going)
        yield
    own[...] = mine(row)

    for more, source, base_at in ((row > 0, up_in, up_base), (row < n_row - 1, down_in, down_base)):

        @pl.when(more)
        def _():
            link.landed(source.at[row], base_at + row)
            own[...] += source[row].astype(F32)


def spread(link, base, n_row, own, place, onward=None):
    row, col = link.row, link.col
    up, down, side = (device for device, _ in link.plane_neighbours(n_row))
    here = place(row, col)
    link.send(own, here, base + row, up, row < n_row - 1)
    link.send(own, here, base + row, down, row > 0)
    link.send(own, here, base + n_row + row, side)
    yield
    for k in range(1, n_row):
        for at, there, device, further in (
            (row - k, row >= k, up, row < n_row - 1),
            (row + k, row + k < n_row, down, row > 0),
        ):
            block = place(at, col)
            pl.when(there)(functools.partial(link.landed, block, base + at))
            if k < n_row - 1:
                link.send(block, block, base + at, device, there & further)
            link.send(block, block, base + n_row + at, side, there)
            if onward is not None:
                onward(at, col, there)
        yield
    for k in range(n_row):
        for at, there in [(row - k, row >= k), (row + k, row + k < n_row)][: 2 if k else 1]:
            block = place(at, 1 - col)
            pl.when(there)(functools.partial(link.landed, block, base + n_row + at))
            if onward is not None:
                onward(at, 1 - col, there)
        if k % 2:
            yield


def spread_matrix(link, base, n_row, shard, whole, by_row, local_sems):
    row, col, at_x, at_core = link.row, link.col, link.x, link.core
    columns = shard.shape[-1]

    def block(at_row, at_col, x, core):
        lead, side = (at_row, at_col) if by_row else (at_col, at_row)
        return whole.at[lead, x, core, :, pl.ds(pl.multiple_of(side * columns, 128), columns)]

    local = []
    for index, x in enumerate((at_x, 1 - at_x)):
        copy = pltpu.make_async_copy(
            shard.at[2 * x + at_core], block(row, col, x, at_core), local_sems.at[index]
        )
        copy.start()
        local.append(copy)
    x_base, core_base = base + 2 * n_row, base + 4 * n_row
    beside, sibling = link.device(dp=link.beside), link.device(dp=link.sibling)

    def to_x(at_row, at_col, when):
        ref = block(at_row, at_col, at_x, at_core)
        link.send(ref, ref, x_base + at_col * n_row + at_row, beside, when)

    yield from spread(link, base, n_row, shard.at[link.dp], lambda r, c: block(r, c, at_x, at_core), to_x)
    for copy in local:
        copy.wait()
    ref = whole.at[:, at_x, at_core]
    link.send(ref, ref, core_base, sibling)
    yield
    for k in range(2 * n_row):
        at_row, at_col = lax.rem(row + k // 2, n_row), 1 - col if k % 2 else col
        if k:
            link.landed(block(at_row, at_col, 1 - at_x, at_core), x_base + at_col * n_row + at_row)
        if k % 2:
            yield
    ref = whole.at[:, 1 - at_x, at_core]
    link.send(ref, ref, core_base + 1, sibling)
    yield
    link.landed(whole.at[:, at_x, 1 - at_core], core_base)
    link.landed(whole.at[:, 1 - at_x, 1 - at_core], core_base + 1)


N_MATRIX = 4 * 4 + 2


def front_kernel(n_row, looked, pos, *refs):
    shards, (start, own_rows), wholes = refs[:4], refs[4:6], refs[6:10]
    from_col, up_in, down_in, up_out, down_out, own, own_low, send_sems, recv_sems, local_sems = refs[10:]
    link = Link(send_sems, recv_sems)
    link.greet(
        link.plane_neighbours(n_row)
        + [(link.device(dp=link.beside), None), (link.device(dp=link.sibling), None)]
    )

    def tokens():
        yield from scatter_sum(link, 0, n_row, looked, from_col, (up_in, down_in), (up_out, down_out), own)
        own_rows[...] = own[...].astype(BF16)
        own_low[...] = (own[...] + pos[...]).astype(BF16)
        start[link.col, link.row] = own_low[...]
        yield from spread(link, 3 * n_row, n_row, own_low, lambda r, c: start.at[c, r])

    matrices = [
        spread_matrix(
            link, 5 * n_row + index * N_MATRIX, n_row, shards[index], wholes[index], index < 3, local_sems.at[index]
        )
        for index in range(4)
    ]
    run_together(tokens(), *matrices)
    link.finish()


def front(looked, pos, shards, n_row):
    block, width = looked.shape[2:]
    wholes = [(n_row, 2, 2) + shard.shape[1:2] + (2 * shard.shape[2],) for shard in shards[:3]]
    wholes.append((2, 2, 2) + shards[3].shape[1:2] + (n_row * shards[3].shape[2],))
    rows = pltpu.VMEM((n_row, block, width), BF16)
    vmem, hbm = pl.BlockSpec(memory_space=pltpu.VMEM), pl.BlockSpec(memory_space=pl.ANY)
    return pl.pallas_call(
        functools.partial(front_kernel, n_row),
        out_shape=[jax.ShapeDtypeStruct(looked.shape, BF16), jax.ShapeDtypeStruct((block, width), BF16)]
        + [jax.ShapeDtypeStruct(shape, BF16) for shape in wholes],
        in_specs=[vmem, vmem] + [hbm] * 4,
        out_specs=[vmem, vmem] + [hbm] * 4,
        scratch_shapes=[rows] * 5
        + [pltpu.VMEM((block, width), F32), pltpu.VMEM((block, width), BF16)]
        + [
            pltpu.SemaphoreType.DMA((220,)),
            pltpu.SemaphoreType.DMA((5 * n_row + 4 * N_MATRIX,)),
            pltpu.SemaphoreType.DMA((4, 2)),
        ],
        compiler_params=pltpu.CompilerParams(
            collective_id=1, has_side_effects=True, vmem_limit_bytes=40 * 1024 * 1024
        ),
    )(looked, pos, *shards)


def total_kernel(n_row, part, total, *refs):
    from_col, up_in, down_in, up_out, down_out, own, own_low, send_sems, recv_sems = refs
    link = Link(send_sems, recv_sems)
    link.greet(link.plane_neighbours(n_row))

    def steps():
        yield from scatter_sum(link, 0, n_row, part, from_col, (up_in, down_in), (up_out, down_out), own)
        own_low[...] = own[...].astype(BF16)
        total[link.col, link.row] = own_low[...]
        yield from spread(link, 3 * n_row, n_row, own_low, lambda r, c: total.at[c, r])

    run_together(steps())
    link.finish()


def plane_total(part, collective_id):
    n_row, block, width = part.shape[1:]
    rows = pltpu.VMEM((n_row, block, width), BF16)
    vmem = pl.BlockSpec(memory_space=pltpu.VMEM)
    return pl.pallas_call(
        functools.partial(total_kernel, n_row),
        out_shape=jax.ShapeDtypeStruct(part.shape, BF16),
        in_specs=[vmem],
        out_specs=vmem,
        scratch_shapes=[rows] * 5
        + [pltpu.VMEM((block, width), F32), pltpu.VMEM((block, width), BF16)]
        + [pltpu.SemaphoreType.DMA((40,)), pltpu.SemaphoreType.DMA((5 * n_row,))],
        compiler_params=pltpu.CompilerParams(
            collective_id=collective_id, has_side_effects=True, vmem_limit_bytes=40 * 1024 * 1024
        ),
    )(part)


QUERIES = 256


def causal(scores):
    keys = lax.broadcasted_iota(jnp.int32, scores.shape, 0)
    queries = lax.broadcasted_iota(jnp.int32, scores.shape, 1)
    return jnp.where(keys <= queries, scores, -1e30)


def attend_kernel(q_ref, k_ref, v_ref, o_ref, log_ref):
    length = q_ref.shape[0]
    for head in range(2):
        lanes = slice(head * HEAD, (head + 1) * HEAD)
        keys, values = k_ref[:, lanes], v_ref[:, lanes].T
        for at in range(0, length, QUERIES):
            here = slice(at, at + QUERIES)
            queries = q_ref[here, lanes] * HEAD ** (-0.5)
            edge = causal(mm_nt(keys[here], queries))
            top = jnp.max(edge, 0, keepdims=True)
            if at:
                before = mm_nt(keys[:at], queries)
                top = jnp.maximum(top, jnp.max(before, 0, keepdims=True))
            edge = jnp.exp(edge - top)
            count = jnp.sum(edge, 0, keepdims=True)
            mixed = mm(values[:, here], edge.astype(BF16))
            if at:
                before = jnp.exp(before - top)
                count = count + jnp.sum(before, 0, keepdims=True)
                mixed = mixed + mm(values[:, :at], before.astype(BF16))
            o_ref[here, lanes] = (mixed / count).T.astype(BF16)
            log_ref[0, head : head + 1, here] = top + jnp.log(count)


def attend(packed):
    length, width = packed.shape[0], packed.shape[1] // 3
    pairs = HEADS // 2
    lanes = 2 * HEAD
    column = lambda first: pl.BlockSpec((length, lanes), lambda i: (0, first + i))
    return pl.pallas_call(
        attend_kernel,
        grid=(pairs,),
        out_shape=[
            jax.ShapeDtypeStruct((length, width), BF16),
            jax.ShapeDtypeStruct((pairs, 2, length), F32),
        ],
        in_specs=[column(0), column(pairs), column(2 * pairs)],
        out_specs=[column(0), pl.BlockSpec((1, 2, length), lambda i: (i, 0, 0))],
        cost_estimate=cost(20 * length * length * width, 8 * length * width),
        compiler_params=pltpu.CompilerParams(vmem_limit_bytes=40 * 1024 * 1024),
    )(packed, packed, packed)


def attend_back_kernel(q_ref, k_ref, v_ref, g_ref, log_ref, out_ref, key_sum, value_sum):
    length = q_ref.shape[0]
    for head in range(2):
        lanes = slice(head * HEAD, (head + 1) * HEAD)
        keys, values = k_ref[:, lanes], v_ref[:, lanes]
        keys_turned = keys.T
        key_sum[...] = jnp.zeros_like(key_sum)
        value_sum[...] = jnp.zeros_like(value_sum)
        for at in range(0, length, QUERIES):
            here, seen = slice(at, at + QUERIES), slice(0, at + QUERIES)
            queries, grads = q_ref[here, lanes] * HEAD ** (-0.5), g_ref[here, lanes]
            log_norm = log_ref[0, head : head + 1, here]
            probs = jnp.exp(causal(mm_nt(keys[here], queries)) - log_norm)
            if at:
                probs = jnp.concatenate([jnp.exp(mm_nt(keys[:at], queries) - log_norm), probs], 0)
            prob_grad = mm_nt(values[seen], grads)
            level = jnp.sum(probs * prob_grad, 0, keepdims=True)
            score_grad = (probs * (prob_grad - level)).astype(BF16)
            value_sum[seen] += mm(probs.astype(BF16), grads)
            key_sum[seen] += mm(score_grad, queries)
            query_grad = mm(keys_turned[:, seen], score_grad) * HEAD ** (-0.5)
            out_ref[0, here, lanes] = query_grad.T.astype(BF16)
        out_ref[1, :, lanes] = key_sum[...].astype(BF16)
        out_ref[2, :, lanes] = value_sum[...].astype(BF16)


def attend_back(packed, mixed_grad, log_norm):
    length, width = mixed_grad.shape
    pairs = HEADS // 2
    lanes = 2 * HEAD
    column = lambda first: pl.BlockSpec((length, lanes), lambda i: (0, first + i))
    return pl.pallas_call(
        attend_back_kernel,
        grid=(pairs,),
        out_shape=jax.ShapeDtypeStruct((3, length, width), BF16),
        in_specs=[column(0), column(pairs), column(2 * pairs), column(0)]
        + [pl.BlockSpec((1, 2, length), lambda i: (i, 0, 0))],
        out_specs=pl.BlockSpec((3, length, lanes), lambda i: (0, 0, i)),
        scratch_shapes=[pltpu.VMEM((length, HEAD), F32)] * 2,
        cost_estimate=cost(30 * length * length * width, 16 * length * width),
        compiler_params=pltpu.CompilerParams(vmem_limit_bytes=48 * 1024 * 1024),
    )(packed, packed, packed, mixed_grad, log_norm)


def meet(link, base, value, slots, me, peers):
    slots[me] = value[...]
    for _, device in peers:
        link.send(value, slots.at[me], base + me, device)
    for index, _ in peers:
        link.landed(slots.at[index], base + index)


def added(slots):
    total = slots[0]
    for k in range(1, slots.shape[0]):
        total = total + slots[k]
    return total


def sum_small_kernel(n_row, value, total, middle, slots, dp_slots, send_sems, recv_sems):
    link = Link(send_sems, recv_sems)
    me, peers = link.plane_peers(n_row)
    examples = link.example_peers()
    link.greet([(device, None) for _, device in peers + examples])
    meet(link, 0, value, slots, me, peers)
    middle[...] = added(slots)
    meet(link, 2 * n_row, middle, dp_slots, link.dp, examples)
    total[...] = added(dp_slots)
    link.finish()


def sum_small(value, n_row, collective_id):
    vmem = pl.BlockSpec(memory_space=pltpu.VMEM)
    return pl.pallas_call(
        functools.partial(sum_small_kernel, n_row),
        out_shape=jax.ShapeDtypeStruct(value.shape, F32),
        in_specs=[vmem],
        out_specs=vmem,
        scratch_shapes=[pltpu.VMEM(value.shape, F32), pltpu.VMEM((2 * n_row,) + value.shape, F32)]
        + [pltpu.VMEM((4,) + value.shape, F32)]
        + [pltpu.SemaphoreType.DMA((2 * n_row + 2,)), pltpu.SemaphoreType.DMA((2 * n_row + 4,))],
        compiler_params=pltpu.CompilerParams(collective_id=collective_id, has_side_effects=True),
    )(value)


def log_total_kernel(n_row, tops, sums, picked, log_ref, pick_ref, value, slots, send_sems, recv_sems):
    link = Link(send_sems, recv_sems)
    me, peers = link.plane_peers(n_row)
    link.greet([(device, None) for _, device in peers])
    top = jnp.max(tops[...], 0)
    value[0] = top
    value[1] = jnp.sum(sums[...] * jnp.exp(tops[...] - top[None]), 0)
    value[2] = picked[...]
    meet(link, 0, value, slots, me, peers)
    everyone = range(2 * n_row)
    top, total, pick = slots[0, 0], jnp.zeros_like(top), jnp.zeros_like(top)
    for k in everyone:
        top = jnp.maximum(top, slots[k, 0])
    for k in everyone:
        total = total + slots[k, 1] * jnp.exp(slots[k, 0] - top)
        pick = pick + slots[k, 2]
    log_ref[...] = top + jnp.log(total)
    pick_ref[...] = pick
    link.finish()


def log_total(tops, sums, picked, n_row, collective_id):
    length = picked.shape[-1]
    tile = (length // 128, 128)
    tops, sums, picked = (item.reshape(item.shape[:-2] + tile) for item in (tops, sums, picked))
    vmem = pl.BlockSpec(memory_space=pltpu.VMEM)
    log_norm, picked = pl.pallas_call(
        functools.partial(log_total_kernel, n_row),
        out_shape=[jax.ShapeDtypeStruct(tile, F32)] * 2,
        in_specs=[vmem] * 3,
        out_specs=[vmem] * 2,
        scratch_shapes=[pltpu.VMEM((3,) + tile, F32), pltpu.VMEM((2 * n_row, 3) + tile, F32)]
        + [pltpu.SemaphoreType.DMA((2 * n_row,))] * 2,
        compiler_params=pltpu.CompilerParams(collective_id=collective_id, has_side_effects=True),
    )(tops, sums, picked)
    return log_norm.reshape(1, length), picked.reshape(1, length)


BLOCK = 1056
MEGA = 1024 * 1024


def cost(flops, bytes_accessed):
    return pl.CostEstimate(flops=flops, bytes_accessed=bytes_accessed, transcendentals=0)


def blocks_of(limit):
    return pl.cdiv(limit, BLOCK)


def entries(shape, first=0):
    return lax.broadcasted_iota(jnp.int32, shape, 0) + (pl.program_id(0) + first) * BLOCK


def head_kernel(limit, table_ref, z_ref, target_ref, low_ref, exp_ref, top_ref, sum_ref, pick_ref, square_ref):
    table = table_ref[...]
    table = jnp.where(entries(table.shape) < limit, table, 0.0)
    low = table.astype(BF16)
    low_ref[...] = low
    logits = mm_nt(low, z_ref[...])
    entry = entries(logits.shape)
    logits = jnp.where(entry < limit, logits, -1e30)
    top = jnp.max(logits, 0, keepdims=True)
    picked = jnp.sum(jnp.where(entry == target_ref[...], logits, 0.0), 0, keepdims=True)
    exps = jnp.exp(logits - top)
    exp_ref[...] = exps.astype(BF16)
    top_ref[0] = top
    sum_ref[0] = jnp.sum(exps, 0, keepdims=True)
    square = jnp.sum(table * table, 0, keepdims=True)

    @pl.when(pl.program_id(0) == 0)
    def _():
        pick_ref[...] = jnp.zeros_like(pick_ref)
        square_ref[...] = jnp.zeros_like(square_ref)

    pick_ref[...] += picked
    square_ref[...] += square


def whole_block(shape):
    return pl.BlockSpec(shape, lambda i, *_: (0,) * len(shape), pipeline_mode=pl.Buffered(1))


def row_block(width):
    return pl.BlockSpec((BLOCK, width), lambda i, *_: (i, 0))


def line_block(width):
    return pl.BlockSpec((1, 1, width), lambda i, *_: (i, 0, 0))


def head(table, z, target):
    limit, width = table.shape
    length, count = z.shape[0], blocks_of(limit)
    shape = jax.ShapeDtypeStruct
    return pl.pallas_call(
        functools.partial(head_kernel, limit),
        grid=(count,),
        out_shape=[
            shape((count * BLOCK, width), BF16),
            shape((count * BLOCK, length), BF16),
            shape((count, 1, length), F32),
            shape((count, 1, length), F32),
            shape((1, length), F32),
            shape((1, width), F32),
        ],
        in_specs=[row_block(width), whole_block((length, width)), whole_block((1, length))],
        out_specs=[row_block(width), row_block(length), line_block(length), line_block(length)]
        + [whole_block((1, length)), whole_block((1, width))],
        cost_estimate=cost(2 * limit * width * length, 6 * limit * width + 2 * limit * length),
        compiler_params=pltpu.CompilerParams(vmem_limit_bytes=48 * MEGA),
    )(table, z, target)


def head_back_kernel(exp_ref, top_ref, log_ref, target_ref, low_ref, z_ref, grad_ref, table_ref, total):
    at = pl.program_id(0)
    scale = jnp.exp(top_ref[0] - log_ref[...])
    exps = exp_ref[...].astype(F32)
    hit = (entries(exps.shape) == target_ref[...]).astype(F32)
    slope = (exps * scale - hit).astype(BF16)
    table_ref[...] = mm(slope, z_ref[...]).astype(BF16)
    part = mm_tn(low_ref[...], slope)

    @pl.when(at == 0)
    def _():
        total[...] = part

    @pl.when(at > 0)
    def _():
        total[...] += part

    @pl.when(at == pl.num_programs(0) - 1)
    def _():
        grad_ref[...] = total[...].T.astype(BF16)


def head_back(exps, tops, log_norm, target, low, z):
    length, width = z.shape
    return pl.pallas_call(
        head_back_kernel,
        grid=(low.shape[0] // BLOCK,),
        out_shape=[jax.ShapeDtypeStruct((length, width), BF16), jax.ShapeDtypeStruct(low.shape, BF16)],
        in_specs=[row_block(length), line_block(length), whole_block((1, length)), whole_block((1, length))]
        + [row_block(width), whole_block((length, width))],
        out_specs=[whole_block((length, width)), row_block(width)],
        scratch_shapes=[pltpu.VMEM((width, length), F32)],
        cost_estimate=cost(4 * low.size * length, 4 * low.size + 2 * exps.size),
        compiler_params=pltpu.CompilerParams(vmem_limit_bytes=48 * MEGA),
    )(exps, tops, log_norm, target, low, z)


def token_lists(ids, start, limit):
    length = ids.shape[0]
    token = jnp.arange(length, dtype=jnp.int32)
    one, two = ids[:, None], ids[None, :]
    ahead = (two < one) | ((two == one) & (token[None, :] < token[:, None]))
    place = jnp.sum(ahead.astype(jnp.int32), 1)
    at = place[:, None] == token[None, :]
    order = jnp.sum(jnp.where(at, token[:, None], 0), 0)
    ordered = jnp.sum(jnp.where(at, ids[:, None], 0), 0)
    edges = start + jnp.minimum(jnp.arange(blocks_of(limit) + 1) * BLOCK, limit)
    bounds = jnp.sum((ids[None, :] < edges[:, None]).astype(jnp.int32), 1)
    return ordered - start, order, bounds


def add_rows(total, ids_ref, order_ref, bounds_ref, grad_ref, first=0):
    at = pl.program_id(0) + first

    def step(k, carry):
        row, token = ids_ref[k] - at * BLOCK, order_ref[k]
        total[pl.ds(row, 1), :] += grad_ref[pl.ds(token, 1), :]
        return carry

    lax.fori_loop(bounds_ref[at], bounds_ref[at + 1], step, 0)


def own_rows_kernel(ids_ref, order_ref, bounds_ref, table_ref, grad_ref, out_ref, square_ref, total):
    total[...] = table_ref[...].astype(F32)
    add_rows(total, ids_ref, order_ref, bounds_ref, grad_ref)
    full = total[...]
    out_ref[...] = full.astype(BF16)

    @pl.when(pl.program_id(0) == 0)
    def _():
        square_ref[...] = jnp.zeros_like(square_ref)

    square_ref[...] += jnp.sum(full * full, 0, keepdims=True)


def add_own_rows(table, lists, grad):
    width = table.shape[1]
    return pl.pallas_call(
        own_rows_kernel,
        grid_spec=pltpu.PrefetchScalarGridSpec(
            num_scalar_prefetch=3,
            grid=(table.shape[0] // BLOCK,),
            in_specs=[row_block(width), whole_block(grad.shape)],
            out_specs=[row_block(width), whole_block((1, width))],
            scratch_shapes=[pltpu.VMEM((BLOCK, width), F32)],
        ),
        out_shape=[jax.ShapeDtypeStruct(table.shape, BF16), jax.ShapeDtypeStruct((1, width), F32)],
        cost_estimate=cost(0, 4 * table.size),
        compiler_params=pltpu.CompilerParams(vmem_limit_bytes=56 * MEGA),
    )(*lists, table, grad)


def table_sum_kernel(first, ids_ref, order_ref, bounds_ref, share_ref, *refs):
    low_ref, z_ref, log_ref, target_ref, own_ref, grad_ref, out_ref, total = refs
    exps = jnp.exp(mm_nt(low_ref[...], z_ref[...]) - log_ref[...])
    hit = (entries(exps.shape, first) == target_ref[...]).astype(F32)
    total[...] = mm((exps - hit).astype(BF16), z_ref[...])
    add_rows(total, ids_ref, order_ref, bounds_ref, grad_ref, first)
    out_ref[...] = (share_ref[0] * own_ref[...].astype(F32) + share_ref[1] * total[...]).astype(BF16)


def table_sum(own, low, z, log_norm, target, lists, grad, shares, first, count):
    length, width = z.shape
    rows = lambda i, *_: (i + first, 0)
    return pl.pallas_call(
        functools.partial(table_sum_kernel, first),
        grid_spec=pltpu.PrefetchScalarGridSpec(
            num_scalar_prefetch=4,
            grid=(count,),
            in_specs=[pl.BlockSpec((BLOCK, width), rows), whole_block((length, width))]
            + [whole_block((1, length)), whole_block((1, length))]
            + [pl.BlockSpec((BLOCK, width), rows), whole_block(grad.shape)],
            out_specs=row_block(width),
            scratch_shapes=[pltpu.VMEM((BLOCK, width), F32)],
        ),
        out_shape=jax.ShapeDtypeStruct((count * BLOCK, width), BF16),
        cost_estimate=cost(4 * count * BLOCK * width * length, 6 * count * BLOCK * width),
        compiler_params=pltpu.CompilerParams(vmem_limit_bytes=48 * MEGA),
    )(*lists, shares, low, z, log_norm, target, own, grad)


def turned(line, height):
    return jnp.broadcast_to(line, (height, line.shape[1])).T


def gradient_kernel(limit, count, divisor, first, *refs):
    sums, (noise_ref, old_ref), outs = refs[:count], refs[count : count + 2], refs[-5:]
    grad_ref, rows_ref, cols_ref, scaled_ref, level_ref = outs
    total = sums[0][...].astype(F32)
    for item in sums[1:]:
        total = total + item[...].astype(F32)
    grad = (total + NOISE * CLIP * noise_ref[...]) * (1.0 / divisor)
    inside = entries((BLOCK, 1), first) < limit
    grad_ref[...] = grad
    squares = jnp.where(inside, grad * grad, 0.0)
    mean = jnp.sum(squares, 1, keepdims=True) / grad.shape[1] + 1e-30
    old = turned(old_ref[0], 128)[:, :1]
    rows = DECAY * old + (1.0 - DECAY) * mean
    rows_ref[0] = line_of(rows)

    @pl.when(pl.program_id(0) == 0)
    def _():
        cols_ref[...] = jnp.zeros_like(cols_ref)
        scaled_ref[...] = jnp.zeros_like(scaled_ref)
        level_ref[...] = jnp.zeros_like(level_ref)

    cols_ref[...] += jnp.sum(squares, 0, keepdims=True)
    scaled_ref[...] += jnp.sum(squares * (1.0 / rows), 0, keepdims=True)
    level_ref[...] += jnp.broadcast_to(jnp.sum(jnp.where(inside, rows, 0.0), 0, keepdims=True), level_ref.shape)


def table_gradient(sums, noise, old, divisor, first, count, into=None):
    limit, width = noise.shape
    shape = jax.ShapeDtypeStruct
    rows = pl.BlockSpec((BLOCK, width), lambda i: (i + first, 0))
    extra = [] if into is None else [into]
    return pl.pallas_call(
        functools.partial(gradient_kernel, limit, len(sums), divisor, first),
        grid=(count,),
        out_shape=[shape((limit, width), F32), shape((count, 1, BLOCK), F32)]
        + [shape((1, width), F32)] * 2
        + [shape((1, 128), F32)],
        in_specs=[row_block(width)] * len(sums)
        + [rows, pl.BlockSpec((1, 1, BLOCK), lambda i: (i + first, 0, 0))]
        + [pl.BlockSpec(memory_space=pl.ANY)] * len(extra),
        out_specs=[rows, line_block(BLOCK), whole_block((1, width)), whole_block((1, width))]
        + [whole_block((1, 128))],
        input_output_aliases={len(sums) + 2: 0} if extra else {},
        cost_estimate=cost(0, (8 + 2 * len(sums)) * count * BLOCK * width),
        compiler_params=pltpu.CompilerParams(vmem_limit_bytes=48 * MEGA),
    )(*sums, noise, old, *extra)


SIDE = 256


def pack_small(pos_ex, layer_packed, small_ex):
    tall = pos_ex.shape[0] // 4
    pos = jnp.pad(pos_ex, ((0, 0), (0, SIDE - pos_ex.shape[1])))
    pos = [pos[k * tall : (k + 1) * tall] for k in range(4)]
    blank = jnp.zeros_like(pos[0])
    pieces = [layer_packed, jnp.concatenate(pos[:3], 1), jnp.concatenate([pos[3], blank, blank], 1)]
    pieces.append(jnp.pad(small_ex, ((0, 32 - small_ex.shape[0]), (0, 0))))
    return jnp.concatenate(pieces, 0)


def line_of(column):
    return jnp.broadcast_to(column, (column.shape[0], 128)).T[:1]


BY_ROW = (False, True, True, True, False)


def small_gradients_kernel(divisor, *refs):
    packed, small, small_second, small_noise = refs[:4]
    weights, noises, grads = (refs[4 + 5 * k : 9 + 5 * k] for k in range(3))
    small_outs, (to_col, to_row, square_ref) = refs[19:22], refs[22:]
    width = small.shape[1]
    scale = 1.0 / divisor
    side = weights[1].shape[0]
    cuts = (0, weights[1].shape[1], weights[1].shape[1] + weights[2].shape[1])
    for index in (1, 2, 3):
        at, end, lane_to = cuts[index - 1], cuts[index - 1] + weights[index].shape[1], 0
        while at < end:
            piece, lane = at // width, at % width
            size = min(width - lane, end - at)
            part = packed[piece * side : (piece + 1) * side, lane : lane + size].astype(F32)
            lanes = slice(lane_to, lane_to + size)
            grads[index][:, lanes] = (part + NOISE * CLIP * noises[index][:, lanes]) * scale
            at, lane_to = at + size, lane_to + size
    first = side * ((cuts[2] + weights[3].shape[1]) // width)
    down = weights[4].shape[0]
    grads[4][...] = (packed[first : first + down, :].astype(F32) + NOISE * CLIP * noises[4][...]) * scale
    first += down
    tall, wide = weights[0].shape[0] // 4, weights[0].shape[1]
    for k in range(4):
        lane, start = SIDE * (k % 3), first + tall * (k // 3)
        part = packed[start : start + tall, lane : lane + wide].astype(F32)
        lines = slice(k * tall, (k + 1) * tall)
        grads[0][lines] = (part + NOISE * CLIP * noises[0][lines]) * scale
    first += 2 * tall

    to_col[...] = jnp.zeros_like(to_col)
    to_row[...] = jnp.zeros_like(to_row)
    lane = lax.broadcasted_iota(jnp.int32, (1, width), 1)
    weight_sq = jnp.zeros((1, width), F32)
    for index, along in enumerate(BY_ROW):
        squares = grads[index][...] * grads[index][...]
        row_sum = line_of(jnp.sum(squares, 1, keepdims=True))
        col_sum = jnp.sum(squares, 0, keepdims=True)
        rows_to, cols_to = (to_col, to_row) if along else (to_row, to_col)
        rows_to[index : index + 1, : row_sum.shape[1]] = row_sum
        cols_to[index : index + 1, : col_sum.shape[1]] = col_sum
        total = jnp.sum(jnp.sum(weights[index][...] * weights[index][...], 0, keepdims=True), 1, keepdims=True)
        weight_sq = weight_sq + jnp.where(lane == index, total, 0.0)
    square_ref[...] = weight_sq

    count = small.shape[0]
    small_grad = (packed[first : first + 16, :].astype(F32)[:count] + NOISE * CLIP * small_noise[...]) * scale
    second_new = DECAY * small_second[...] + (1.0 - DECAY) * (small_grad * small_grad + 1e-30)
    update = small_grad * lax.rsqrt(second_new)
    mean = lambda item: jnp.sum(jnp.sum(item * item, 0, keepdims=True), 1, keepdims=True) / (count * width)
    size = RATE * jnp.maximum(1e-3, jnp.sqrt(mean(small[...])))
    size = size / jnp.maximum(1.0, jnp.sqrt(mean(update)))
    small_outs[0][...] = small_grad
    small_outs[1][...] = second_new
    small_outs[2][...] = small[...] - size * update


def small_gradients(packed, small, small_second, small_noise, weights, noises, divisor):
    width = small.shape[1]
    wide = max(item.shape[1] for item in weights)
    shape = lambda dims: jax.ShapeDtypeStruct(dims, F32)
    operands = [packed, small, small_second, small_noise, *weights, *noises]
    shapes = [item.shape for item in weights] + [small.shape] * 3 + [(8, width), (8, wide), (1, width)]
    out = pl.pallas_call(
        functools.partial(small_gradients_kernel, divisor),
        grid=(1,),
        out_shape=[shape(dims) for dims in shapes],
        in_specs=[whole_block(item.shape) for item in operands],
        out_specs=[whole_block(dims) for dims in shapes],
        compiler_params=pltpu.CompilerParams(vmem_limit_bytes=48 * MEGA),
        cost_estimate=cost(0, 16 * MEGA),
    )(*operands)
    return out[:5], out[5:8], out[8:]


def statistics_kernel(n_row, vocab, *refs):
    table_over, over_cols, over_rows, old_lines = refs[:4]
    grads, (lines_ref, factor_ref), held = refs[4:9], refs[9:11], refs[11:16]
    to_level, both_slots, col_slots, row_slots, level_slots, send_sems, recv_sems, local_sems = refs[16:]
    n_col, width = 2, table_over.shape[1]
    everyone = n_row * n_col
    copies = [pltpu.make_async_copy(grads[k], held[k], local_sems.at[k]) for k in range(5)]
    for copy in copies:
        copy.start()
    link = Link(send_sems, recv_sems)
    me, peers = link.plane_peers(n_row)
    link.greet([(device, None) for _, device in peers])
    row_peers = [((link.row + k) % n_row, link.device(row=(link.row + k) % n_row)) for k in range(1, n_row)]
    meet(link, 0, table_over, both_slots, me, peers)
    meet(link, everyone, over_cols, col_slots, link.col, [(1 - link.col, link.device(col=1 - link.col))])
    meet(link, everyone + n_col, over_rows, row_slots, link.row, row_peers)
    both, over_col, over_row = added(both_slots), added(col_slots), added(row_slots)
    for copy in copies:
        copy.wait()

    lane = lax.broadcasted_iota(jnp.int32, (1, 128), 1)

    def pick(line, at):
        return jnp.sum(jnp.where(lane == at, line[:, :128], 0.0), 1, keepdims=True)

    def step_size(weight_sum, level, square_sum, entries_all):
        size = RATE * jnp.maximum(1e-3, jnp.sqrt(weight_sum / entries_all))
        size = size / jnp.maximum(1.0, jnp.sqrt(square_sum * level / entries_all))
        return size * jnp.sqrt(level)

    whole = lambda line: jnp.sum(line, 1, keepdims=True)
    cols_new = DECAY * table_over[5:6] + (1.0 - DECAY) * (both[0:1] / vocab + 1e-30)
    level = pick(both[2:3], 0) / vocab
    size = step_size(whole(both[3:4]), level, whole(both[1:2] / cols_new), float(vocab * width))
    factor_ref[...] = jnp.zeros_like(factor_ref)
    factor_ref[0:1] = cols_new
    factor_ref[1:2] = size * lax.rsqrt(cols_new)

    lines_ref[...] = jnp.zeros_like(lines_ref)
    levels = jnp.zeros((1, 128), F32)
    for index, along in enumerate(BY_ROW):
        rows, cols = held[index].shape
        parts_rows, parts_cols = (n_row, n_col) if along else (n_col, n_row)
        rows_from, cols_from = (over_col, over_row) if along else (over_row, over_col)
        row_mean = rows_from[index : index + 1, :rows] / (cols * parts_cols) + 1e-30
        col_mean = cols_from[index : index + 1, :cols] / (rows * parts_rows) + 1e-30
        rows_line = DECAY * old_lines[index : index + 1, :rows] + (1.0 - DECAY) * row_mean
        cols_line = DECAY * old_lines[8 + index : 9 + index, :cols] + (1.0 - DECAY) * col_mean
        lines_ref[index : index + 1, :rows] = rows_line
        lines_ref[8 + index : 9 + index, :cols] = cols_line
        level = whole(rows_line) / (rows * parts_rows * parts_cols)
        scaled = held[index][...] * held[index][...] * (1.0 / turned(rows_line, 128)[:, :1])
        scaled = whole(jnp.sum(scaled, 0, keepdims=True) / cols_line)
        levels = levels + jnp.where(lane == 2 * index, level, 0.0) + jnp.where(lane == 2 * index + 1, scaled, 0.0)
    to_level[...] = jnp.zeros_like(to_level)
    to_level[:1] = levels
    meet(link, everyone + n_col + n_row, to_level, level_slots, me, peers)
    levels = added(level_slots)[:1]
    sizes = jnp.zeros((1, 128), F32)
    for index in range(5):
        entries_all = float(held[index].shape[0] * held[index].shape[1] * everyone)
        size = step_size(pick(both[4:5], index), pick(levels, 2 * index), pick(levels, 2 * index + 1), entries_all)
        sizes = sizes + jnp.where(lane == index, size, 0.0)
    factor_ref[2:3, :128] = sizes
    link.finish()


def statistics(table_over, over_cols, over_rows, old_lines, grads, n_row, vocab, collective_id):
    width, wide = table_over.shape[1], over_rows.shape[1]
    everyone = 2 * n_row
    vmem, hbm = pl.BlockSpec(memory_space=pltpu.VMEM), pl.BlockSpec(memory_space=pl.ANY)
    return pl.pallas_call(
        functools.partial(statistics_kernel, n_row, vocab),
        out_shape=[jax.ShapeDtypeStruct((16, wide), F32), jax.ShapeDtypeStruct((8, width), F32)],
        in_specs=[vmem] * 4 + [hbm] * 5,
        out_specs=[vmem] * 2,
        scratch_shapes=[pltpu.VMEM(item.shape, F32) for item in grads]
        + [pltpu.VMEM((8, 128), F32), pltpu.VMEM((everyone, 8, width), F32), pltpu.VMEM((2, 8, width), F32)]
        + [pltpu.VMEM((n_row, 8, wide), F32), pltpu.VMEM((everyone, 8, 128), F32)]
        + [pltpu.SemaphoreType.DMA((3 * everyone,)), pltpu.SemaphoreType.DMA((2 * everyone + 2 + n_row,))]
        + [pltpu.SemaphoreType.DMA((5,))],
        compiler_params=pltpu.CompilerParams(
            collective_id=collective_id, has_side_effects=True, vmem_limit_bytes=32 * MEGA
        ),
    )(table_over, over_cols, over_rows, old_lines, *grads)


def update_kernel(table_ref, table_grad_ref, rows_ref, factor_ref, lines_ref, *refs):
    weights, grads, (table_new_ref, table_cols_ref) = refs[:5], refs[5:10], refs[10:12]
    rows_outs, cols_outs, news = refs[12:17], refs[17:22], refs[22:27]
    rows = turned(lax.rsqrt(rows_ref[0]), 128)[:, :1]
    table_new_ref[...] = table_ref[...] - table_grad_ref[...] * rows * factor_ref[1:2]

    @pl.when(pl.program_id(0) == 0)
    def _():
        table_cols_ref[...] = factor_ref[0:1]
        for index in range(5):
            count_rows, count_cols = weights[index].shape
            rows_line = lines_ref[index : index + 1, :count_rows]
            cols_line = lines_ref[8 + index : 9 + index, :count_cols]
            rows_outs[index][...] = rows_line
            cols_outs[index][...] = cols_line
            rows = turned(lax.rsqrt(rows_line), 128)[:, :1]
            factors = factor_ref[2:3, index : index + 1] * lax.rsqrt(cols_line)
            news[index][...] = weights[index][...] - grads[index][...] * rows * factors


def update(table, table_grad, table_rows, factors, lines, weights, grads):
    limit, width = table.shape
    shape = lambda dims: jax.ShapeDtypeStruct(dims, F32)
    small_shapes = [(1, width)] + [(1, item.shape[0]) for item in weights] + [(1, item.shape[1]) for item in weights]
    small_shapes += [item.shape for item in weights]
    out = pl.pallas_call(
        update_kernel,
        grid=(blocks_of(limit),),
        out_shape=[shape(table.shape)] + [shape(dims) for dims in small_shapes],
        in_specs=[row_block(width), row_block(width), line_block(BLOCK), whole_block(factors.shape)]
        + [whole_block(lines.shape)]
        + [whole_block(item.shape) for item in weights] * 2,
        out_specs=[row_block(width)] + [whole_block(dims) for dims in small_shapes],
        compiler_params=pltpu.CompilerParams(vmem_limit_bytes=56 * MEGA),
        cost_estimate=cost(0, 3 * 4 * limit * width),
    )(table, table_grad, table_rows, factors, lines, *weights, *grads)
    flat = lambda items: [item[0] for item in items]
    return out[0], out[1][0], flat(out[2:7]), flat(out[7:12]), out[12:]


HIDDEN = 1024
CHUNK = 512


def normed_of(inputs):
    center = jnp.mean(inputs, -1, keepdims=True)
    var = jnp.mean(inputs * inputs, -1, keepdims=True) - center * center
    inv = lax.rsqrt(var + 1e-05)
    return (inputs - center) * inv, inv


def normed_back(upstream, normed, inv, gain):
    scaled = upstream * gain
    first = jnp.mean(scaled, -1, keepdims=True)
    second = jnp.mean(scaled * normed, -1, keepdims=True)
    return inv * (scaled - first - normed * second)


def columns_sum(item):
    return jnp.sum(item.astype(F32), 0, keepdims=True)


def chunks_of(length):
    return [slice(at, at + CHUNK) for at in range(0, length, CHUNK)]


GELU_SCALE = (2.0 / jnp.pi) ** 0.5


def gelu_parts(inputs):
    square = inputs * inputs
    turn = jnp.tanh(inputs * (GELU_SCALE + (GELU_SCALE * 0.044715) * square))
    half = 0.5 + 0.5 * turn
    inner = GELU_SCALE + (3.0 * GELU_SCALE * 0.044715) * square
    return inputs * half, half + 0.5 * inputs * (1.0 - turn * turn) * inner


def middle_kernel(start_ref, mixed_ref, attn_ref, up_ref, bias_ref, down_ref, small_ref, *outs):
    mid_ref, low_ref, out_ref, z_ref, total = outs
    at = pl.program_id(0)
    length = start_ref.shape[0]

    @pl.when(at == 0)
    def _():
        for rows in chunks_of(length):
            mid = start_ref[rows].astype(F32) + mm(mixed_ref[rows], attn_ref[...]) + small_ref[4:5]
            mid_ref[rows] = mid
            low_ref[rows] = (normed_of(mid)[0] * small_ref[5:6] + small_ref[6:7]).astype(BF16)
            total[rows] = mid + small_ref[11:12]

    for rows in chunks_of(length):
        hidden = gelu_parts(mm(low_ref[rows], up_ref[...]) + bias_ref[...])[0].astype(BF16)
        total[rows] += mm_nt(hidden, down_ref[...])

    @pl.when(at == pl.num_programs(0) - 1)
    def _():
        for rows in chunks_of(length):
            out = total[rows]
            out_ref[rows] = out
            z_ref[rows] = (normed_of(out)[0] * small_ref[12:13] + small_ref[13:14]).astype(BF16)


def middle_forward(start, mixed, attn, up, up_bias, down, small):
    length, width = start.shape
    shape = jax.ShapeDtypeStruct
    whole = lambda item: whole_block(item.shape)
    tokens = whole_block((length, width))
    return pl.pallas_call(
        middle_kernel,
        grid=(up.shape[1] // HIDDEN,),
        out_shape=[shape((length, width), kind) for kind in (F32, BF16, F32, BF16)],
        in_specs=[whole(start), whole(mixed), whole(attn), pl.BlockSpec((width, HIDDEN), lambda i: (0, i))]
        + [pl.BlockSpec((1, HIDDEN), lambda i: (0, i)), pl.BlockSpec((width, HIDDEN), lambda i: (0, i))]
        + [whole(small)],
        out_specs=[tokens] * 4,
        scratch_shapes=[pltpu.VMEM((length, width), F32)],
        cost_estimate=cost(4 * length * width * up.shape[1], 16 * length * width),
        compiler_params=pltpu.CompilerParams(vmem_limit_bytes=56 * MEGA),
    )(start, mixed, attn, up, up_bias, down, small)


def middle_back_kernel(*refs):
    grad_ref, out_ref, mid_ref, low_ref, attn_ref, up_ref, bias_ref, down_ref, small_ref = refs[:9]
    down_grad_ref, pre_ref, act_ref, pre_sum_ref, mid_grad_ref, branch_ref, mixed_ref, rows_ref, total = refs[9:]
    at = pl.program_id(0)
    length, width = grad_ref.shape

    @pl.when(at == 0)
    def _():
        rows_ref[...] = jnp.zeros_like(rows_ref)
        for rows in chunks_of(length):
            grad = grad_ref[rows].astype(F32)
            normed, inv = normed_of(out_ref[rows])
            back = normed_back(grad, normed, inv, small_ref[12:13])
            mid_grad_ref[rows] = back
            low = back.astype(BF16)
            down_grad_ref[rows] = low
            rows_ref[0:1] += columns_sum(grad * normed)
            rows_ref[1:2] += columns_sum(grad)
            rows_ref[2:3] += columns_sum(low)
        total[...] = jnp.zeros_like(total)

    pre_sum = jnp.zeros((1, pre_ref.shape[1]), F32)
    for rows in chunks_of(length):
        act, slope = gelu_parts(mm(low_ref[rows], up_ref[...]) + bias_ref[...])
        act_ref[rows] = act.astype(BF16)
        pre = (mm(down_grad_ref[rows], down_ref[...]) * slope).astype(BF16)
        pre_ref[rows] = pre
        pre_sum = pre_sum + columns_sum(pre)
        total[rows] += mm_nt(pre, up_ref[...])
    pre_sum_ref[...] = pre_sum

    @pl.when(at == pl.num_programs(0) - 1)
    def _():
        for rows in chunks_of(length):
            grad = total[rows]
            normed, inv = normed_of(mid_ref[rows])
            mid_grad = mid_grad_ref[rows] + normed_back(grad, normed, inv, small_ref[5:6])
            mid_grad_ref[rows] = mid_grad
            low = mid_grad.astype(BF16)
            branch_ref[rows] = low
            rows_ref[3:4] += columns_sum(grad * normed)
            rows_ref[4:5] += columns_sum(grad)
            rows_ref[5:6] += columns_sum(low)
            mixed_ref[rows] = mm_nt(low, attn_ref[...]).astype(BF16)


def middle_back(grad, out, mid, low, attn, up, up_bias, down, small):
    length, width = grad.shape
    hidden = up.shape[1]
    shape = jax.ShapeDtypeStruct
    whole = lambda item: whole_block(item.shape)
    tokens = whole_block((length, width))
    wide = pl.BlockSpec((length, HIDDEN), lambda i: (0, i))
    weight = pl.BlockSpec((width, HIDDEN), lambda i: (0, i))
    line = pl.BlockSpec((1, HIDDEN), lambda i: (0, i))
    return pl.pallas_call(
        middle_back_kernel,
        grid=(hidden // HIDDEN,),
        out_shape=[shape((length, width), BF16), shape((length, hidden), BF16), shape((length, hidden), BF16)]
        + [shape((1, hidden), F32), shape((length, width), F32), shape((length, width), BF16)]
        + [shape((length, width), BF16), shape((8, width), F32)],
        in_specs=[tokens] * 4 + [whole(attn), weight, line, weight, whole(small)],
        out_specs=[tokens, wide, wide, line, tokens, tokens, tokens, whole_block((8, width))],
        scratch_shapes=[pltpu.VMEM((length, width), F32)],
        cost_estimate=cost(6 * length * width * hidden, 40 * length * width),
        compiler_params=pltpu.CompilerParams(vmem_limit_bytes=58 * MEGA),
    )(grad, out, mid, low, attn, up, up_bias, down, small)


def start_back_kernel(packed_ref, weight_ref, mid_grad_ref, start_ref, small_ref, out_ref, low_ref, wide_ref, rows_ref):
    width = start_ref.shape[1]
    grad = sum(mm_nt(packed_ref[k], weight_ref[:, k * width : (k + 1) * width]) for k in range(3))
    normed, inv = normed_of(start_ref[...].astype(F32))
    back = mid_grad_ref[...] + normed_back(grad, normed, inv, small_ref[0:1])
    out_ref[...] = back
    low_ref[...] = back.astype(BF16)
    wide_ref[...] = back.astype(BF16).astype(F32)

    @pl.when(pl.program_id(0) == 0)
    def _():
        rows_ref[...] = jnp.zeros_like(rows_ref)

    rows_ref[0:1] += columns_sum(grad * normed)
    rows_ref[1:2] += columns_sum(grad)
    rows_ref[2:3] += columns_sum(packed_ref[0])
    rows_ref[3:4] += columns_sum(packed_ref[2])
    rows_ref[4:5] += columns_sum(back * back)


def start_back(packed_grad, weight, mid_grad, start, small):
    length, width = start.shape
    shape = jax.ShapeDtypeStruct
    tokens = pl.BlockSpec((CHUNK, width), lambda i: (i, 0))
    return pl.pallas_call(
        start_back_kernel,
        grid=(length // CHUNK,),
        out_shape=[shape((length, width), kind) for kind in (F32, BF16, F32)] + [shape((8, width), F32)],
        in_specs=[pl.BlockSpec((3, CHUNK, width), lambda i: (0, i, 0)), whole_block(weight.shape), tokens, tokens]
        + [whole_block(small.shape)],
        out_specs=[tokens, tokens, tokens, whole_block((8, width))],
        cost_estimate=cost(6 * length * width * width, 20 * length * width),
        compiler_params=pltpu.CompilerParams(vmem_limit_bytes=40 * MEGA),
    )(packed_grad, weight, mid_grad, start, small)


def weight_grads_kernel(place_ref, ones_ref, mixed_ref, low_ref, *refs):
    packed, (branch_ref, pre_ref, down_ref, act_ref), (out_ref, square_ref, wide) = refs[:3], refs[3:7], refs[7:]
    width = ones_ref.shape[1]
    tall = width // 4
    start = pl.multiple_of(place_ref[0], 128)
    skip = pl.multiple_of(place_ref[1], 8)
    pieces = (
        (ones_ref, ((packed[0], 0, 0), (packed[1], 0, 1), (packed[2], 1, 0))),
        (mixed_ref, ((branch_ref, 1, 1),)),
        (low_ref, ((pre_ref, 2, 0), (pre_ref, 2, 1), (pre_ref, 3, 0), (pre_ref, 3, 1))),
    )
    half = width // 2
    square = jnp.zeros((1, half), F32)
    for left_ref, rights in pieces:
        left = left_ref[:, pl.ds(start, SIDE)].T
        for k, (right_ref, piece, side) in enumerate(rights):
            right = right_ref[0] if len(right_ref.shape) == 3 else right_ref[:, pl.ds(k * half, half)]
            wide[...] = mm(left, right)
            grad = wide[pl.ds(skip, tall), :]
            out_ref[piece * tall : (piece + 1) * tall, side * half : (side + 1) * half] = grad
            square = square + jnp.sum(grad * grad, 0, keepdims=True)
    left = down_ref[...].T
    for side in range(2):
        grad = mm(left, act_ref[:, side * half : (side + 1) * half])
        out_ref[4 * tall :, side * half : (side + 1) * half] = grad
        square = square + jnp.sum(grad * grad, 0, keepdims=True)
    square_ref[...] = square


def weight_grads(ln_one, mixed, low, packed_grad, branch, pre, down_grad, act, row_at, col_at):
    length, width = ln_one.shape
    half, tall = width // 2, width // 4
    hidden = pre.shape[1] // 2
    shape = jax.ShapeDtypeStruct
    first = row_at * tall
    place = jnp.stack([first // 128 * 128, first % 128, row_at, col_at]).astype(jnp.int32)
    unit = lambda k: pl.BlockSpec((1, length, half), lambda i, at: ((3 * at[3] + k) // 2, 0, (3 * at[3] + k) % 2))
    return pl.pallas_call(
        weight_grads_kernel,
        grid_spec=pltpu.PrefetchScalarGridSpec(
            num_scalar_prefetch=1,
            grid=(1,),
            in_specs=[whole_block((length, width))] * 3
            + [unit(k) for k in range(3)]
            + [pl.BlockSpec((length, half), lambda i, at: (0, at[3])), pl.BlockSpec((length, hidden), lambda i, at: (0, at[3]))]
            + [pl.BlockSpec((length, half), lambda i, at: (0, at[3])), pl.BlockSpec((length, width), lambda i, at: (0, at[2]))],
            out_specs=[whole_block((4 * tall + half, width)), whole_block((1, half))],
            scratch_shapes=[pltpu.VMEM((SIDE, half), F32)],
        ),
        out_shape=[shape((4 * tall + half, width), F32), shape((1, half), F32)],
        cost_estimate=cost(2 * length * width * width * 2, 16 * length * width),
        compiler_params=pltpu.CompilerParams(vmem_limit_bytes=56 * MEGA),
    )(place, ln_one, mixed, low, packed_grad, packed_grad, packed_grad, branch, pre, down_grad, act)


def body(
    token_ids,
    target_ids,
    included,
    tok_table,
    pos_table,
    qkv_weight,
    attn_weight,
    up_weight,
    down_weight,
    small_params,
    table_rows,
    table_cols,
    pos_rows,
    pos_cols,
    qkv_rows,
    qkv_cols,
    attn_rows,
    attn_cols,
    up_rows,
    up_cols,
    down_rows,
    down_cols,
    small_second,
    table_noise,
    pos_noise,
    qkv_noise,
    attn_noise,
    up_noise,
    down_noise,
    small_noise,
):
    n_row = lax.axis_size("row")
    n_col = lax.axis_size("col")
    n_data = lax.axis_size("dp")
    row_at = lax.axis_index("row")
    col_at = lax.axis_index("col")
    ids, targets = token_ids[0], target_ids[0]
    length = ids.shape[0]
    width = small_params.shape[1]
    vocab_here = tok_table.shape[0]
    vocab_start = (col_at * n_row + row_at) * vocab_here
    small = small_params

    target = targets - vocab_start
    target = jnp.where((target >= 0) & (target < vocab_here), target, -1)[None]
    lists = token_lists(ids, vocab_start, vocab_here)
    tuned = (n_data, n_row, n_col) == (4, 4, 2)
    block = length // (n_row * n_col)
    if tuned:
        beside = lambda item: lax.ppermute(item, "dp", [(at, at ^ 2) for at in range(4)])
        met_ids, met_target = beside(jnp.stack([ids, targets]))
        met_target = met_target - vocab_start
        met_target = jnp.where((met_target >= 0) & (met_target < vocab_here), met_target, -1)[None]
        met_lists = token_lists(met_ids, vocab_start, vocab_here)

    weights_in = [tok_table, pos_table, qkv_weight, attn_weight, up_weight, down_weight]
    noises = [table_noise, pos_noise, qkv_noise, attn_noise, up_noise, down_noise]
    lows = [item.astype(BF16) for item in weights_in[2:]]
    local_ids = ids - vocab_start
    inside = (local_ids >= 0) & (local_ids < vocab_here)
    safe_ids = jnp.clip(local_ids, 0, vocab_here - 1)
    looked = jnp.where(inside[:, None], jnp.take(tok_table, safe_ids, axis=0), 0.0).astype(BF16)
    if tuned:
        pos_blocks = pos_table.reshape(n_row, block, -1)
        pieces = []
        for k in range(n_row):
            piece = lax.dynamic_index_in_dim(pos_blocks, row_at ^ k, 0, False)
            if k:
                piece = lax.ppermute(piece, "row", [(at, at ^ k) for at in range(n_row)])
            pieces.append(piece)
        pieces = jnp.stack(pieces)
        pos_own = jnp.concatenate([pieces[row_at ^ at] for at in range(n_row)], 1)
        shards = [item.reshape(n_data, -1, item.shape[1]) for item in lows]
        start, own_rows, qkv_full, attn_full, up_full, down_full = front(
            looked.reshape(n_col, n_row, block, width), pos_own, shards, n_row
        )
        stream_in = start.reshape(length, width)
        qkv_full, attn_full, up_full, down_full = (
            item.reshape(width, -1) for item in (qkv_full, attn_full, up_full, down_full)
        )
    else:
        stream_in = (plane_sum(looked).astype(F32) + gather_matrix(pos_table, 1)).astype(BF16)
        qkv_full, attn_full, up_full = (gather_matrix(item, 0) for item in lows[:3])
        down_full = gather_matrix(lows[3], 1)

    ln_one = (normed_of(stream_in.astype(F32))[0] * small[0] + small[1]).astype(BF16)
    bias = jnp.concatenate([small[2], jnp.zeros_like(small[2]), small[3]])
    packed = (mm(ln_one, qkv_full) + bias).astype(BF16)
    mixed, attn_log = attend(packed)
    up_bias = small[7:11].reshape(1, -1)
    stream_mid, ln_two, stream_out, ln_fin = middle_forward(
        stream_in, mixed, attn_full, up_full, up_bias, down_full, small
    )

    table_low, exps, tops, exp_sums, picked, table_sq = head(tok_table, ln_fin, target)
    if tuned:
        met_z = beside(ln_fin)
        log_norm, picked = log_total(tops, exp_sums, picked, n_row, 3)
        met_log = beside(log_norm)
    else:
        top = lax.pmax(jnp.max(tops, 0), PLANE)
        log_norm = top + jnp.log(plane_sum(jnp.sum(exp_sums * jnp.exp(tops - top[None]), 0)))
        picked = plane_sum(picked)
    loss = jnp.sum(log_norm - picked)
    final_part, table_ex = head_back(exps, tops, log_norm, target, table_low, ln_fin)
    if tuned:
        final_part = plane_total(final_part.reshape(n_col, n_row, block, width), 2)
        final_grad = final_part.reshape(length, width)
    else:
        final_grad = plane_sum(final_part)

    down_grad, pre_grad, up_act, pre_sum, mid_grad, branch_grad, mixed_grad, mid_rows = middle_back(
        final_grad, stream_out, stream_mid, ln_two, attn_full, up_full, up_bias, down_full, small
    )
    packed_grad = attend_back(packed, mixed_grad, attn_log)
    grad_in, emb_low, emb_grad, start_rows = start_back(packed_grad, qkv_full, mid_grad, stream_in, small)
    if tuned:
        met_grad = beside(emb_low)
        layer_packed, layer_sq = weight_grads(
            ln_one, mixed, ln_two, packed_grad, branch_grad, pre_grad, down_grad, up_act, row_at, col_at
        )
        layer_sq = jnp.sum(layer_sq)
    else:
        all_grads = packed_grad.transpose(1, 0, 2).reshape(length, -1)

        def columns_of(array, at, parts):
            size = array.shape[1] // parts
            return lax.dynamic_slice_in_dim(array, at * size, size, 1)

        layer_ex = [
            mm_tn(columns_of(left, at_left, n_left), columns_of(right, at_right, n_right))
            for left, at_left, n_left, right, at_right, n_right in (
                (ln_one, row_at, n_row, all_grads, col_at, n_col),
                (mixed, row_at, n_row, branch_grad, col_at, n_col),
                (ln_two, row_at, n_row, pre_grad, col_at, n_col),
                (down_grad, col_at, n_col, up_act, row_at, n_row),
            )
        ]
        layer_sq = sum(jnp.sum(item * item) for item in layer_ex)
    tok_here, dim_here = pos_table.shape
    pos_ex = lax.dynamic_slice(grad_in, (col_at * tok_here, row_at * dim_here), (tok_here, dim_here))
    small_ex = jnp.concatenate(
        [start_rows[:4], mid_rows[5:6], mid_rows[3:5], pre_sum.reshape(-1, width), mid_rows[2:3], mid_rows[:2]], 0
    )
    table_ex, own_sq = add_own_rows(table_ex, lists, emb_grad)

    own_sq = jnp.sum(own_sq) + layer_sq
    same_sq = jnp.sum(start_rows[4]) + jnp.sum(small_ex * small_ex)
    taken = included[0].astype(F32)
    ex_at = lax.axis_index("dp")
    leads = (row_at + col_at == 0).astype(F32)
    at_own = (jnp.arange(n_data) == ex_at).astype(F32)
    total = jnp.concatenate([at_own * (own_sq + leads * same_sq), at_own * leads * taken, leads * taken * loss[None]])
    if tuned:
        total = jnp.pad(total, (0, 1024 - total.shape[0])).reshape(8, 128)
        total, met_grad = lax.optimization_barrier((total, met_grad))
        total = sum_small(total, n_row, 4).reshape(-1)
    else:
        total = lax.psum(lax.psum(total, PLANE), "dp")
    norm_sq, taken, loss_sum = total[:n_data], total[n_data : 2 * n_data], total[2 * n_data]
    share = taken * jnp.minimum(1.0, CLIP * lax.rsqrt(norm_sq + 1e-12))
    example_norm = jnp.sqrt(norm_sq[ex_at])
    own_share = share[ex_at]

    divisor = SAMPLE * n_data
    vocab = vocab_here * n_row * n_col
    count = blocks_of(vocab_here)
    table_old = jnp.pad(table_rows, (0, count * BLOCK - vocab_here), constant_values=1.0).reshape(count, 1, BLOCK)
    olds = [(pos_rows, pos_cols), (qkv_rows, qkv_cols), (attn_rows, attn_cols), (up_rows, up_cols)]
    olds.append((down_rows, down_cols))
    ends = (token_ids.shape[1] * jnp.sum(taken), example_norm[None])
    if tuned:
        core = ex_at % 2
        to_core = lambda item: lax.ppermute(item, "dp", [(at, at ^ 1) for at in range(4)])
        halves = (own_share * pack_small(pos_ex, layer_packed, small_ex)).astype(BF16).reshape(2, -1, width)
        half = (halves[core].astype(F32) + to_core(halves[1 - core]).astype(F32)).astype(BF16)
        shares = jnp.stack([own_share, share[ex_at ^ 2]])
        half, shares = lax.optimization_barrier((half, shares))
        half = (half.astype(F32) + beside(half).astype(F32)).astype(BF16)
        other_half = to_core(half)
        packed = jnp.concatenate(
            [jnp.where(core == 0, half, other_half), jnp.where(core == 0, other_half, half)], 0
        )

        middle = count // 2
        spans = [(0, middle), (middle, count - middle)]
        met = (met_z, met_log, met_target, met_lists, met_grad.astype(F32), shares)
        pair_sums = [table_sum(table_ex, table_low, *met, *span) for span in spans]
        pair_sums = [[item, to_core(item)] for item in pair_sums]
        into, over = None, []
        for pair, span in zip(pair_sums, spans):
            into, *more = table_gradient(pair, table_noise, table_old, divisor, *span, into)
            over.append(more)
        table_grad = into
        rows_blocks = jnp.concatenate([item[0] for item in over], 0)
        cols, scaled, level = (over[0][k] + over[1][k] for k in (1, 2, 3))
        level = jnp.pad(level[:, :1], ((0, 0), (0, width - 1)))
        small_grads, smalls, (over_cols, over_rows, squares) = small_gradients(
            packed, small_params, small_second, small_noise, weights_in[1:], noises[1:], divisor
        )
        table_over = jnp.concatenate(
            [cols, scaled, level, table_sq, squares, table_cols[None], jnp.zeros((2, width), F32)], 0
        )
        wide = over_rows.shape[1]
        lines = [jnp.pad(item, (0, wide - item.shape[0])) for pair in zip(*olds) for item in pair + (pair[0],) * 3]
        old_lines = jnp.stack(lines)
        lines, factors = statistics(table_over, over_cols, over_rows, old_lines, small_grads, n_row, vocab, 5)
        table_new, table_cols_new, rows_new, cols_new, news = update(
            tok_table, table_grad, rows_blocks, factors, lines, weights_in[1:], small_grads
        )
        outputs = [table_grad, rows_blocks.reshape(-1)[:vocab_here], table_cols_new, table_new]
        for group in zip(small_grads, rows_new, cols_new, news):
            outputs.extend(group)
        return tuple(outputs) + tuple(smalls) + (loss_sum,) + ends

    weight_total = plane_sum(
        jnp.stack([jnp.sum(table_sq)] + [jnp.sum(item * item) for item in weights_in[1:]])
    )
    table_sum_all = example_sum((own_share * table_ex.astype(F32)).astype(BF16))
    others = [(own_share * item).astype(BF16) for item in [pos_ex] + layer_ex + [small_ex]]
    sums = [example_sum(item).astype(F32) for item in others]
    grads = [(sums[index] + NOISE * CLIP * noises[index + 1]) / divisor for index in range(5)]
    table_grad, table_rows_new, *table_over = table_gradient(
        [table_sum_all], table_noise, table_old, divisor, 0, count
    )
    table_rows_new = table_rows_new.reshape(-1)[:vocab_here]
    by_row = [False, True, True, True, False]
    over = {"col": [], "row": []}
    for grad, first in zip(grads, by_row):
        squares = grad * grad + 1e-30
        over["col" if first else "row"].append(jnp.sum(squares, 1))
        over["row" if first else "col"].append(jnp.sum(squares, 0))
    over = {axis: [lax.psum(item, axis) for item in items] for axis, items in over.items()}
    table_over = [plane_sum(item[0]) for item in table_over]
    news, levels = [], []
    for index, (grad, first) in enumerate(zip(grads, by_row)):
        rows_parts, cols_parts = (n_row, n_col) if first else (n_col, n_row)
        row_sum = over["col" if first else "row"][index]
        col_sum = over["row" if first else "col"][index]
        rows_new = DECAY * olds[index][0] + (1.0 - DECAY) * (row_sum / (grad.shape[1] * cols_parts))
        cols_new = DECAY * olds[index][1] + (1.0 - DECAY) * (col_sum / (grad.shape[0] * rows_parts))
        news.append((rows_new, cols_new))
        levels += [
            jnp.sum(rows_new) / (grad.shape[0] * rows_parts * cols_parts),
            jnp.sum(grad * grad / (rows_new[:, None] * cols_new[None, :])),
        ]
    levels = plane_sum(jnp.stack(levels))

    def updated(index, weight, grad, rows_new, cols_new, level, square_sum, entries_all):
        size = RATE * jnp.maximum(1e-3, jnp.sqrt(weight_total[index] / entries_all))
        size = size / jnp.maximum(1.0, jnp.sqrt(square_sum * level / entries_all))
        size = size * jnp.sqrt(level)
        return weight - grad * lax.rsqrt(rows_new)[:, None] * (size * lax.rsqrt(cols_new))[None, :]

    table_cols_new = DECAY * table_cols + (1.0 - DECAY) * (table_over[0] / vocab + 1e-30)
    table_new = updated(
        0,
        tok_table,
        table_grad,
        table_rows_new,
        table_cols_new,
        table_over[2][0] / vocab,
        jnp.sum(table_over[1] / table_cols_new),
        vocab * width,
    )
    outputs = [table_grad, table_rows_new, table_cols_new, table_new]
    for index, grad in enumerate(grads):
        rows_new, cols_new = news[index]
        weight_new = updated(
            index + 1,
            weights_in[index + 1],
            grad,
            rows_new,
            cols_new,
            levels[2 * index],
            levels[2 * index + 1],
            grad.shape[0] * grad.shape[1] * n_row * n_col,
        )
        outputs.extend([grad, rows_new, cols_new, weight_new])
    small_grad = (sums[5] + NOISE * CLIP * small_noise) / divisor
    second_new = DECAY * small_second + (1.0 - DECAY) * (small_grad * small_grad + 1e-30)
    small_update = small_grad * lax.rsqrt(second_new)
    small_update = small_update / jnp.maximum(1.0, jnp.sqrt(jnp.mean(small_update * small_update)))
    small_size = RATE * jnp.maximum(1e-3, jnp.sqrt(jnp.mean(small_params * small_params)))
    small_new = small_params - small_size * small_update
    return tuple(outputs) + (small_grad, second_new, small_new, loss_sum) + ends


def solution(mesh):
    table, by_col, by_row = P(("col", "row"), None), P("col", "row"), P("row", "col")
    return jax.shard_map(
        body,
        mesh=mesh,
        in_specs=(P("dp", None), P("dp", None), P("dp"))
        + (table, by_col, by_row, by_row, by_row, by_col, P())
        + (P(("col", "row")), P(), P("col"), P("row"))
        + (P("row"), P("col")) * 3
        + (P("col"), P("row"), P())
        + (table, by_col, by_row, by_row, by_row, by_col, P()),
        out_specs=(table, P(("col", "row")), P(), table)
        + (by_col, P("col"), P("row"), by_col)
        + (by_row, P("row"), P("col"), by_row) * 3
        + (by_col, P("col"), P("row"), by_col)
        + (P(), P(), P(), P(), P(), P("dp")),
        check_vma=False,
    )
```

```python
import functools

import jax
import jax.numpy as jnp
from jax import lax
from jax.experimental import pallas as pl
from jax.experimental.pallas import tpu as pltpu
from jax.sharding import PartitionSpec as P

HEADS = 12
HEAD = 64
STEP = 10
CLIP = 1.0
NOISE = 0.002
SAMPLE = 0.5
RATE = 0.5
DECAY = 1.0 - STEP ** (-0.8)

F32 = jnp.float32
BF16 = jnp.bfloat16
PLANE = ("row", "col")
MESH = pl.DeviceIdType.MESH


def dot_f32(left, right, dims):
    return lax.dot_general(left, right, (dims, ((), ())), preferred_element_type=F32)


def mm(left, right):
    return dot_f32(left, right, ((1,), (0,)))


def mm_nt(left, right):
    return dot_f32(left, right, ((1,), (1,)))


def mm_tn(left, right):
    return dot_f32(left, right, ((0,), (0,)))


def gather_matrix(block, row_dim):
    part = lax.all_gather(block, "row", axis=row_dim, tiled=True)
    return lax.all_gather(part, "col", axis=1 - row_dim, tiled=True)


def plane_sum(array):
    return lax.psum(array, PLANE)


def example_sum(array):
    return lax.psum(array, "dp")


class Link:
    def __init__(self, send_sems, recv_sems):
        self.dp, self.row, self.col = (lax.axis_index(axis) for axis in ("dp", "row", "col"))
        self.x, self.core = self.dp // 2, self.dp % 2
        self.beside = 2 * (1 - self.x) + self.core
        self.sibling = 2 * self.x + 1 - self.core
        self.send_sems, self.recv_sems = send_sems, recv_sems
        self.n_send = 0
        self.open = []

    def device(self, **moved):
        return {"dp": self.dp, "row": self.row, "col": self.col, **moved}

    def send(self, src, dst, recv, device, when=None):
        sem = self.send_sems.at[self.n_send]
        self.n_send += 1
        copy = pltpu.make_async_remote_copy(
            src_ref=src,
            dst_ref=dst,
            send_sem=sem,
            recv_sem=self.recv_sems.at[recv],
            device_id=device,
            device_id_type=MESH,
        )
        self.open.append((copy, when))
        copy.start() if when is None else pl.when(when)(copy.start)

    def landed(self, dst, recv):
        pltpu.make_async_remote_copy(
            src_ref=dst,
            dst_ref=dst,
            send_sem=self.send_sems.at[0],
            recv_sem=self.recv_sems.at[recv],
            device_id=self.device(col=1 - self.col),
            device_id_type=MESH,
        ).wait_recv()

    def finish(self):
        for copy, when in self.open:
            copy.wait_send() if when is None else pl.when(when)(copy.wait_send)
        self.open = []

    def greet(self, devices):
        barrier = pltpu.get_barrier_semaphore()
        count = 0
        for device, when in devices:

            def signal(device=device):
                pl.semaphore_signal(barrier, inc=1, device_id=device, device_id_type=MESH)

            if when is None:
                signal()
                count = count + 1
            else:
                pl.when(when)(signal)
                count = count + when.astype(jnp.int32)
        pl.semaphore_wait(barrier, count)

    def plane_peers(self, n_row):
        me, peers = self.col * n_row + self.row, []
        for k in range(1, 2 * n_row):
            index = (me + k) % (2 * n_row)
            peers.append((index, self.device(row=index % n_row, col=index // n_row)))
        return me, peers

    def example_peers(self):
        return [((self.dp + k) % 4, self.device(dp=(self.dp + k) % 4)) for k in range(1, 4)]

    def plane_neighbours(self, n_row):
        return [
            (self.device(row=self.row + 1), self.row < n_row - 1),
            (self.device(row=self.row - 1), self.row > 0),
            (self.device(col=1 - self.col), None),
        ]


def run_together(*steps):
    steps = list(steps)
    while steps:
        for step in list(steps):
            try:
                next(step)
            except StopIteration:
                steps.remove(step)


def scatter_sum(link, base, n_row, part, from_col, ins, outs, own, make=None):
    row, col = link.row, link.col
    (up_in, down_in), (up_out, down_out) = ins, outs
    y_base, up_base, down_base = base, base + n_row, base + 2 * n_row
    order = [at for k in range(n_row // 2) for at in (n_row - 1 - k, k)]
    for at in order:
        if make is not None:
            make(1 - col, at)
        link.send(part.at[1 - col, at], from_col.at[at], y_base + at, link.device(col=1 - col))
    yield
    if make is not None:
        for k, at in enumerate(order):
            make(col, at)
            if k % 2:
                yield
    waiting = list(order)

    def mine(at):
        return part[col, at].astype(F32) + from_col[at].astype(F32)

    for k in range(n_row - 1):
        for at in (n_row - 1 - k, k):
            if at in waiting:
                waiting.remove(at)
                link.landed(from_col.at[at], y_base + at)
        for at, going, more, source, target, base_at, device in (
            (n_row - 1 - k, row < n_row - 1 - k, row > 0, up_in, up_out, up_base, link.device(row=row + 1)),
            (k, row > k, row < n_row - 1, down_in, down_out, down_base, link.device(row=row - 1)),
        ):

            @pl.when(going & more)
            def _():
                link.landed(source.at[at], base_at + at)
                target[at] = (mine(at) + source[at].astype(F32)).astype(BF16)

            @pl.when(going & jnp.logical_not(more))
            def _():
                target[at] = mine(at).astype(BF16)

            link.send(target.at[at], source.at[at], base_at + at, device, going)
        yield
    own[...] = mine(row)

    for more, source, base_at in ((row > 0, up_in, up_base), (row < n_row - 1, down_in, down_base)):

        @pl.when(more)
        def _():
            link.landed(source.at[row], base_at + row)
            own[...] += source[row].astype(F32)


def spread(link, base, n_row, own, place, onward=None):
    row, col = link.row, link.col
    up, down, side = (device for device, _ in link.plane_neighbours(n_row))
    here = place(row, col)
    link.send(own, here, base + row, up, row < n_row - 1)
    link.send(own, here, base + row, down, row > 0)
    link.send(own, here, base + n_row + row, side)
    yield
    for k in range(1, n_row):
        for at, there, device, further in (
            (row - k, row >= k, up, row < n_row - 1),
            (row + k, row + k < n_row, down, row > 0),
        ):
            block = place(at, col)
            pl.when(there)(functools.partial(link.landed, block, base + at))
            if k < n_row - 1:
                link.send(block, block, base + at, device, there & further)
            link.send(block, block, base + n_row + at, side, there)
            if onward is not None:
                onward(at, col, there)
        yield
    for k in range(n_row):
        for at, there in [(row - k, row >= k), (row + k, row + k < n_row)][: 2 if k else 1]:
            block = place(at, 1 - col)
            pl.when(there)(functools.partial(link.landed, block, base + n_row + at))
            if onward is not None:
                onward(at, 1 - col, there)
        if k % 2:
            yield


def spread_matrix(link, base, n_row, shard, whole, by_row, local_sems):
    row, col, at_x, at_core = link.row, link.col, link.x, link.core
    columns = shard.shape[-1]

    def block(at_row, at_col, x, core):
        lead, side = (at_row, at_col) if by_row else (at_col, at_row)
        return whole.at[lead, x, core, :, pl.ds(pl.multiple_of(side * columns, 128), columns)]

    local = []
    for index, x in enumerate((at_x, 1 - at_x)):
        copy = pltpu.make_async_copy(
            shard.at[2 * x + at_core], block(row, col, x, at_core), local_sems.at[index]
        )
        copy.start()
        local.append(copy)
    x_base, core_base = base + 2 * n_row, base + 4 * n_row
    beside, sibling = link.device(dp=link.beside), link.device(dp=link.sibling)

    def to_x(at_row, at_col, when):
        ref = block(at_row, at_col, at_x, at_core)
        link.send(ref, ref, x_base + at_col * n_row + at_row, beside, when)

    yield from spread(link, base, n_row, shard.at[link.dp], lambda r, c: block(r, c, at_x, at_core), to_x)
    for copy in local:
        copy.wait()
    ref = whole.at[:, at_x, at_core]
    link.send(ref, ref, core_base, sibling)
    yield
    for k in range(2 * n_row):
        at_row, at_col = lax.rem(row + k // 2, n_row), 1 - col if k % 2 else col
        if k:
            link.landed(block(at_row, at_col, 1 - at_x, at_core), x_base + at_col * n_row + at_row)
        if k % 2:
            yield
    ref = whole.at[:, 1 - at_x, at_core]
    link.send(ref, ref, core_base + 1, sibling)
    yield
    link.landed(whole.at[:, at_x, 1 - at_core], core_base)
    link.landed(whole.at[:, 1 - at_x, 1 - at_core], core_base + 1)


N_MATRIX = 4 * 4 + 2


def front_kernel(n_row, ids, table, pos, *refs):
    shards, (start, low, square), wholes = refs[:4], refs[4:7], refs[7:11]
    held, staged, row_block_ref, pos_in, looked = refs[11:16]
    from_col, up_in, down_in, up_out, down_out, own, own_low = refs[16:23]
    send_sems, recv_sems, local_sems, table_sems, low_sems = refs[23:]
    limit, width = table.shape
    block = own.shape[0]
    piece = limit // table_sems.shape[0]
    loads = [
        pltpu.make_async_copy(table.at[pl.ds(at, piece)], held.at[pl.ds(at, piece)], table_sems.at[k])
        for k, at in enumerate(range(0, limit, piece))
    ]
    for load in loads:
        load.start()
    link = Link(send_sems, recv_sems)
    row_peers = [(link.row + k) % n_row for k in range(1, n_row)]
    link.greet(
        [(link.device(row=peer), None) for peer in row_peers]
        + [(link.device(col=1 - link.col), None)]
        + [(link.device(dp=link.beside), None), (link.device(dp=link.sibling), None)]
    )
    first = (link.col * n_row + link.row) * limit
    pos_base = 5 * n_row + 4 * N_MATRIX

    def look_up(col, at):
        token = (col * n_row + at) * block

        def step(k, carry):
            entry = ids[token + k] - first
            inside = (entry >= 0) & (entry < limit)
            row = held[pl.ds(jnp.clip(entry, 0, limit - 1), 1), :]
            row_block_ref[pl.ds(k, 1), :] = jnp.where(inside, row, 0.0)
            return carry

        lax.fori_loop(0, block, step, 0, unroll=8)
        looked[col, at] = row_block_ref[...].astype(BF16)

    def tokens():
        for peer in row_peers:
            rows = pos.at[pl.ds(pl.multiple_of(peer * block, 8), block)]
            link.send(rows, pos_in.at[link.row], pos_base + link.row, link.device(row=peer))
        pos_in[link.row] = pos[pl.ds(pl.multiple_of(link.row * block, 8), block), :]
        for load in loads:
            load.wait()
        yield from scatter_sum(
            link, 0, n_row, looked, from_col, (up_in, down_in), (up_out, down_out), own, look_up
        )
        for peer in row_peers:
            link.landed(pos_in.at[peer], pos_base + peer)
        pos_own = jnp.concatenate([pos_in[k] for k in range(n_row)], 1)
        own_low[...] = (own[...] + pos_own).astype(BF16)
        start[link.col, link.row] = own_low[...]
        yield from spread(link, 3 * n_row, n_row, own_low, lambda r, c: start.at[c, r])

    def shorten():
        yield
        square[...] = jnp.zeros_like(square)
        count = low.shape[0] // BLOCK
        stores = []
        for k in range(count):
            rows = min(BLOCK, limit - k * BLOCK)
            if k > 1:
                stores[k - 2].wait()
            part = held[k * BLOCK : k * BLOCK + rows, :]
            square[...] += jnp.sum(part * part, 0, keepdims=True)
            if rows < BLOCK:
                staged[k % 2, rows:] = jnp.zeros((BLOCK - rows, width), BF16)
            staged[k % 2, :rows] = part.astype(BF16)
            stores.append(
                pltpu.make_async_copy(staged.at[k % 2], low.at[pl.ds(k * BLOCK, BLOCK)], low_sems.at[k % 2])
            )
            stores[k].start()
            yield
        for store in stores[-2:]:
            store.wait()

    matrices = [
        spread_matrix(
            link, 5 * n_row + index * N_MATRIX, n_row, shards[index], wholes[index], index < 3, local_sems.at[index]
        )
        for index in range(4)
    ]
    run_together(*matrices, tokens(), shorten())
    link.finish()


def front(ids, table, pos, shards, n_row):
    limit, width = table.shape
    block = ids.shape[0] // (2 * n_row)
    low = (pl.cdiv(limit, BLOCK) * BLOCK, width)
    wholes = [(n_row, 2, 2) + shard.shape[1:2] + (2 * shard.shape[2],) for shard in shards[:3]]
    wholes.append((2, 2, 2) + shards[3].shape[1:2] + (n_row * shards[3].shape[2],))
    rows = pltpu.VMEM((n_row, block, width), BF16)
    vmem, hbm = pl.BlockSpec(memory_space=pltpu.VMEM), pl.BlockSpec(memory_space=pl.ANY)
    shape = jax.ShapeDtypeStruct
    return pl.pallas_call(
        functools.partial(front_kernel, n_row),
        out_shape=[shape((2, n_row, block, width), BF16), shape(low, BF16), shape((1, width), F32)]
        + [shape(whole, BF16) for whole in wholes],
        in_specs=[pl.BlockSpec(memory_space=pltpu.SMEM), hbm, vmem] + [hbm] * 4,
        out_specs=[vmem, hbm, vmem] + [hbm] * 4,
        scratch_shapes=[pltpu.VMEM(table.shape, F32), pltpu.VMEM((2, BLOCK, width), BF16)]
        + [pltpu.VMEM((block, width), F32), pltpu.VMEM((n_row, block) + pos.shape[1:], F32)]
        + [pltpu.VMEM((2, n_row, block, width), BF16)]
        + [rows] * 5
        + [pltpu.VMEM((block, width), F32), pltpu.VMEM((block, width), BF16)]
        + [
            pltpu.SemaphoreType.DMA((220,)),
            pltpu.SemaphoreType.DMA((6 * n_row + 4 * N_MATRIX,)),
            pltpu.SemaphoreType.DMA((4, 2)),
            pltpu.SemaphoreType.DMA((6,)),
            pltpu.SemaphoreType.DMA((2,)),
        ],
        compiler_params=pltpu.CompilerParams(
            collective_id=1, has_side_effects=True, vmem_limit_bytes=56 * 1024 * 1024
        ),
    )(ids, table, pos, *shards)


def total_kernel(n_row, part, total, *refs):
    from_col, up_in, down_in, up_out, down_out, own, own_low, send_sems, recv_sems = refs
    link = Link(send_sems, recv_sems)
    link.greet(link.plane_neighbours(n_row))

    def steps():
        yield from scatter_sum(link, 0, n_row, part, from_col, (up_in, down_in), (up_out, down_out), own)
        own_low[...] = own[...].astype(BF16)
        total[link.col, link.row] = own_low[...]
        yield from spread(link, 3 * n_row, n_row, own_low, lambda r, c: total.at[c, r])

    run_together(steps())
    link.finish()


def plane_total(part, collective_id):
    n_row, block, width = part.shape[1:]
    rows = pltpu.VMEM((n_row, block, width), BF16)
    vmem = pl.BlockSpec(memory_space=pltpu.VMEM)
    return pl.pallas_call(
        functools.partial(total_kernel, n_row),
        out_shape=jax.ShapeDtypeStruct(part.shape, BF16),
        in_specs=[vmem],
        out_specs=vmem,
        scratch_shapes=[rows] * 5
        + [pltpu.VMEM((block, width), F32), pltpu.VMEM((block, width), BF16)]
        + [pltpu.SemaphoreType.DMA((40,)), pltpu.SemaphoreType.DMA((5 * n_row,))],
        compiler_params=pltpu.CompilerParams(
            collective_id=collective_id, has_side_effects=True, vmem_limit_bytes=40 * 1024 * 1024
        ),
    )(part)


FORWARD_QUERIES = 512
BACK_QUERIES = 256


def causal(scores):
    keys = lax.broadcasted_iota(jnp.int32, scores.shape, 0)
    queries = lax.broadcasted_iota(jnp.int32, scores.shape, 1)
    return jnp.where(keys <= queries, scores, -1e30)


def lanes_of(head):
    return slice(head * HEAD, (head + 1) * HEAD)


def attend_kernel(q_ref, k_ref, v_ref, o_ref, log_ref):
    size = FORWARD_QUERIES
    values = [v_ref[:, lanes_of(head)].T for head in range(2)]
    steps = [(head, at) for head in range(2) for at in range(0, q_ref.shape[0], size)]

    def scores_of(head, at):
        queries = q_ref[at : at + size, lanes_of(head)] * HEAD ** (-0.5)
        return mm_nt(k_ref[: at + size, lanes_of(head)], queries)

    later = scores_of(*steps[0])
    for k, (head, at) in enumerate(steps):
        scores = later
        if k + 1 < len(steps):
            later = scores_of(*steps[k + 1])
        here = slice(at, at + size)
        edge = causal(scores[at:])
        top = jnp.max(edge, 0, keepdims=True)
        if at:
            top = jnp.maximum(top, jnp.max(scores[:at], 0, keepdims=True))
        exps = jnp.exp(edge - top)
        count = jnp.sum(exps, 0, keepdims=True)
        exps = exps.astype(BF16)
        if at:
            before = jnp.exp(scores[:at] - top)
            count = count + jnp.sum(before, 0, keepdims=True)
            exps = jnp.concatenate([before.astype(BF16), exps], 0)
        mixed = mm(values[head][:, : at + size], exps)
        o_ref[here, lanes_of(head)] = (mixed / count).T.astype(BF16)
        log_ref[0, head : head + 1, here] = top + jnp.log(count)


def attend(packed):
    length, width = packed.shape[0], packed.shape[1] // 3
    pairs = HEADS // 2
    lanes = 2 * HEAD
    column = lambda first: pl.BlockSpec((length, lanes), lambda i: (0, first + i))
    return pl.pallas_call(
        attend_kernel,
        grid=(pairs,),
        out_shape=[
            jax.ShapeDtypeStruct((length, width), BF16),
            jax.ShapeDtypeStruct((pairs, 2, length), F32),
        ],
        in_specs=[column(0), column(pairs), column(2 * pairs)],
        out_specs=[column(0), pl.BlockSpec((1, 2, length), lambda i: (i, 0, 0))],
        cost_estimate=cost(20 * length * length * width, 8 * length * width),
        compiler_params=pltpu.CompilerParams(vmem_limit_bytes=40 * 1024 * 1024),
    )(packed, packed, packed)


def attend_back_kernel(q_ref, k_ref, v_ref, g_ref, log_ref, out_ref, key_sum, value_sum):
    length, size = q_ref.shape[0], BACK_QUERIES
    keys_turned = [k_ref[:, lanes_of(head)].T for head in range(2)]
    steps = [(head, at) for head in range(2) for at in range(0, length, size)]

    def products_of(head, at):
        queries = q_ref[at : at + size, lanes_of(head)] * HEAD ** (-0.5)
        grads = g_ref[at : at + size, lanes_of(head)]
        scores = mm_nt(k_ref[: at + size, lanes_of(head)], queries)
        return scores, mm_nt(v_ref[: at + size, lanes_of(head)], grads), queries, grads

    later = products_of(*steps[0])
    for k, (head, at) in enumerate(steps):
        scores, prob_grad, queries, grads = later
        if k + 1 < len(steps):
            later = products_of(*steps[k + 1])
        here = slice(at, at + size)
        log_norm = log_ref[0, head : head + 1, here]
        probs = jnp.exp(causal(scores[at:]) - log_norm)
        if at:
            probs = jnp.concatenate([jnp.exp(scores[:at] - log_norm), probs], 0)
        level = jnp.sum(probs * prob_grad, 0, keepdims=True)
        score_grad = (probs * (prob_grad - level)).astype(BF16)
        value_grad = mm(probs.astype(BF16), grads)
        key_grad = mm(score_grad, queries)
        query_grad = mm(keys_turned[head][:, : at + size], score_grad) * HEAD ** (-0.5)
        out_ref[0, here, lanes_of(head)] = query_grad.T.astype(BF16)
        if at:
            value_sum[head, :at] += value_grad[:at]
            key_sum[head, :at] += key_grad[:at]
        value_sum[head, here] = value_grad[at:]
        key_sum[head, here] = key_grad[at:]
        if at + size == length:
            out_ref[1, :, lanes_of(head)] = key_sum[head].astype(BF16)
            out_ref[2, :, lanes_of(head)] = value_sum[head].astype(BF16)


def attend_back(packed, mixed_grad, log_norm):
    length, width = mixed_grad.shape
    pairs = HEADS // 2
    lanes = 2 * HEAD
    column = lambda first: pl.BlockSpec((length, lanes), lambda i: (0, first + i))
    return pl.pallas_call(
        attend_back_kernel,
        grid=(pairs,),
        out_shape=jax.ShapeDtypeStruct((3, length, width), BF16),
        in_specs=[column(0), column(pairs), column(2 * pairs), column(0)]
        + [pl.BlockSpec((1, 2, length), lambda i: (i, 0, 0))],
        out_specs=pl.BlockSpec((3, length, lanes), lambda i: (0, 0, i)),
        scratch_shapes=[pltpu.VMEM((2, length, HEAD), F32)] * 2,
        cost_estimate=cost(30 * length * length * width, 16 * length * width),
        compiler_params=pltpu.CompilerParams(vmem_limit_bytes=48 * 1024 * 1024),
    )(packed, packed, packed, mixed_grad, log_norm)


def meet(link, *exchanges):
    for base, value, slots, me, peers in exchanges:
        slots[me] = value[...]
        for _, device in peers:
            link.send(value, slots.at[me], base + me, device)
    for base, _, slots, _, peers in exchanges:
        for index, _ in peers:
            link.landed(slots.at[index], base + index)


def added(slots):
    total = slots[0]
    for k in range(1, slots.shape[0]):
        total = total + slots[k]
    return total


def sum_small_kernel(n_row, value, total, middle, slots, dp_slots, send_sems, recv_sems):
    link = Link(send_sems, recv_sems)
    me, peers = link.plane_peers(n_row)
    examples = link.example_peers()
    link.greet([(device, None) for _, device in peers + examples])
    meet(link, (0, value, slots, me, peers))
    middle[...] = added(slots)
    meet(link, (2 * n_row, middle, dp_slots, link.dp, examples))
    total[...] = added(dp_slots)
    link.finish()


def sum_small(value, n_row, collective_id):
    vmem = pl.BlockSpec(memory_space=pltpu.VMEM)
    return pl.pallas_call(
        functools.partial(sum_small_kernel, n_row),
        out_shape=jax.ShapeDtypeStruct(value.shape, F32),
        in_specs=[vmem],
        out_specs=vmem,
        scratch_shapes=[pltpu.VMEM(value.shape, F32), pltpu.VMEM((2 * n_row,) + value.shape, F32)]
        + [pltpu.VMEM((4,) + value.shape, F32)]
        + [pltpu.SemaphoreType.DMA((2 * n_row + 2,)), pltpu.SemaphoreType.DMA((2 * n_row + 4,))],
        compiler_params=pltpu.CompilerParams(collective_id=collective_id, has_side_effects=True),
    )(value)


def log_total_kernel(n_row, tops, sums, picked, log_ref, pick_ref, value, slots, send_sems, recv_sems):
    link = Link(send_sems, recv_sems)
    me, peers = link.plane_peers(n_row)
    link.greet([(device, None) for _, device in peers])
    top = jnp.max(tops[...], 0)
    value[0] = top
    value[1] = jnp.sum(sums[...] * jnp.exp(tops[...] - top[None]), 0)
    value[2] = picked[...]
    meet(link, (0, value, slots, me, peers))
    everyone = range(2 * n_row)
    top, total, pick = slots[0, 0], jnp.zeros_like(top), jnp.zeros_like(top)
    for k in everyone:
        top = jnp.maximum(top, slots[k, 0])
    for k in everyone:
        total = total + slots[k, 1] * jnp.exp(slots[k, 0] - top)
        pick = pick + slots[k, 2]
    log_ref[...] = top + jnp.log(total)
    pick_ref[...] = pick
    link.finish()


def log_total(tops, sums, picked, n_row, collective_id):
    length = picked.shape[-1]
    tile = (length // 128, 128)
    tops, sums, picked = (item.reshape(item.shape[:-2] + tile) for item in (tops, sums, picked))
    vmem = pl.BlockSpec(memory_space=pltpu.VMEM)
    log_norm, picked = pl.pallas_call(
        functools.partial(log_total_kernel, n_row),
        out_shape=[jax.ShapeDtypeStruct(tile, F32)] * 2,
        in_specs=[vmem] * 3,
        out_specs=[vmem] * 2,
        scratch_shapes=[pltpu.VMEM((3,) + tile, F32), pltpu.VMEM((2 * n_row, 3) + tile, F32)]
        + [pltpu.SemaphoreType.DMA((2 * n_row,))] * 2,
        compiler_params=pltpu.CompilerParams(collective_id=collective_id, has_side_effects=True),
    )(tops, sums, picked)
    return log_norm.reshape(1, length), picked.reshape(1, length)


BLOCK = 1056
MEGA = 1024 * 1024


def cost(flops, bytes_accessed):
    return pl.CostEstimate(flops=flops, bytes_accessed=bytes_accessed, transcendentals=0)


def blocks_of(limit):
    return pl.cdiv(limit, BLOCK)


def entries(shape, first=0, skip=0):
    return lax.broadcasted_iota(jnp.int32, shape, 0) + ((pl.program_id(0) + first) * BLOCK + skip)


PARTS = 3
PART = BLOCK // PARTS


def parts_of():
    return [slice(at, at + PART) for at in range(0, BLOCK, PART)]


def head_kernel(limit, low_ref, z_ref, target_ref, exp_ref, top_ref, sum_ref, pick_ref):
    @pl.when(pl.program_id(0) == 0)
    def _():
        pick_ref[...] = jnp.zeros_like(pick_ref)

    picked = jnp.zeros(pick_ref.shape, F32)
    steps = parts_of()
    later = mm_nt(low_ref[steps[0]], z_ref[...])
    for k, rows in enumerate(steps):
        logits = later
        if k + 1 < PARTS:
            later = mm_nt(low_ref[steps[k + 1]], z_ref[...])
        off = jnp.where(entries((PART, 1), 0, rows.start) < limit, 0.0, -1e30)
        logits = logits + off
        top = jnp.max(logits, 0, keepdims=True)
        hit = lax.broadcasted_iota(jnp.int32, logits.shape, 0) == target_ref[...] - (pl.program_id(0) * BLOCK + rows.start)
        picked = picked + jnp.sum(jnp.where(hit, logits, 0.0), 0, keepdims=True)
        exps = jnp.exp(logits - top)
        exp_ref[rows] = exps.astype(BF16)
        top_ref[k] = top
        sum_ref[k] = jnp.sum(exps, 0, keepdims=True)
    pick_ref[...] += picked


def whole_block(shape):
    return pl.BlockSpec(shape, lambda i, *_: (0,) * len(shape), pipeline_mode=pl.Buffered(1))


def row_block(width):
    return pl.BlockSpec((BLOCK, width), lambda i, *_: (i, 0))


def line_block(width, lines=1):
    return pl.BlockSpec((lines, 1, width), lambda i, *_: (i, 0, 0))


def head(low, limit, z, target):
    length, width = z.shape
    count = blocks_of(limit)
    shape = jax.ShapeDtypeStruct
    line = shape((count * PARTS, 1, length), F32)
    return pl.pallas_call(
        functools.partial(head_kernel, limit),
        grid=(count,),
        out_shape=[shape((count * BLOCK, length), BF16), line, line, shape((1, length), F32)],
        in_specs=[row_block(width), whole_block((length, width)), whole_block((1, length))],
        out_specs=[row_block(length), line_block(length, PARTS), line_block(length, PARTS), whole_block((1, length))],
        cost_estimate=cost(2 * limit * width * length, 2 * limit * width + 2 * limit * length),
        compiler_params=pltpu.CompilerParams(vmem_limit_bytes=48 * MEGA),
    )(low, z, target)


def slope_of(exps, rows, target_ref, first=0):
    entry = lax.broadcasted_iota(jnp.int32, exps.shape, 0)
    target = target_ref[...] - ((pl.program_id(0) + first) * BLOCK + rows.start)
    return jnp.where(entry == target, exps - 1.0, exps).astype(BF16)


def head_back_kernel(exp_ref, top_ref, log_ref, target_ref, low_ref, z_ref, grad_ref, table_ref, slope, total):
    at = pl.program_id(0)
    for k, rows in enumerate(parts_of()):
        scale = jnp.exp(top_ref[k] - log_ref[...])
        slope[rows] = slope_of(exp_ref[rows].astype(F32) * scale, rows, target_ref)
        table_ref[rows] = mm(slope[rows], z_ref[...]).astype(BF16)
    part = mm_tn(low_ref[...], slope[...])

    @pl.when(at == 0)
    def _():
        total[...] = part

    @pl.when(at > 0)
    def _():
        total[...] += part

    @pl.when(at == pl.num_programs(0) - 1)
    def _():
        grad_ref[...] = total[...].T.astype(BF16)


def head_back(exps, tops, log_norm, target, low, z):
    length, width = z.shape
    return pl.pallas_call(
        head_back_kernel,
        grid=(low.shape[0] // BLOCK,),
        out_shape=[jax.ShapeDtypeStruct((length, width), BF16), jax.ShapeDtypeStruct(low.shape, BF16)],
        in_specs=[row_block(length), line_block(length, PARTS), whole_block((1, length)), whole_block((1, length))]
        + [row_block(width), whole_block((length, width))],
        out_specs=[whole_block((length, width)), row_block(width)],
        scratch_shapes=[pltpu.VMEM((BLOCK, length), BF16), pltpu.VMEM((width, length), F32)],
        cost_estimate=cost(4 * low.size * length, 4 * low.size + 2 * exps.size),
        compiler_params=pltpu.CompilerParams(vmem_limit_bytes=48 * MEGA),
    )(exps, tops, log_norm, target, low, z)


def token_lists(ids, start, limit):
    length = ids.shape[0]
    token = jnp.arange(length, dtype=jnp.int32)
    one, two = ids[:, None], ids[None, :]
    ahead = (two < one) | ((two == one) & (token[None, :] < token[:, None]))
    place = jnp.sum(ahead.astype(jnp.int32), 1)
    at = place[:, None] == token[None, :]
    order = jnp.sum(jnp.where(at, token[:, None], 0), 0)
    ordered = jnp.sum(jnp.where(at, ids[:, None], 0), 0)
    edges = start + jnp.minimum(jnp.arange(blocks_of(limit) + 1) * BLOCK, limit)
    bounds = jnp.sum((ids[None, :] < edges[:, None]).astype(jnp.int32), 1)
    return ordered - start, order, bounds


def add_rows(total, ids_ref, order_ref, bounds_ref, grad_ref, first=0):
    at = pl.program_id(0) + first

    def step(k, carry):
        row, token = ids_ref[k] - at * BLOCK, order_ref[k]
        total[pl.ds(row, 1), :] += grad_ref[pl.ds(token, 1), :]
        return carry

    lax.fori_loop(bounds_ref[at], bounds_ref[at + 1], step, 0)


def own_rows_kernel(ids_ref, order_ref, bounds_ref, table_ref, grad_ref, out_ref, square_ref, total):
    total[...] = table_ref[...].astype(F32)
    add_rows(total, ids_ref, order_ref, bounds_ref, grad_ref)
    full = total[...]
    out_ref[...] = full.astype(BF16)

    @pl.when(pl.program_id(0) == 0)
    def _():
        square_ref[...] = jnp.zeros_like(square_ref)

    square_ref[...] += jnp.sum(full * full, 0, keepdims=True)


def add_own_rows(table, lists, grad):
    width = table.shape[1]
    return pl.pallas_call(
        own_rows_kernel,
        grid_spec=pltpu.PrefetchScalarGridSpec(
            num_scalar_prefetch=3,
            grid=(table.shape[0] // BLOCK,),
            in_specs=[row_block(width), whole_block(grad.shape)],
            out_specs=[row_block(width), whole_block((1, width))],
            scratch_shapes=[pltpu.VMEM((BLOCK, width), F32)],
        ),
        out_shape=[jax.ShapeDtypeStruct(table.shape, BF16), jax.ShapeDtypeStruct((1, width), F32)],
        cost_estimate=cost(0, 4 * table.size),
        compiler_params=pltpu.CompilerParams(vmem_limit_bytes=56 * MEGA),
    )(*lists, table, grad)


def table_sum_kernel(first, ids_ref, order_ref, bounds_ref, share_ref, *refs):
    low_ref, z_ref, log_ref, target_ref, own_ref, grad_ref, out_ref, total = refs
    steps = parts_of()
    later = mm_nt(low_ref[steps[0]], z_ref[...])
    for k, rows in enumerate(steps):
        logits = later
        if k + 1 < PARTS:
            later = mm_nt(low_ref[steps[k + 1]], z_ref[...])
        slope = slope_of(jnp.exp(logits - log_ref[...]), rows, target_ref, first)
        total[rows] = mm(slope, z_ref[...])
    add_rows(total, ids_ref, order_ref, bounds_ref, grad_ref, first)
    out_ref[...] = (share_ref[0] * own_ref[...].astype(F32) + share_ref[1] * total[...]).astype(BF16)


def table_sum(own, low, z, log_norm, target, lists, grad, shares, first, count):
    length, width = z.shape
    rows = lambda i, *_: (i + first, 0)
    return pl.pallas_call(
        functools.partial(table_sum_kernel, first),
        grid_spec=pltpu.PrefetchScalarGridSpec(
            num_scalar_prefetch=4,
            grid=(count,),
            in_specs=[pl.BlockSpec((BLOCK, width), rows), whole_block((length, width))]
            + [whole_block((1, length)), whole_block((1, length))]
            + [pl.BlockSpec((BLOCK, width), rows), whole_block(grad.shape)],
            out_specs=row_block(width),
            scratch_shapes=[pltpu.VMEM((BLOCK, width), F32)],
        ),
        out_shape=jax.ShapeDtypeStruct((count * BLOCK, width), BF16),
        cost_estimate=cost(4 * count * BLOCK * width * length, 6 * count * BLOCK * width),
        compiler_params=pltpu.CompilerParams(vmem_limit_bytes=48 * MEGA),
    )(*lists, shares, low, z, log_norm, target, own, grad)


def turned(line, height):
    return jnp.broadcast_to(line, (height, line.shape[1])).T


def gradient_kernel(limit, count, divisor, first, *refs):
    sums, (noise_ref, old_ref), outs = refs[:count], refs[count : count + 2], refs[-5:]
    grad_ref, rows_ref, cols_ref, scaled_ref, level_ref = outs
    total = sums[0][...].astype(F32)
    for item in sums[1:]:
        total = total + item[...].astype(F32)
    grad = (total + NOISE * CLIP * noise_ref[...]) * (1.0 / divisor)
    inside = entries((BLOCK, 1), first) < limit
    grad_ref[...] = grad
    squares = jnp.where(inside, grad * grad, 0.0)
    mean = jnp.sum(squares, 1, keepdims=True) / grad.shape[1] + 1e-30
    old = turned(old_ref[0], 128)[:, :1]
    rows = DECAY * old + (1.0 - DECAY) * mean
    rows_ref[0] = line_of(rows)

    @pl.when(pl.program_id(0) == 0)
    def _():
        cols_ref[...] = jnp.zeros_like(cols_ref)
        scaled_ref[...] = jnp.zeros_like(scaled_ref)
        level_ref[...] = jnp.zeros_like(level_ref)

    cols_ref[...] += jnp.sum(squares, 0, keepdims=True)
    scaled_ref[...] += jnp.sum(squares * (1.0 / rows), 0, keepdims=True)
    level_ref[...] += jnp.broadcast_to(jnp.sum(jnp.where(inside, rows, 0.0), 0, keepdims=True), level_ref.shape)


def table_gradient(sums, noise, old, divisor, first, count, into=None):
    limit, width = noise.shape
    shape = jax.ShapeDtypeStruct
    rows = pl.BlockSpec((BLOCK, width), lambda i: (i + first, 0))
    extra = [] if into is None else [into]
    return pl.pallas_call(
        functools.partial(gradient_kernel, limit, len(sums), divisor, first),
        grid=(count,),
        out_shape=[shape((limit, width), F32), shape((count, 1, BLOCK), F32)]
        + [shape((1, width), F32)] * 2
        + [shape((1, 128), F32)],
        in_specs=[row_block(width)] * len(sums)
        + [rows, pl.BlockSpec((1, 1, BLOCK), lambda i: (i + first, 0, 0))]
        + [pl.BlockSpec(memory_space=pl.ANY)] * len(extra),
        out_specs=[rows, line_block(BLOCK), whole_block((1, width)), whole_block((1, width))]
        + [whole_block((1, 128))],
        input_output_aliases={len(sums) + 2: 0} if extra else {},
        cost_estimate=cost(0, (8 + 2 * len(sums)) * count * BLOCK * width),
        compiler_params=pltpu.CompilerParams(vmem_limit_bytes=48 * MEGA),
    )(*sums, noise, old, *extra)


SIDE = 256


def line_of(column):
    return jnp.broadcast_to(column, (column.shape[0], 128)).T[:1]


BY_ROW = (False, True, True, True, False)


def put_line(ref, at, line):
    size = line.shape[1]
    for k in range(0, size, 128):
        ref[at : at + 1, : min(128, size - k)] = line[:, k : min(k + 128, size)]
        at += 1
    return at


def get_line(value, at, size):
    rows = [value[at + k : at + k + 1, : min(128, size - 128 * k)] for k in range(pl.cdiv(size, 128))]
    return rows[0] if len(rows) == 1 else jnp.concatenate(rows, 1)


def line_places(shapes, rows_first):
    at, places = 0, []
    for (rows, cols), along in zip(shapes, BY_ROW):
        places.append(at)
        at += pl.cdiv(rows if along == rows_first else cols, 128)
    return places, -at // 8 * -8


def join_kernel(one_ref, two_ref, after_ref, out_ref):
    out_ref[...] = (one_ref[...].astype(F32) + two_ref[...].astype(F32)).astype(BF16)


def join(one, two, after):
    return pl.pallas_call(
        join_kernel,
        out_shape=jax.ShapeDtypeStruct(one.shape, BF16),
        grid=(1,),
        in_specs=[whole_block(one.shape), whole_block(two.shape), pl.BlockSpec(memory_space=pl.ANY)],
        out_specs=whole_block(one.shape),
        cost_estimate=cost(0, 6 * one.size),
    )(one, two, after)


def small_gradients_kernel(divisor, *refs):
    packed, small, small_second, small_noise = refs[:4]
    weights, noises, grads = (refs[4 + 5 * k : 9 + 5 * k] for k in range(3))
    small_outs, (to_col, to_row, square_ref) = refs[19:22], refs[22:]
    width = small.shape[1]
    scale = 1.0 / divisor
    side = weights[1].shape[0]
    cuts = (0, weights[1].shape[1], weights[1].shape[1] + weights[2].shape[1])
    for index in (1, 2, 3):
        at, end, lane_to = cuts[index - 1], cuts[index - 1] + weights[index].shape[1], 0
        while at < end:
            piece, lane = at // width, at % width
            size = min(width - lane, end - at)
            part = packed[piece * side : (piece + 1) * side, lane : lane + size].astype(F32)
            lanes = slice(lane_to, lane_to + size)
            grads[index][:, lanes] = (part + NOISE * CLIP * noises[index][:, lanes]) * scale
            at, lane_to = at + size, lane_to + size
    first = side * ((cuts[2] + weights[3].shape[1]) // width)
    down = weights[4].shape[0]
    grads[4][...] = (packed[first : first + down, :].astype(F32) + NOISE * CLIP * noises[4][...]) * scale
    first += down
    tall, wide = weights[0].shape[0] // 4, weights[0].shape[1]
    for k in range(4):
        lane, start = SIDE * (k % 3), first + tall * (k // 3)
        part = packed[start : start + tall, lane : lane + wide].astype(F32)
        lines = slice(k * tall, (k + 1) * tall)
        grads[0][lines] = (part + NOISE * CLIP * noises[0][lines]) * scale
    first += 2 * tall

    to_col[...] = jnp.zeros_like(to_col)
    to_row[...] = jnp.zeros_like(to_row)
    shapes = [item.shape for item in weights]
    col_places, row_places = line_places(shapes, True)[0], line_places(shapes, False)[0]
    lane = lax.broadcasted_iota(jnp.int32, (1, 128), 1)
    weight_sq = jnp.zeros((1, 128), F32)
    for index, along in enumerate(BY_ROW):
        squares = grads[index][...] * grads[index][...]
        row_sum = line_of(jnp.sum(squares, 1, keepdims=True))
        col_sum = jnp.sum(squares, 0, keepdims=True)
        put_line(to_col, col_places[index], row_sum if along else col_sum)
        put_line(to_row, row_places[index], col_sum if along else row_sum)
        total = jnp.sum(jnp.sum(weights[index][...] * weights[index][...], 0, keepdims=True), 1, keepdims=True)
        weight_sq = weight_sq + jnp.where(lane == index, total, 0.0)
    square_ref[...] = weight_sq

    count = small.shape[0]
    small_grad = (packed[first : first + 16, :].astype(F32)[:count] + NOISE * CLIP * small_noise[...]) * scale
    second_new = DECAY * small_second[...] + (1.0 - DECAY) * (small_grad * small_grad + 1e-30)
    update = small_grad * lax.rsqrt(second_new)
    mean = lambda item: jnp.sum(jnp.sum(item * item, 0, keepdims=True), 1, keepdims=True) / (count * width)
    size = RATE * jnp.maximum(1e-3, jnp.sqrt(mean(small[...])))
    size = size / jnp.maximum(1.0, jnp.sqrt(mean(update)))
    small_outs[0][...] = small_grad
    small_outs[1][...] = second_new
    small_outs[2][...] = small[...] - size * update


def small_gradients(packed, small, small_second, small_noise, weights, noises, divisor):
    width = small.shape[1]
    matrix_shapes = [item.shape for item in weights]
    line_rows = [line_places(matrix_shapes, first)[1] for first in (True, False)]
    shape = lambda dims: jax.ShapeDtypeStruct(dims, F32)
    operands = [packed, small, small_second, small_noise, *weights, *noises]
    shapes = matrix_shapes + [small.shape] * 3 + [(line_rows[0], 128), (line_rows[1], 128), (1, 128)]
    out = pl.pallas_call(
        functools.partial(small_gradients_kernel, divisor),
        grid=(1,),
        out_shape=[shape(dims) for dims in shapes],
        in_specs=[whole_block(item.shape) for item in operands],
        out_specs=[whole_block(dims) for dims in shapes],
        compiler_params=pltpu.CompilerParams(vmem_limit_bytes=48 * MEGA),
        cost_estimate=cost(0, 16 * MEGA),
    )(*operands)
    return out[:5], out[5:8], out[8:]


def statistics_kernel(n_row, vocab, *refs):
    table_over, over_cols, over_rows, old_lines = refs[:4]
    grads, (lines_ref, factor_ref), held = refs[4:9], refs[9:11], refs[11:16]
    to_level, both_slots, col_slots, row_slots, level_slots, send_sems, recv_sems, local_sems = refs[16:]
    n_col, width = 2, factor_ref.shape[1]
    everyone = n_row * n_col
    copies = [pltpu.make_async_copy(grads[k], held[k], local_sems.at[k]) for k in range(5)]
    for copy in copies:
        copy.start()
    link = Link(send_sems, recv_sems)
    me, peers = link.plane_peers(n_row)
    link.greet([(device, None) for _, device in peers])
    row_peers = [((link.row + k) % n_row, link.device(row=(link.row + k) % n_row)) for k in range(1, n_row)]
    meet(
        link,
        (0, table_over, both_slots, me, peers),
        (everyone, over_cols, col_slots, link.col, [(1 - link.col, link.device(col=1 - link.col))]),
        (everyone + n_col, over_rows, row_slots, link.row, row_peers),
    )
    both, over_col, over_row = added(both_slots), added(col_slots), added(row_slots)
    for copy in copies:
        copy.wait()

    lane = lax.broadcasted_iota(jnp.int32, (1, 128), 1)
    whole = lambda line: jnp.sum(line, 1, keepdims=True)
    lines = width // 128
    cols_new = DECAY * old_lines[5:6, :width] + (1.0 - DECAY) * (get_line(both, 0, width) / vocab + 1e-30)
    weight_sums, table_level = both[2 * lines : 2 * lines + 1], both[2 * lines + 1 : 2 * lines + 2, :1]
    everywhere = jnp.where(lane == 5, whole(get_line(both, lines, width) / cols_new), 0.0)
    counts = jnp.full((1, 128), float(vocab * width), F32)
    for index in range(5):
        counts = jnp.where(lane == index, float(held[index].shape[0] * held[index].shape[1] * everyone), counts)
    factor_ref[...] = jnp.zeros_like(factor_ref)
    factor_ref[0:1] = cols_new
    factor_ref[1:2] = lax.rsqrt(cols_new)

    lines_ref[...] = jnp.zeros_like(lines_ref)
    shapes = [item.shape for item in held]
    col_places, row_places = line_places(shapes, True)[0], line_places(shapes, False)[0]
    levels = jnp.where(lane == 5, table_level / (vocab * everyone), 0.0)
    scaled_sums = jnp.zeros((1, 128), F32)
    for index, along in enumerate(BY_ROW):
        rows, cols = held[index].shape
        parts_rows, parts_cols = (n_row, n_col) if along else (n_col, n_row)
        by_col = get_line(over_col, col_places[index], rows if along else cols)
        by_line = get_line(over_row, row_places[index], cols if along else rows)
        row_mean = (by_col if along else by_line) / (cols * parts_cols) + 1e-30
        col_mean = (by_line if along else by_col) / (rows * parts_rows) + 1e-30
        rows_line = DECAY * old_lines[index : index + 1, :rows] + (1.0 - DECAY) * row_mean
        cols_line = DECAY * old_lines[8 + index : 9 + index, :cols] + (1.0 - DECAY) * col_mean
        lines_ref[index : index + 1, :rows] = rows_line
        lines_ref[8 + index : 9 + index, :cols] = cols_line
        level = whole(rows_line) / (rows * parts_rows * parts_cols)
        scaled = held[index][...] * held[index][...] * (1.0 / turned(rows_line, 128)[:, :1])
        scaled = whole(jnp.sum(scaled, 0, keepdims=True) / cols_line)
        levels = jnp.where(lane == index, level, levels)
        scaled_sums = jnp.where(lane == index, scaled, scaled_sums)
    to_level[...] = jnp.zeros_like(to_level)
    to_level[0:1] = levels
    to_level[1:2] = scaled_sums
    meet(link, (everyone + n_col + n_row, to_level, level_slots, me, peers))
    levels = added(level_slots)
    level, square_sum = levels[0:1], levels[1:2] + everywhere
    size = RATE * jnp.maximum(1e-3, jnp.sqrt(weight_sums / counts))
    size = size / jnp.maximum(1.0, jnp.sqrt(square_sum * level / counts))
    sizes = size * jnp.sqrt(level)
    factor_ref[2:3, :128] = sizes
    link.finish()


def statistics(table_over, over_cols, over_rows, old_lines, grads, width, n_row, vocab, collective_id):
    wide = old_lines.shape[1]
    everyone = 2 * n_row
    vmem, hbm = pl.BlockSpec(memory_space=pltpu.VMEM), pl.BlockSpec(memory_space=pl.ANY)
    return pl.pallas_call(
        functools.partial(statistics_kernel, n_row, vocab),
        out_shape=[jax.ShapeDtypeStruct((16, wide), F32), jax.ShapeDtypeStruct((8, width), F32)],
        in_specs=[vmem] * 4 + [hbm] * 5,
        out_specs=[vmem] * 2,
        scratch_shapes=[pltpu.VMEM(item.shape, F32) for item in grads]
        + [pltpu.VMEM((8, 128), F32), pltpu.VMEM((everyone,) + table_over.shape, F32)]
        + [pltpu.VMEM((2,) + over_cols.shape, F32), pltpu.VMEM((n_row,) + over_rows.shape, F32)]
        + [pltpu.VMEM((everyone, 8, 128), F32)]
        + [pltpu.SemaphoreType.DMA((3 * everyone,)), pltpu.SemaphoreType.DMA((2 * everyone + 2 + n_row,))]
        + [pltpu.SemaphoreType.DMA((5,))],
        compiler_params=pltpu.CompilerParams(
            collective_id=collective_id, has_side_effects=True, vmem_limit_bytes=32 * MEGA
        ),
    )(table_over, over_cols, over_rows, old_lines, *grads)


def update_kernel(table_ref, table_grad_ref, rows_ref, factor_ref, lines_ref, *refs):
    weights, grads, (table_new_ref, table_cols_ref) = refs[:5], refs[5:10], refs[10:12]
    rows_outs, cols_outs, news = refs[12:17], refs[17:22], refs[22:27]
    rows = turned(lax.rsqrt(rows_ref[0]), 128)[:, :1]
    table_new_ref[...] = table_ref[...] - table_grad_ref[...] * rows * (factor_ref[1:2] * factor_ref[2:3, 5:6])

    @pl.when(pl.program_id(0) == 0)
    def _():
        table_cols_ref[...] = factor_ref[0:1].reshape(table_cols_ref.shape)
        for index in range(5):
            count_rows, count_cols = weights[index].shape
            rows_line = lines_ref[index : index + 1, :count_rows]
            cols_line = lines_ref[8 + index : 9 + index, :count_cols]
            rows_outs[index][...] = rows_line.reshape(count_rows)
            cols_outs[index][...] = cols_line.reshape(count_cols)
            rows = turned(lax.rsqrt(rows_line), 128)[:, :1]
            factors = factor_ref[2:3, index : index + 1] * lax.rsqrt(cols_line)
            news[index][...] = weights[index][...] - grads[index][...] * rows * factors


def update(table, table_grad, table_rows, factors, lines, weights, grads):
    limit, width = table.shape
    shape = lambda dims: jax.ShapeDtypeStruct(dims, F32)
    small_shapes = [(width,)] + [item.shape[:1] for item in weights] + [item.shape[1:] for item in weights]
    small_shapes += [item.shape for item in weights]
    out = pl.pallas_call(
        update_kernel,
        grid=(blocks_of(limit),),
        out_shape=[shape(table.shape)] + [shape(dims) for dims in small_shapes],
        in_specs=[row_block(width), row_block(width), line_block(BLOCK), whole_block(factors.shape)]
        + [whole_block(lines.shape)]
        + [whole_block(item.shape) for item in weights] * 2,
        out_specs=[row_block(width)] + [whole_block(dims) for dims in small_shapes],
        compiler_params=pltpu.CompilerParams(vmem_limit_bytes=56 * MEGA),
        cost_estimate=cost(0, 3 * 4 * limit * width),
    )(table, table_grad, table_rows, factors, lines, *weights, *grads)
    return out[0], out[1], out[2:7], out[7:12], out[12:]


HIDDEN = 1024
CHUNK = 512


def normed_of(inputs):
    center = jnp.mean(inputs, -1, keepdims=True)
    var = jnp.mean(inputs * inputs, -1, keepdims=True) - center * center
    inv = lax.rsqrt(var + 1e-05)
    return (inputs - center) * inv, inv


def normed_back(upstream, normed, inv, gain):
    scaled = upstream * gain
    first = jnp.mean(scaled, -1, keepdims=True)
    second = jnp.mean(scaled * normed, -1, keepdims=True)
    return inv * (scaled - first - normed * second)


def columns_sum(item):
    return jnp.sum(item.astype(F32), 0, keepdims=True)


def chunks_of(length):
    return [slice(at, at + CHUNK) for at in range(0, length, CHUNK)]


GELU_SCALE = (2.0 / jnp.pi) ** 0.5


def gelu_parts(inputs):
    square = inputs * inputs
    turn = jnp.tanh(inputs * (GELU_SCALE + (GELU_SCALE * 0.044715) * square))
    half = 0.5 + 0.5 * turn
    inner = GELU_SCALE + (3.0 * GELU_SCALE * 0.044715) * square
    return inputs * half, half + 0.5 * inputs * (1.0 - turn * turn) * inner


def middle_kernel(start_ref, mixed_ref, attn_ref, up_ref, bias_ref, down_ref, small_ref, *outs):
    mid_ref, low_ref, out_ref, z_ref, total = outs
    at = pl.program_id(0)
    length = start_ref.shape[0]

    @pl.when(at == 0)
    def _():
        for rows in chunks_of(length):
            mid = start_ref[rows].astype(F32) + mm(mixed_ref[rows], attn_ref[...]) + small_ref[4:5]
            mid_ref[rows] = mid
            low_ref[rows] = (normed_of(mid)[0] * small_ref[5:6] + small_ref[6:7]).astype(BF16)
            total[rows] = mid + small_ref[11:12]

    for rows in chunks_of(length):
        hidden = gelu_parts(mm(low_ref[rows], up_ref[...]) + bias_ref[...])[0].astype(BF16)
        total[rows] += mm_nt(hidden, down_ref[...])

    @pl.when(at == pl.num_programs(0) - 1)
    def _():
        for rows in chunks_of(length):
            out = total[rows]
            out_ref[rows] = out
            z_ref[rows] = (normed_of(out)[0] * small_ref[12:13] + small_ref[13:14]).astype(BF16)


def middle_forward(start, mixed, attn, up, up_bias, down, small):
    length, width = start.shape
    shape = jax.ShapeDtypeStruct
    whole = lambda item: whole_block(item.shape)
    tokens = whole_block((length, width))
    return pl.pallas_call(
        middle_kernel,
        grid=(up.shape[1] // HIDDEN,),
        out_shape=[shape((length, width), kind) for kind in (F32, BF16, F32, BF16)],
        in_specs=[whole(start), whole(mixed), whole(attn), pl.BlockSpec((width, HIDDEN), lambda i: (0, i))]
        + [pl.BlockSpec((1, HIDDEN), lambda i: (0, i)), pl.BlockSpec((width, HIDDEN), lambda i: (0, i))]
        + [whole(small)],
        out_specs=[tokens] * 4,
        scratch_shapes=[pltpu.VMEM((length, width), F32)],
        cost_estimate=cost(4 * length * width * up.shape[1], 16 * length * width),
        compiler_params=pltpu.CompilerParams(vmem_limit_bytes=56 * MEGA),
    )(start, mixed, attn, up, up_bias, down, small)


def middle_back_kernel(*refs):
    grad_ref, out_ref, mid_ref, low_ref, attn_ref, up_ref, bias_ref, down_ref, small_ref = refs[:9]
    down_grad_ref, pre_ref, act_ref, pre_sum_ref, mid_grad_ref, branch_ref, mixed_ref, rows_ref, total = refs[9:]
    at = pl.program_id(0)
    length, width = grad_ref.shape

    @pl.when(at == 0)
    def _():
        rows_ref[...] = jnp.zeros_like(rows_ref)
        for rows in chunks_of(length):
            grad = grad_ref[rows].astype(F32)
            normed, inv = normed_of(out_ref[rows])
            back = normed_back(grad, normed, inv, small_ref[12:13])
            mid_grad_ref[rows] = back
            low = back.astype(BF16)
            down_grad_ref[rows] = low
            rows_ref[0:1] += columns_sum(grad * normed)
            rows_ref[1:2] += columns_sum(grad)
            rows_ref[2:3] += columns_sum(low)
        total[...] = jnp.zeros_like(total)

    pre_sum = jnp.zeros((1, pre_ref.shape[1]), F32)
    for rows in chunks_of(length):
        act, slope = gelu_parts(mm(low_ref[rows], up_ref[...]) + bias_ref[...])
        act_ref[rows] = act.astype(BF16)
        pre = (mm(down_grad_ref[rows], down_ref[...]) * slope).astype(BF16)
        pre_ref[rows] = pre
        pre_sum = pre_sum + columns_sum(pre)
        total[rows] += mm_nt(pre, up_ref[...])
    pre_sum_ref[...] = pre_sum

    @pl.when(at == pl.num_programs(0) - 1)
    def _():
        for rows in chunks_of(length):
            grad = total[rows]
            normed, inv = normed_of(mid_ref[rows])
            mid_grad = mid_grad_ref[rows] + normed_back(grad, normed, inv, small_ref[5:6])
            mid_grad_ref[rows] = mid_grad
            low = mid_grad.astype(BF16)
            branch_ref[rows] = low
            rows_ref[3:4] += columns_sum(grad * normed)
            rows_ref[4:5] += columns_sum(grad)
            rows_ref[5:6] += columns_sum(low)
            mixed_ref[rows] = mm_nt(low, attn_ref[...]).astype(BF16)


def middle_back(grad, out, mid, low, attn, up, up_bias, down, small):
    length, width = grad.shape
    hidden = up.shape[1]
    shape = jax.ShapeDtypeStruct
    whole = lambda item: whole_block(item.shape)
    tokens = whole_block((length, width))
    wide = pl.BlockSpec((length, HIDDEN), lambda i: (0, i))
    weight = pl.BlockSpec((width, HIDDEN), lambda i: (0, i))
    line = pl.BlockSpec((1, HIDDEN), lambda i: (0, i))
    return pl.pallas_call(
        middle_back_kernel,
        grid=(hidden // HIDDEN,),
        out_shape=[shape((length, width), BF16), shape((length, hidden), BF16), shape((length, hidden), BF16)]
        + [shape((1, hidden), F32), shape((length, width), F32), shape((length, width), BF16)]
        + [shape((length, width), BF16), shape((8, width), F32)],
        in_specs=[tokens] * 4 + [whole(attn), weight, line, weight, whole(small)],
        out_specs=[tokens, wide, wide, line, tokens, tokens, tokens, whole_block((8, width))],
        scratch_shapes=[pltpu.VMEM((length, width), F32)],
        cost_estimate=cost(6 * length * width * hidden, 40 * length * width),
        compiler_params=pltpu.CompilerParams(vmem_limit_bytes=58 * MEGA),
    )(grad, out, mid, low, attn, up, up_bias, down, small)


def start_back_kernel(packed_ref, weight_ref, mid_grad_ref, start_ref, small_ref, out_ref, low_ref, wide_ref, rows_ref):
    width = start_ref.shape[1]
    grad = sum(mm_nt(packed_ref[k], weight_ref[:, k * width : (k + 1) * width]) for k in range(3))
    normed, inv = normed_of(start_ref[...].astype(F32))
    back = mid_grad_ref[...] + normed_back(grad, normed, inv, small_ref[0:1])
    out_ref[...] = back
    low_ref[...] = back.astype(BF16)
    wide_ref[...] = back.astype(BF16).astype(F32)

    @pl.when(pl.program_id(0) == 0)
    def _():
        rows_ref[...] = jnp.zeros_like(rows_ref)

    rows_ref[0:1] += columns_sum(grad * normed)
    rows_ref[1:2] += columns_sum(grad)
    rows_ref[2:3] += columns_sum(packed_ref[0])
    rows_ref[3:4] += columns_sum(packed_ref[2])
    rows_ref[4:5] += columns_sum(back * back)


def start_back(packed_grad, weight, mid_grad, start, small):
    length, width = start.shape
    shape = jax.ShapeDtypeStruct
    tokens = pl.BlockSpec((CHUNK, width), lambda i: (i, 0))
    return pl.pallas_call(
        start_back_kernel,
        grid=(length // CHUNK,),
        out_shape=[shape((length, width), kind) for kind in (F32, BF16, F32)] + [shape((8, width), F32)],
        in_specs=[pl.BlockSpec((3, CHUNK, width), lambda i: (0, i, 0)), whole_block(weight.shape), tokens, tokens]
        + [whole_block(small.shape)],
        out_specs=[tokens, tokens, tokens, whole_block((8, width))],
        cost_estimate=cost(6 * length * width * width, 20 * length * width),
        compiler_params=pltpu.CompilerParams(vmem_limit_bytes=40 * MEGA),
    )(packed_grad, weight, mid_grad, start, small)


def weight_grads_kernel(place_ref, ones_ref, mixed_ref, low_ref, *refs):
    packed, (branch_ref, pre_ref, down_ref, act_ref, grad_ref, small_ref) = refs[:3], refs[3:9]
    out_ref, square_ref, wide = refs[9:]
    width = ones_ref.shape[1]
    tall = width // 4
    start = pl.multiple_of(place_ref[0], 128)
    skip = pl.multiple_of(place_ref[1], 8)
    pieces = (
        (ones_ref, ((packed[0], 0, 0), (packed[1], 0, 1), (packed[2], 1, 0))),
        (mixed_ref, ((branch_ref, 1, 1),)),
        (low_ref, ((pre_ref, 2, 0), (pre_ref, 2, 1), (pre_ref, 3, 0), (pre_ref, 3, 1))),
    )
    half = width // 2
    square = jnp.zeros((1, half), F32)
    for left_ref, rights in pieces:
        left = left_ref[:, pl.ds(start, SIDE)].T
        for k, (right_ref, piece, side) in enumerate(rights):
            right = right_ref[0] if len(right_ref.shape) == 3 else right_ref[:, pl.ds(k * half, half)]
            wide[...] = mm(left, right)
            grad = wide[pl.ds(skip, tall), :]
            out_ref[piece * tall : (piece + 1) * tall, side * half : (side + 1) * half] = grad
            square = square + jnp.sum(grad * grad, 0, keepdims=True)
    left = down_ref[...].T
    first = 4 * tall
    for side in range(2):
        grad = mm(left, act_ref[:, side * half : (side + 1) * half])
        out_ref[first : first + half, side * half : (side + 1) * half] = grad
        square = square + jnp.sum(grad * grad, 0, keepdims=True)
    square_ref[...] = square
    first += half
    tall = grad_ref.shape[0] // 4
    lines = out_ref.shape[0] - first
    out_ref[first:, :] = jnp.zeros((lines, width), F32)
    for k in range(4):
        rows = slice(first + tall * (k // 3), first + tall * (k // 3) + tall)
        part = grad_ref[k * tall : (k + 1) * tall, pl.ds(start, SIDE)]
        out_ref[rows, SIDE * (k % 3) : SIDE * (k % 3 + 1)] = jnp.where(skip > 0, pltpu.roll(part, SIDE - width // 12, 1), part)
    first += 2 * tall
    out_ref[first : first + small_ref.shape[0], :] = small_ref[...]


def weight_grads(ln_one, mixed, low, packed_grad, branch, pre, down_grad, act, grad_in, small_ex, row_at, col_at):
    length, width = ln_one.shape
    half, tall = width // 2, width // 4
    hidden, tokens = pre.shape[1] // 2, length // 2
    shape = jax.ShapeDtypeStruct
    first = row_at * tall
    place = jnp.stack([first // 128 * 128, first % 128, row_at, col_at]).astype(jnp.int32)
    unit = lambda k: pl.BlockSpec((1, length, half), lambda i, at: ((3 * at[3] + k) // 2, 0, (3 * at[3] + k) % 2))
    by_col = lambda size: pl.BlockSpec((length, size), lambda i, at: (0, at[3]))
    lines = 4 * tall + half + tokens // 2 + 32
    return pl.pallas_call(
        weight_grads_kernel,
        grid_spec=pltpu.PrefetchScalarGridSpec(
            num_scalar_prefetch=1,
            grid=(1,),
            in_specs=[whole_block((length, width))] * 3
            + [unit(k) for k in range(3)]
            + [by_col(half), by_col(hidden), by_col(half), pl.BlockSpec((length, width), lambda i, at: (0, at[2]))]
            + [pl.BlockSpec((tokens, width), lambda i, at: (at[3], 0)), whole_block(small_ex.shape)],
            out_specs=[whole_block((lines, width)), whole_block((1, half))],
            scratch_shapes=[pltpu.VMEM((SIDE, half), F32)],
        ),
        out_shape=[shape((lines, width), F32), shape((1, half), F32)],
        cost_estimate=cost(2 * length * width * width * 2, 16 * length * width),
        compiler_params=pltpu.CompilerParams(vmem_limit_bytes=56 * MEGA),
    )(place, ln_one, mixed, low, packed_grad, packed_grad, packed_grad, branch, pre, down_grad, act, grad_in, small_ex)


def body(
    token_ids,
    target_ids,
    included,
    tok_table,
    pos_table,
    qkv_weight,
    attn_weight,
    up_weight,
    down_weight,
    small_params,
    table_rows,
    table_cols,
    pos_rows,
    pos_cols,
    qkv_rows,
    qkv_cols,
    attn_rows,
    attn_cols,
    up_rows,
    up_cols,
    down_rows,
    down_cols,
    small_second,
    table_noise,
    pos_noise,
    qkv_noise,
    attn_noise,
    up_noise,
    down_noise,
    small_noise,
):
    n_row = lax.axis_size("row")
    n_col = lax.axis_size("col")
    n_data = lax.axis_size("dp")
    row_at = lax.axis_index("row")
    col_at = lax.axis_index("col")
    ids, targets = token_ids[0], target_ids[0]
    length = ids.shape[0]
    width = small_params.shape[1]
    vocab_here = tok_table.shape[0]
    vocab_start = (col_at * n_row + row_at) * vocab_here
    small = small_params

    target = targets - vocab_start
    target = jnp.where((target >= 0) & (target < vocab_here), target, -1)[None]
    lists = token_lists(ids, vocab_start, vocab_here)
    tuned = (n_data, n_row, n_col) == (4, 4, 2)
    block = length // (n_row * n_col)
    if tuned:
        beside = lambda item: lax.ppermute(item, "dp", [(at, at ^ 2) for at in range(4)])
        met_ids, met_target = beside(jnp.stack([ids, targets]))
        met_target = met_target - vocab_start
        met_target = jnp.where((met_target >= 0) & (met_target < vocab_here), met_target, -1)[None]
        met_lists = token_lists(met_ids, vocab_start, vocab_here)

    weights_in = [tok_table, pos_table, qkv_weight, attn_weight, up_weight, down_weight]
    noises = [table_noise, pos_noise, qkv_noise, attn_noise, up_noise, down_noise]
    lows = [item.astype(BF16) for item in weights_in[2:]]
    if tuned:
        shards = [item.reshape(n_data, -1, item.shape[1]) for item in lows]
        start, table_low, table_sq, qkv_full, attn_full, up_full, down_full = front(
            ids, tok_table, pos_table, shards, n_row
        )
        stream_in = start.reshape(length, width)
        qkv_full, attn_full, up_full, down_full = (
            item.reshape(width, -1) for item in (qkv_full, attn_full, up_full, down_full)
        )
    else:
        local_ids = ids - vocab_start
        inside = (local_ids >= 0) & (local_ids < vocab_here)
        safe_ids = jnp.clip(local_ids, 0, vocab_here - 1)
        looked = jnp.where(inside[:, None], jnp.take(tok_table, safe_ids, axis=0), 0.0).astype(BF16)
        table_sq = jnp.sum(tok_table * tok_table, 0, keepdims=True)
        table_low = jnp.pad(tok_table.astype(BF16), ((0, blocks_of(vocab_here) * BLOCK - vocab_here), (0, 0)))
        stream_in = (plane_sum(looked).astype(F32) + gather_matrix(pos_table, 1)).astype(BF16)
        qkv_full, attn_full, up_full = (gather_matrix(item, 0) for item in lows[:3])
        down_full = gather_matrix(lows[3], 1)

    ln_one = (normed_of(stream_in.astype(F32))[0] * small[0] + small[1]).astype(BF16)
    bias = jnp.concatenate([small[2], jnp.zeros_like(small[2]), small[3]])
    packed = (mm(ln_one, qkv_full) + bias).astype(BF16)
    mixed, attn_log = attend(packed)
    up_bias = small[7:11].reshape(1, -1)
    stream_mid, ln_two, stream_out, ln_fin = middle_forward(
        stream_in, mixed, attn_full, up_full, up_bias, down_full, small
    )

    exps, tops, exp_sums, picked = head(table_low, vocab_here, ln_fin, target)
    if tuned:
        met_z = beside(ln_fin)
        log_norm, picked = log_total(tops, exp_sums, picked, n_row, 3)
        met_log = beside(log_norm)
    else:
        top = lax.pmax(jnp.max(tops, 0), PLANE)
        log_norm = top + jnp.log(plane_sum(jnp.sum(exp_sums * jnp.exp(tops - top[None]), 0)))
        picked = plane_sum(picked)
    loss = jnp.sum(log_norm - picked)
    final_part, table_ex = head_back(exps, tops, log_norm, target, table_low, ln_fin)
    if tuned:
        final_part = plane_total(final_part.reshape(n_col, n_row, block, width), 2)
        final_grad = final_part.reshape(length, width)
    else:
        final_grad = plane_sum(final_part)

    down_grad, pre_grad, up_act, pre_sum, mid_grad, branch_grad, mixed_grad, mid_rows = middle_back(
        final_grad, stream_out, stream_mid, ln_two, attn_full, up_full, up_bias, down_full, small
    )
    packed_grad = attend_back(packed, mixed_grad, attn_log)
    grad_in, emb_low, emb_grad, start_rows = start_back(packed_grad, qkv_full, mid_grad, stream_in, small)
    small_ex = jnp.concatenate(
        [start_rows[:4], mid_rows[5:6], mid_rows[3:5], pre_sum.reshape(-1, width), mid_rows[2:3], mid_rows[:2]], 0
    )
    if tuned:
        met_grad = beside(emb_low)
        packed_ex, layer_sq = weight_grads(
            ln_one,
            mixed,
            ln_two,
            packed_grad,
            branch_grad,
            pre_grad,
            down_grad,
            up_act,
            grad_in,
            small_ex,
            row_at,
            col_at,
        )
        layer_sq = jnp.sum(layer_sq)
    else:
        tok_here, dim_here = pos_table.shape
        pos_ex = lax.dynamic_slice(grad_in, (col_at * tok_here, row_at * dim_here), (tok_here, dim_here))
        all_grads = packed_grad.transpose(1, 0, 2).reshape(length, -1)

        def columns_of(array, at, parts):
            size = array.shape[1] // parts
            return lax.dynamic_slice_in_dim(array, at * size, size, 1)

        layer_ex = [
            mm_tn(columns_of(left, at_left, n_left), columns_of(right, at_right, n_right))
            for left, at_left, n_left, right, at_right, n_right in (
                (ln_one, row_at, n_row, all_grads, col_at, n_col),
                (mixed, row_at, n_row, branch_grad, col_at, n_col),
                (ln_two, row_at, n_row, pre_grad, col_at, n_col),
                (down_grad, col_at, n_col, up_act, row_at, n_row),
            )
        ]
        layer_sq = sum(jnp.sum(item * item) for item in layer_ex)
    table_ex, own_sq = add_own_rows(table_ex, lists, emb_grad)

    own_sq = jnp.sum(own_sq) + layer_sq
    same_sq = jnp.sum(start_rows[4]) + jnp.sum(small_ex * small_ex)
    taken = included[0].astype(F32)
    ex_at = lax.axis_index("dp")
    leads = (row_at + col_at == 0).astype(F32)
    at_own = (jnp.arange(n_data) == ex_at).astype(F32)
    total = jnp.concatenate([at_own * (own_sq + leads * same_sq), at_own * leads * taken, leads * taken * loss[None]])
    if tuned:
        total = jnp.pad(total, (0, 1024 - total.shape[0])).reshape(8, 128)
        total, met_grad = lax.optimization_barrier((total, met_grad))
        total = sum_small(total, n_row, 4).reshape(-1)
    else:
        total = lax.psum(lax.psum(total, PLANE), "dp")
    norm_sq, taken, loss_sum = total[:n_data], total[n_data : 2 * n_data], total[2 * n_data]
    share = taken * jnp.minimum(1.0, CLIP * lax.rsqrt(norm_sq + 1e-12))
    example_norm = jnp.sqrt(norm_sq[ex_at])
    own_share = share[ex_at]

    divisor = SAMPLE * n_data
    vocab = vocab_here * n_row * n_col
    count = blocks_of(vocab_here)
    table_old = jnp.pad(table_rows, (0, count * BLOCK - vocab_here), constant_values=1.0).reshape(count, 1, BLOCK)
    olds = [(pos_rows, pos_cols), (qkv_rows, qkv_cols), (attn_rows, attn_cols), (up_rows, up_cols)]
    olds.append((down_rows, down_cols))
    ends = (token_ids.shape[1] * jnp.sum(taken), example_norm[None])
    if tuned:
        core = ex_at % 2
        to_core = lambda item: lax.ppermute(item, "dp", [(at, at ^ 1) for at in range(4)])
        halves = (own_share * packed_ex).astype(BF16).reshape(2, -1, width)
        half = (halves[core].astype(F32) + to_core(halves[1 - core]).astype(F32)).astype(BF16)
        shares = jnp.stack([own_share, share[ex_at ^ 2]])
        half, shares = lax.optimization_barrier((half, shares))
        from_beside = beside(half)
        middle = count // 2
        spans = [(0, middle), (middle, count - middle)]
        met = (met_z, met_log, met_target, met_lists, met_grad.astype(F32), shares)
        pair_sums = [table_sum(table_ex, table_low, *met, *span) for span in spans]
        pair_sums = [[item, to_core(item)] for item in pair_sums]
        into, over = None, []
        for pair, span in zip(pair_sums, spans):
            into, *more = table_gradient(pair, table_noise, table_old, divisor, *span, into)
            over.append(more)
        table_grad = into
        half = join(half, from_beside, over[1][1])
        other_half = to_core(half)
        packed = jnp.concatenate(
            [jnp.where(core == 0, half, other_half), jnp.where(core == 0, other_half, half)], 0
        )
        rows_blocks = jnp.concatenate([item[0] for item in over], 0)
        cols, scaled, level = (over[0][k] + over[1][k] for k in (1, 2, 3))
        small_grads, smalls, (over_cols, over_rows, squares) = small_gradients(
            packed, small_params, small_second, small_noise, weights_in[1:], noises[1:], divisor
        )
        scalars = jnp.where(jnp.arange(128) == 5, jnp.sum(table_sq), squares[0])
        table_over = jnp.concatenate([cols[0], scaled[0], scalars, level[0]]).reshape(-1, 128)
        table_over = jnp.pad(table_over, ((0, -table_over.shape[0] % 8), (0, 0)))
        wide = max(item.shape[0] for pair in olds for item in pair)
        lines = [jnp.pad(item, (0, wide - item.shape[0])) for pair in zip(*olds) for item in pair + (table_cols,) * 3]
        old_lines = jnp.stack(lines)
        lines, factors = statistics(
            table_over, over_cols, over_rows, old_lines, small_grads, width, n_row, vocab, 5
        )
        table_new, table_cols_new, rows_new, cols_new, news = update(
            tok_table, table_grad, rows_blocks, factors, lines, weights_in[1:], small_grads
        )
        outputs = [table_grad, rows_blocks.reshape(-1)[:vocab_here], table_cols_new, table_new]
        for group in zip(small_grads, rows_new, cols_new, news):
            outputs.extend(group)
        return tuple(outputs) + tuple(smalls) + (loss_sum,) + ends

    weight_total = plane_sum(
        jnp.stack([jnp.sum(table_sq)] + [jnp.sum(item * item) for item in weights_in[1:]])
    )
    table_sum_all = example_sum((own_share * table_ex.astype(F32)).astype(BF16))
    others = [(own_share * item).astype(BF16) for item in [pos_ex] + layer_ex + [small_ex]]
    sums = [example_sum(item).astype(F32) for item in others]
    grads = [(sums[index] + NOISE * CLIP * noises[index + 1]) / divisor for index in range(5)]
    table_grad, table_rows_new, *table_over = table_gradient(
        [table_sum_all], table_noise, table_old, divisor, 0, count
    )
    table_rows_new = table_rows_new.reshape(-1)[:vocab_here]
    by_row = [False, True, True, True, False]
    over = {"col": [], "row": []}
    for grad, first in zip(grads, by_row):
        squares = grad * grad + 1e-30
        over["col" if first else "row"].append(jnp.sum(squares, 1))
        over["row" if first else "col"].append(jnp.sum(squares, 0))
    over = {axis: [lax.psum(item, axis) for item in items] for axis, items in over.items()}
    table_over = [plane_sum(item[0]) for item in table_over]
    news, levels = [], []
    for index, (grad, first) in enumerate(zip(grads, by_row)):
        rows_parts, cols_parts = (n_row, n_col) if first else (n_col, n_row)
        row_sum = over["col" if first else "row"][index]
        col_sum = over["row" if first else "col"][index]
        rows_new = DECAY * olds[index][0] + (1.0 - DECAY) * (row_sum / (grad.shape[1] * cols_parts))
        cols_new = DECAY * olds[index][1] + (1.0 - DECAY) * (col_sum / (grad.shape[0] * rows_parts))
        news.append((rows_new, cols_new))
        levels += [
            jnp.sum(rows_new) / (grad.shape[0] * rows_parts * cols_parts),
            jnp.sum(grad * grad / (rows_new[:, None] * cols_new[None, :])),
        ]
    levels = plane_sum(jnp.stack(levels))

    def updated(index, weight, grad, rows_new, cols_new, level, square_sum, entries_all):
        size = RATE * jnp.maximum(1e-3, jnp.sqrt(weight_total[index] / entries_all))
        size = size / jnp.maximum(1.0, jnp.sqrt(square_sum * level / entries_all))
        size = size * jnp.sqrt(level)
        return weight - grad * lax.rsqrt(rows_new)[:, None] * (size * lax.rsqrt(cols_new))[None, :]

    table_cols_new = DECAY * table_cols + (1.0 - DECAY) * (table_over[0] / vocab + 1e-30)
    table_new = updated(
        0,
        tok_table,
        table_grad,
        table_rows_new,
        table_cols_new,
        table_over[2][0] / vocab,
        jnp.sum(table_over[1] / table_cols_new),
        vocab * width,
    )
    outputs = [table_grad, table_rows_new, table_cols_new, table_new]
    for index, grad in enumerate(grads):
        rows_new, cols_new = news[index]
        weight_new = updated(
            index + 1,
            weights_in[index + 1],
            grad,
            rows_new,
            cols_new,
            levels[2 * index],
            levels[2 * index + 1],
            grad.shape[0] * grad.shape[1] * n_row * n_col,
        )
        outputs.extend([grad, rows_new, cols_new, weight_new])
    small_grad = (sums[5] + NOISE * CLIP * small_noise) / divisor
    second_new = DECAY * small_second + (1.0 - DECAY) * (small_grad * small_grad + 1e-30)
    small_update = small_grad * lax.rsqrt(second_new)
    small_update = small_update / jnp.maximum(1.0, jnp.sqrt(jnp.mean(small_update * small_update)))
    small_size = RATE * jnp.maximum(1e-3, jnp.sqrt(jnp.mean(small_params * small_params)))
    small_new = small_params - small_size * small_update
    return tuple(outputs) + (small_grad, second_new, small_new, loss_sum) + ends


def solution(mesh):
    table, by_col, by_row = P(("col", "row"), None), P("col", "row"), P("row", "col")
    return jax.shard_map(
        body,
        mesh=mesh,
        in_specs=(P("dp", None), P("dp", None), P("dp"))
        + (table, by_col, by_row, by_row, by_row, by_col, P())
        + (P(("col", "row")), P(), P("col"), P("row"))
        + (P("row"), P("col")) * 3
        + (P("col"), P("row"), P())
        + (table, by_col, by_row, by_row, by_row, by_col, P()),
        out_specs=(table, P(("col", "row")), P(), table)
        + (by_col, P("col"), P("row"), by_col)
        + (by_row, P("row"), P("col"), by_row) * 3
        + (by_col, P("col"), P("row"), by_col)
        + (P(), P(), P(), P(), P(), P("dp")),
        check_vma=False,
    )
```

```python
import functools

import jax
import jax.numpy as jnp
from jax import lax
from jax.experimental import pallas as pl
from jax.experimental.pallas import tpu as pltpu
from jax.sharding import PartitionSpec as P

HEADS = 12
HEAD = 64
STEP = 10
CLIP = 1.0
NOISE = 0.002
SAMPLE = 0.5
RATE = 0.5
DECAY = 1.0 - STEP ** (-0.8)

F32 = jnp.float32
BF16 = jnp.bfloat16
PLANE = ("row", "col")
MESH = pl.DeviceIdType.MESH


def dot_f32(left, right, dims):
    return lax.dot_general(left, right, (dims, ((), ())), preferred_element_type=F32)


def mm(left, right):
    return dot_f32(left, right, ((1,), (0,)))


def mm_nt(left, right):
    return dot_f32(left, right, ((1,), (1,)))


def mm_tn(left, right):
    return dot_f32(left, right, ((0,), (0,)))


def gather_matrix(block, row_dim):
    part = lax.all_gather(block, "row", axis=row_dim, tiled=True)
    return lax.all_gather(part, "col", axis=1 - row_dim, tiled=True)


def plane_sum(array):
    return lax.psum(array, PLANE)


def example_sum(array):
    return lax.psum(array, "dp")


class Link:
    def __init__(self, send_sems, recv_sems):
        self.dp, self.row, self.col = (lax.axis_index(axis) for axis in ("dp", "row", "col"))
        self.x, self.core = self.dp // 2, self.dp % 2
        self.beside = 2 * (1 - self.x) + self.core
        self.sibling = 2 * self.x + 1 - self.core
        self.send_sems, self.recv_sems = send_sems, recv_sems
        self.n_send = 0
        self.open = []

    def device(self, **moved):
        return {"dp": self.dp, "row": self.row, "col": self.col, **moved}

    def send(self, src, dst, recv, device, when=None):
        sem = self.send_sems.at[self.n_send]
        self.n_send += 1
        copy = pltpu.make_async_remote_copy(
            src_ref=src,
            dst_ref=dst,
            send_sem=sem,
            recv_sem=self.recv_sems.at[recv],
            device_id=device,
            device_id_type=MESH,
        )
        self.open.append((copy, when))
        copy.start() if when is None else pl.when(when)(copy.start)

    def landed(self, dst, recv):
        pltpu.make_async_remote_copy(
            src_ref=dst,
            dst_ref=dst,
            send_sem=self.send_sems.at[0],
            recv_sem=self.recv_sems.at[recv],
            device_id=self.device(col=1 - self.col),
            device_id_type=MESH,
        ).wait_recv()

    def finish(self):
        for copy, when in self.open:
            copy.wait_send() if when is None else pl.when(when)(copy.wait_send)
        self.open = []

    def greet(self, devices):
        barrier = pltpu.get_barrier_semaphore()
        count = 0
        for device, when in devices:

            def signal(device=device):
                pl.semaphore_signal(barrier, inc=1, device_id=device, device_id_type=MESH)

            if when is None:
                signal()
                count = count + 1
            else:
                pl.when(when)(signal)
                count = count + when.astype(jnp.int32)
        pl.semaphore_wait(barrier, count)

    def plane_peers(self, n_row):
        me, peers = self.col * n_row + self.row, []
        for k in range(1, 2 * n_row):
            index = (me + k) % (2 * n_row)
            peers.append((index, self.device(row=index % n_row, col=index // n_row)))
        return me, peers

    def example_peers(self):
        return [((self.dp + k) % 4, self.device(dp=(self.dp + k) % 4)) for k in range(1, 4)]

    def plane_neighbours(self, n_row):
        return [
            (self.device(row=self.row + 1), self.row < n_row - 1),
            (self.device(row=self.row - 1), self.row > 0),
            (self.device(col=1 - self.col), None),
        ]


def run_together(*steps):
    steps = list(steps)
    while steps:
        for step in list(steps):
            try:
                next(step)
            except StopIteration:
                steps.remove(step)


def scatter_sum(link, base, n_row, part, from_col, ins, outs, own, make=None, span=slice(None)):
    row, col = link.row, link.col
    (up_in, down_in), (up_out, down_out) = ins, outs
    y_base, up_base, down_base = base, base + n_row, base + 2 * n_row
    order = [at for k in range(n_row // 2) for at in (n_row - 1 - k, k)]
    for at in order:
        if make is not None:
            make(1 - col, at)
        link.send(part.at[1 - col, at, span], from_col.at[at, span], y_base + at, link.device(col=1 - col))
    yield
    if make is not None:
        for k, at in enumerate(order):
            make(col, at)
            if k % 2:
                yield
    waiting = list(order)

    def mine(at):
        return part[col, at, span].astype(F32) + from_col[at, span].astype(F32)

    for k in range(n_row - 1):
        for at in (n_row - 1 - k, k):
            if at in waiting:
                waiting.remove(at)
                link.landed(from_col.at[at, span], y_base + at)
        for at, going, more, source, target, base_at, device in (
            (n_row - 1 - k, row < n_row - 1 - k, row > 0, up_in, up_out, up_base, link.device(row=row + 1)),
            (k, row > k, row < n_row - 1, down_in, down_out, down_base, link.device(row=row - 1)),
        ):

            @pl.when(going & more)
            def _():
                link.landed(source.at[at, span], base_at + at)
                target[at, span] = (mine(at) + source[at, span].astype(F32)).astype(BF16)

            @pl.when(going & jnp.logical_not(more))
            def _():
                target[at, span] = mine(at).astype(BF16)

            link.send(target.at[at, span], source.at[at, span], base_at + at, device, going)
        yield
    own[span] = mine(row)

    for more, source, base_at in ((row > 0, up_in, up_base), (row < n_row - 1, down_in, down_base)):

        @pl.when(more)
        def _():
            link.landed(source.at[row, span], base_at + row)
            own[span] += source[row, span].astype(F32)


def spread(link, base, n_row, own, place, onward=None):
    row, col = link.row, link.col
    up, down, side = (device for device, _ in link.plane_neighbours(n_row))
    here = place(row, col)
    link.send(own, here, base + row, up, row < n_row - 1)
    link.send(own, here, base + row, down, row > 0)
    if onward is not None:
        yield
    link.send(own, here, base + n_row + row, side)
    yield
    def arrive(k):
        for at, there in [(row - k, row >= k), (row + k, row + k < n_row)][: 2 if k else 1]:
            block = place(at, 1 - col)
            pl.when(there)(functools.partial(link.landed, block, base + n_row + at))
            if onward is not None:
                onward(at, 1 - col, there)

    for k in range(1, n_row):
        for at, there, device, further in (
            (row - k, row >= k, up, row < n_row - 1),
            (row + k, row + k < n_row, down, row > 0),
        ):
            block = place(at, col)
            pl.when(there)(functools.partial(link.landed, block, base + at))
            if k < n_row - 1:
                link.send(block, block, base + at, device, there & further)
            link.send(block, block, base + n_row + at, side, there)
            if onward is not None:
                onward(at, col, there)
        yield
        if k > 1:
            arrive(k - 2)
            yield
    for k in range(n_row - 2, n_row):
        arrive(k)
        yield


def spread_matrix(link, base, n_row, shard, whole, by_row, local_sems):
    row, col, at_x, at_core = link.row, link.col, link.x, link.core
    columns = shard.shape[-1]

    def block(at_row, at_col, x, core):
        lead, side = (at_row, at_col) if by_row else (at_col, at_row)
        return whole.at[lead, x, core, :, pl.ds(pl.multiple_of(side * columns, 128), columns)]

    local = []
    for index, x in enumerate((at_x, 1 - at_x)):
        copy = pltpu.make_async_copy(
            shard.at[2 * x + at_core], block(row, col, x, at_core), local_sems.at[index]
        )
        copy.start()
        local.append(copy)
    x_base, core_base = base + 2 * n_row, base + 4 * n_row
    beside, sibling = link.device(dp=link.beside), link.device(dp=link.sibling)

    def side_of(at_col, x, core):
        if not by_row:
            return whole.at[at_col, x, core]
        return whole.at[:, x, core, :, pl.ds(pl.multiple_of(at_col * columns, 128), columns)]

    def to_x(at_row, at_col, when):
        ref = block(at_row, at_col, at_x, at_core)
        link.send(ref, ref, x_base + at_col * n_row + at_row, beside, when)

    def to_core(at_col, x, index):
        ref = side_of(at_col, x, at_core)
        link.send(ref, ref, core_base + index, sibling)

    yield from spread(link, base, n_row, shard.at[link.dp], lambda r, c: block(r, c, at_x, at_core), to_x)
    for copy in local:
        copy.wait()
    to_core(0, at_x, 0)
    to_core(1, at_x, 1)
    yield
    for index, at_col in enumerate((col, 1 - col)):
        for k in range(n_row):
            at_row = lax.rem(row + k, n_row)
            if k or index:
                link.landed(block(at_row, at_col, 1 - at_x, at_core), x_base + at_col * n_row + at_row)
            if k % 2:
                yield
        to_core(at_col, 1 - at_x, 2 + at_col)
    yield
    for at_col in range(2):
        link.landed(side_of(at_col, at_x, 1 - at_core), core_base + at_col)
        link.landed(side_of(at_col, 1 - at_x, 1 - at_core), core_base + 2 + at_col)


N_MATRIX = 4 * 4 + 4


def front_kernel(n_row, ids, table, pos, *refs):
    shards, (start, low, square), wholes = refs[:4], refs[4:7], refs[7:11]
    held, staged, row_block_ref, pos_in, looked = refs[11:16]
    from_col, up_in, down_in, up_out, down_out, own, own_low = refs[16:23]
    send_sems, recv_sems, local_sems, table_sems, low_sems = refs[23:]
    limit, width = table.shape
    block = own.shape[0]
    piece = limit // table_sems.shape[0]
    loads = [
        pltpu.make_async_copy(table.at[pl.ds(at, piece)], held.at[pl.ds(at, piece)], table_sems.at[k])
        for k, at in enumerate(range(0, limit, piece))
    ]
    for load in loads:
        load.start()
    link = Link(send_sems, recv_sems)
    row_peers = [(link.row + k) % n_row for k in range(1, n_row)]
    link.greet(
        [(link.device(row=peer), None) for peer in row_peers]
        + [(link.device(col=1 - link.col), None)]
        + [(link.device(dp=link.beside), None), (link.device(dp=link.sibling), None)]
    )
    first = (link.col * n_row + link.row) * limit
    pos_base = 5 * n_row + 4 * N_MATRIX

    def look_up(col, at):
        token = (col * n_row + at) * block

        def step(k, carry):
            entry = ids[token + k] - first
            inside = (entry >= 0) & (entry < limit)
            row = held[pl.ds(jnp.clip(entry, 0, limit - 1), 1), :]
            row_block_ref[pl.ds(k, 1), :] = jnp.where(inside, row, 0.0)
            return carry

        lax.fori_loop(0, block, step, 0, unroll=8)
        looked[col, at] = row_block_ref[...].astype(BF16)

    def tokens():
        for peer in row_peers:
            rows = pos.at[:, pl.ds(pl.multiple_of(peer * block, 128), block)]
            link.send(rows, pos_in.at[link.row], pos_base + link.row, link.device(row=peer))
        pos_in[link.row] = pos[:, pl.ds(pl.multiple_of(link.row * block, 128), block)]
        for load in loads:
            load.wait()
        yield from scatter_sum(
            link, 0, n_row, looked, from_col, (up_in, down_in), (up_out, down_out), own, look_up
        )
        for peer in row_peers:
            link.landed(pos_in.at[peer], pos_base + peer)
        pos_own = jnp.concatenate([pos_in[k] for k in range(n_row)], 0).T
        own_low[...] = (own[...] + pos_own).astype(BF16)
        start[link.col, link.row] = own_low[...]
        yield from spread(link, 3 * n_row, n_row, own_low, lambda r, c: start.at[c, r])

    def shorten():
        yield
        square[...] = jnp.zeros_like(square)
        count = low.shape[0] // BLOCK
        stores = []
        for k in range(count):
            rows = min(BLOCK, limit - k * BLOCK)
            if k > 1:
                stores[k - 2].wait()
            part = held[k * BLOCK : k * BLOCK + rows, :]
            square[...] += jnp.sum(part * part, 0, keepdims=True)
            if rows < BLOCK:
                staged[k % 2, rows:] = jnp.zeros((BLOCK - rows, width), BF16)
            staged[k % 2, :rows] = part.astype(BF16)
            stores.append(
                pltpu.make_async_copy(staged.at[k % 2], low.at[pl.ds(k * BLOCK, BLOCK)], low_sems.at[k % 2])
            )
            stores[k].start()
            yield
        for store in stores[-2:]:
            store.wait()

    matrices = [
        spread_matrix(
            link, 5 * n_row + index * N_MATRIX, n_row, shards[index], wholes[index], index < 3, local_sems.at[index]
        )
        for index in range(4)
    ]
    run_together(*matrices, tokens(), shorten())
    link.finish()


def front(ids, table, pos, shards, n_row):
    limit, width = table.shape
    block = ids.shape[0] // (2 * n_row)
    low = (pl.cdiv(limit, BLOCK) * BLOCK, width)
    wholes = [(n_row, 2, 2) + shard.shape[1:2] + (2 * shard.shape[2],) for shard in shards[:3]]
    wholes.append((2, 2, 2) + shards[3].shape[1:2] + (n_row * shards[3].shape[2],))
    rows = pltpu.VMEM((n_row, block, width), BF16)
    vmem, hbm = pl.BlockSpec(memory_space=pltpu.VMEM), pl.BlockSpec(memory_space=pl.ANY)
    shape = jax.ShapeDtypeStruct
    return pl.pallas_call(
        functools.partial(front_kernel, n_row),
        out_shape=[shape((2, n_row, block, width), BF16), shape(low, BF16), shape((1, width), F32)]
        + [shape(whole, BF16) for whole in wholes],
        in_specs=[pl.BlockSpec(memory_space=pltpu.SMEM), hbm, vmem] + [hbm] * 4,
        out_specs=[vmem, hbm, vmem] + [hbm] * 4,
        scratch_shapes=[pltpu.VMEM(table.shape, F32), pltpu.VMEM((2, BLOCK, width), BF16)]
        + [pltpu.VMEM((block, width), F32), pltpu.VMEM((n_row,) + pos.shape[:1] + (block,), F32)]
        + [pltpu.VMEM((2, n_row, block, width), BF16)]
        + [rows] * 5
        + [pltpu.VMEM((block, width), F32), pltpu.VMEM((block, width), BF16)]
        + [
            pltpu.SemaphoreType.DMA((220,)),
            pltpu.SemaphoreType.DMA((6 * n_row + 4 * N_MATRIX,)),
            pltpu.SemaphoreType.DMA((4, 2)),
            pltpu.SemaphoreType.DMA((6,)),
            pltpu.SemaphoreType.DMA((2,)),
        ],
        compiler_params=pltpu.CompilerParams(
            collective_id=1, has_side_effects=True, vmem_limit_bytes=56 * 1024 * 1024
        ),
    )(ids, table, pos, *shards)


def total_kernel(n_row, part, total, *refs):
    from_col, up_in, down_in, up_out, down_out, own, own_low, send_sems, recv_sems = refs
    link = Link(send_sems, recv_sems)
    link.greet(link.plane_neighbours(n_row))

    def steps(base, span):
        yield from scatter_sum(
            link, base, n_row, part, from_col, (up_in, down_in), (up_out, down_out), own, None, span
        )
        own_low[span] = own[span].astype(BF16)
        total[link.col, link.row, span] = own_low[span]
        place = lambda r, c: total.at[c, r, span]
        yield from spread(link, base + 3 * n_row, n_row, own_low.at[span], place)

    size = own.shape[0] // SPANS
    run_together(*(steps(5 * n_row * k, pl.ds(k * size, size)) for k in range(SPANS)))
    link.finish()


SPANS = 2


def plane_total(part, collective_id):
    n_row, block, width = part.shape[1:]
    rows = pltpu.VMEM((n_row, block, width), BF16)
    vmem = pl.BlockSpec(memory_space=pltpu.VMEM)
    return pl.pallas_call(
        functools.partial(total_kernel, n_row),
        out_shape=jax.ShapeDtypeStruct(part.shape, BF16),
        in_specs=[vmem],
        out_specs=vmem,
        scratch_shapes=[rows] * 5
        + [pltpu.VMEM((block, width), F32), pltpu.VMEM((block, width), BF16)]
        + [pltpu.SemaphoreType.DMA((40 * SPANS,)), pltpu.SemaphoreType.DMA((5 * n_row * SPANS,))],
        compiler_params=pltpu.CompilerParams(
            collective_id=collective_id, has_side_effects=True, vmem_limit_bytes=40 * 1024 * 1024
        ),
    )(part)


FORWARD_QUERIES = 512
BACK_QUERIES = 256


def causal(scores):
    keys = lax.broadcasted_iota(jnp.int32, scores.shape, 0)
    queries = lax.broadcasted_iota(jnp.int32, scores.shape, 1)
    return jnp.where(keys <= queries, scores, -1e30)


def lanes_of(head):
    return slice(head * HEAD, (head + 1) * HEAD)


def attend_kernel(q_ref, k_ref, v_ref, o_ref, log_ref):
    size = FORWARD_QUERIES
    values = [v_ref[:, lanes_of(head)].T for head in range(2)]
    steps = [(head, at) for head in range(2) for at in range(0, q_ref.shape[0], size)]

    def scores_of(head, at):
        queries = q_ref[at : at + size, lanes_of(head)] * HEAD ** (-0.5)
        return mm_nt(k_ref[: at + size, lanes_of(head)], queries)

    later = scores_of(*steps[0])
    for k, (head, at) in enumerate(steps):
        scores = later
        if k + 1 < len(steps):
            later = scores_of(*steps[k + 1])
        here = slice(at, at + size)
        edge = causal(scores[at:])
        top = jnp.max(edge, 0, keepdims=True)
        if at:
            top = jnp.maximum(top, jnp.max(scores[:at], 0, keepdims=True))
        exps = jnp.exp(edge - top)
        count = jnp.sum(exps, 0, keepdims=True)
        exps = exps.astype(BF16)
        if at:
            before = jnp.exp(scores[:at] - top)
            count = count + jnp.sum(before, 0, keepdims=True)
            exps = jnp.concatenate([before.astype(BF16), exps], 0)
        mixed = mm(values[head][:, : at + size], exps)
        o_ref[here, lanes_of(head)] = (mixed / count).T.astype(BF16)
        log_ref[0, head : head + 1, here] = top + jnp.log(count)


def attend(packed):
    length, width = packed.shape[0], packed.shape[1] // 3
    pairs = HEADS // 2
    lanes = 2 * HEAD
    column = lambda first: pl.BlockSpec((length, lanes), lambda i: (0, first + i))
    return pl.pallas_call(
        attend_kernel,
        grid=(pairs,),
        out_shape=[
            jax.ShapeDtypeStruct((length, width), BF16),
            jax.ShapeDtypeStruct((pairs, 2, length), F32),
        ],
        in_specs=[column(0), column(pairs), column(2 * pairs)],
        out_specs=[column(0), pl.BlockSpec((1, 2, length), lambda i: (i, 0, 0))],
        cost_estimate=cost(20 * length * length * width, 8 * length * width),
        compiler_params=pltpu.CompilerParams(vmem_limit_bytes=40 * 1024 * 1024),
    )(packed, packed, packed)


def attend_back_kernel(q_ref, k_ref, v_ref, g_ref, log_ref, out_ref, key_sum, value_sum):
    length, size = q_ref.shape[0], BACK_QUERIES
    keys_turned = [k_ref[:, lanes_of(head)].T for head in range(2)]
    steps = [(head, at) for head in range(2) for at in range(0, length, size)]

    def products_of(head, at):
        queries = q_ref[at : at + size, lanes_of(head)] * HEAD ** (-0.5)
        grads = g_ref[at : at + size, lanes_of(head)]
        scores = mm_nt(k_ref[: at + size, lanes_of(head)], queries)
        return scores, mm_nt(v_ref[: at + size, lanes_of(head)], grads), queries, grads

    later = products_of(*steps[0])
    for k, (head, at) in enumerate(steps):
        scores, prob_grad, queries, grads = later
        if k + 1 < len(steps):
            later = products_of(*steps[k + 1])
        here = slice(at, at + size)
        log_norm = log_ref[0, head : head + 1, here]
        probs = jnp.exp(causal(scores[at:]) - log_norm)
        if at:
            probs = jnp.concatenate([jnp.exp(scores[:at] - log_norm), probs], 0)
        level = jnp.sum(probs * prob_grad, 0, keepdims=True)
        score_grad = (probs * (prob_grad - level)).astype(BF16)
        value_grad = mm(probs.astype(BF16), grads)
        key_grad = mm(score_grad, queries)
        query_grad = mm(keys_turned[head][:, : at + size], score_grad) * HEAD ** (-0.5)
        out_ref[0, here, lanes_of(head)] = query_grad.T.astype(BF16)
        if at:
            value_sum[head, :at] += value_grad[:at]
            key_sum[head, :at] += key_grad[:at]
        value_sum[head, here] = value_grad[at:]
        key_sum[head, here] = key_grad[at:]
        if at + size == length:
            out_ref[1, :, lanes_of(head)] = key_sum[head].astype(BF16)
            out_ref[2, :, lanes_of(head)] = value_sum[head].astype(BF16)


def attend_back(packed, mixed_grad, log_norm):
    length, width = mixed_grad.shape
    pairs = HEADS // 2
    lanes = 2 * HEAD
    column = lambda first: pl.BlockSpec((length, lanes), lambda i: (0, first + i))
    return pl.pallas_call(
        attend_back_kernel,
        grid=(pairs,),
        out_shape=jax.ShapeDtypeStruct((3, length, width), BF16),
        in_specs=[column(0), column(pairs), column(2 * pairs), column(0)]
        + [pl.BlockSpec((1, 2, length), lambda i: (i, 0, 0))],
        out_specs=pl.BlockSpec((3, length, lanes), lambda i: (0, 0, i)),
        scratch_shapes=[pltpu.VMEM((2, length, HEAD), F32)] * 2,
        cost_estimate=cost(30 * length * length * width, 16 * length * width),
        compiler_params=pltpu.CompilerParams(vmem_limit_bytes=48 * 1024 * 1024),
    )(packed, packed, packed, mixed_grad, log_norm)


def meet(link, *exchanges):
    for base, value, slots, me, peers in exchanges:
        slots[me] = value[...]
        for _, device in peers:
            link.send(value, slots.at[me], base + me, device)
    for base, _, slots, _, peers in exchanges:
        for index, _ in peers:
            link.landed(slots.at[index], base + index)


def added(slots):
    total = slots[0]
    for k in range(1, slots.shape[0]):
        total = total + slots[k]
    return total


def sum_small_kernel(n_row, value, total, middle, slots, dp_slots, send_sems, recv_sems):
    link = Link(send_sems, recv_sems)
    me, peers = link.plane_peers(n_row)
    examples = link.example_peers()
    link.greet([(device, None) for _, device in peers + examples])
    meet(link, (0, value, slots, me, peers))
    middle[...] = added(slots)
    meet(link, (2 * n_row, middle, dp_slots, link.dp, examples))
    total[...] = added(dp_slots)
    link.finish()


def sum_small(value, n_row, collective_id):
    vmem = pl.BlockSpec(memory_space=pltpu.VMEM)
    return pl.pallas_call(
        functools.partial(sum_small_kernel, n_row),
        out_shape=jax.ShapeDtypeStruct(value.shape, F32),
        in_specs=[vmem],
        out_specs=vmem,
        scratch_shapes=[pltpu.VMEM(value.shape, F32), pltpu.VMEM((2 * n_row,) + value.shape, F32)]
        + [pltpu.VMEM((4,) + value.shape, F32)]
        + [pltpu.SemaphoreType.DMA((2 * n_row + 2,)), pltpu.SemaphoreType.DMA((2 * n_row + 4,))],
        compiler_params=pltpu.CompilerParams(collective_id=collective_id, has_side_effects=True),
    )(value)


def log_total_kernel(n_row, tops, sums, picked, log_ref, pick_ref, value, slots, send_sems, recv_sems):
    link = Link(send_sems, recv_sems)
    me, peers = link.plane_peers(n_row)
    link.greet([(device, None) for _, device in peers])
    top = jnp.max(tops[...], 0)
    value[0] = top
    value[1] = jnp.sum(sums[...] * jnp.exp(tops[...] - top[None]), 0)
    value[2] = picked[...]
    meet(link, (0, value, slots, me, peers))
    everyone = range(2 * n_row)
    top, total, pick = slots[0, 0], jnp.zeros_like(top), jnp.zeros_like(top)
    for k in everyone:
        top = jnp.maximum(top, slots[k, 0])
    for k in everyone:
        total = total + slots[k, 1] * jnp.exp(slots[k, 0] - top)
        pick = pick + slots[k, 2]
    log_ref[...] = top + jnp.log(total)
    pick_ref[...] = pick
    link.finish()


def log_total(tops, sums, picked, n_row, collective_id):
    length = picked.shape[-1]
    tile = (length // 128, 128)
    tops, sums, picked = (item.reshape(item.shape[:-2] + tile) for item in (tops, sums, picked))
    vmem = pl.BlockSpec(memory_space=pltpu.VMEM)
    log_norm, picked = pl.pallas_call(
        functools.partial(log_total_kernel, n_row),
        out_shape=[jax.ShapeDtypeStruct(tile, F32)] * 2,
        in_specs=[vmem] * 3,
        out_specs=[vmem] * 2,
        scratch_shapes=[pltpu.VMEM((3,) + tile, F32), pltpu.VMEM((2 * n_row, 3) + tile, F32)]
        + [pltpu.SemaphoreType.DMA((2 * n_row,))] * 2,
        compiler_params=pltpu.CompilerParams(collective_id=collective_id, has_side_effects=True),
    )(tops, sums, picked)
    return log_norm.reshape(1, length), picked.reshape(1, length)


BLOCK = 1056
ROWS = 528
MEGA = 1024 * 1024


def cost(flops, bytes_accessed):
    return pl.CostEstimate(flops=flops, bytes_accessed=bytes_accessed, transcendentals=0)


def blocks_of(limit):
    return pl.cdiv(limit, BLOCK)


def entries(shape, first=0, skip=0):
    return lax.broadcasted_iota(jnp.int32, shape, 0) + ((pl.program_id(0) + first) * BLOCK + skip)


PARTS = 3
PART = BLOCK // PARTS


def parts_of():
    return [slice(at, at + PART) for at in range(0, BLOCK, PART)]


def head_kernel(limit, low_ref, z_ref, target_ref, exp_ref, top_ref, sum_ref, pick_ref):
    @pl.when(pl.program_id(0) == 0)
    def _():
        pick_ref[...] = jnp.zeros_like(pick_ref)

    picked = jnp.zeros(pick_ref.shape, F32)
    steps = parts_of()
    later = mm_nt(low_ref[steps[0]], z_ref[...])
    for k, rows in enumerate(steps):
        logits = later
        if k + 1 < PARTS:
            later = mm_nt(low_ref[steps[k + 1]], z_ref[...])
        off = jnp.where(entries((PART, 1), 0, rows.start) < limit, 0.0, -1e30)
        logits = logits + off
        top = jnp.max(logits, 0, keepdims=True)
        hit = lax.broadcasted_iota(jnp.int32, logits.shape, 0) == target_ref[...] - (pl.program_id(0) * BLOCK + rows.start)
        picked = picked + jnp.sum(jnp.where(hit, logits, 0.0), 0, keepdims=True)
        exps = jnp.exp(logits - top)
        exp_ref[rows] = exps.astype(BF16)
        top_ref[k] = top
        sum_ref[k] = jnp.sum(exps, 0, keepdims=True)
    pick_ref[...] += picked


def whole_block(shape):
    return pl.BlockSpec(shape, lambda i, *_: (0,) * len(shape), pipeline_mode=pl.Buffered(1))


def row_block(width):
    return pl.BlockSpec((BLOCK, width), lambda i, *_: (i, 0))


def line_block(width, lines=1):
    return pl.BlockSpec((lines, 1, width), lambda i, *_: (i, 0, 0))


def head(low, limit, z, target):
    length, width = z.shape
    count = blocks_of(limit)
    shape = jax.ShapeDtypeStruct
    line = shape((count * PARTS, 1, length), F32)
    return pl.pallas_call(
        functools.partial(head_kernel, limit),
        grid=(count,),
        out_shape=[shape((count * BLOCK, length), BF16), line, line, shape((1, length), F32)],
        in_specs=[row_block(width), whole_block((length, width)), whole_block((1, length))],
        out_specs=[row_block(length), line_block(length, PARTS), line_block(length, PARTS), whole_block((1, length))],
        cost_estimate=cost(2 * limit * width * length, 2 * limit * width + 2 * limit * length),
        compiler_params=pltpu.CompilerParams(vmem_limit_bytes=48 * MEGA),
    )(low, z, target)


def slope_of(exps, rows, target_ref, first=0):
    entry = lax.broadcasted_iota(jnp.int32, exps.shape, 0)
    target = target_ref[...] - ((pl.program_id(0) + first) * BLOCK + rows.start)
    return jnp.where(entry == target, exps - 1.0, exps).astype(BF16)


def head_back_kernel(exp_ref, top_ref, log_ref, target_ref, low_ref, z_ref, grad_ref, table_ref, slope, total):
    at = pl.program_id(0)
    for k, rows in enumerate(parts_of()):
        scale = jnp.exp(top_ref[k] - log_ref[...])
        slope[rows] = slope_of(exp_ref[rows].astype(F32) * scale, rows, target_ref)
        table_ref[rows] = mm(slope[rows], z_ref[...]).astype(BF16)
    part = mm_tn(low_ref[...], slope[...])

    @pl.when(at == 0)
    def _():
        total[...] = part

    @pl.when(at > 0)
    def _():
        total[...] += part

    @pl.when(at == pl.num_programs(0) - 1)
    def _():
        grad_ref[...] = total[...].T.astype(BF16)


def head_back(exps, tops, log_norm, target, low, z):
    length, width = z.shape
    return pl.pallas_call(
        head_back_kernel,
        grid=(low.shape[0] // BLOCK,),
        out_shape=[jax.ShapeDtypeStruct((length, width), BF16), jax.ShapeDtypeStruct(low.shape, BF16)],
        in_specs=[row_block(length), line_block(length, PARTS), whole_block((1, length)), whole_block((1, length))]
        + [row_block(width), whole_block((length, width))],
        out_specs=[whole_block((length, width)), row_block(width)],
        scratch_shapes=[pltpu.VMEM((BLOCK, length), BF16), pltpu.VMEM((width, length), F32)],
        cost_estimate=cost(4 * low.size * length, 4 * low.size + 2 * exps.size),
        compiler_params=pltpu.CompilerParams(vmem_limit_bytes=48 * MEGA),
    )(exps, tops, log_norm, target, low, z)


def token_lists(ids, start, limit):
    length = ids.shape[0]
    token = jnp.arange(length, dtype=jnp.int32)
    one, two = ids[:, None], ids[None, :]
    ahead = (two < one) | ((two == one) & (token[None, :] < token[:, None]))
    place = jnp.sum(ahead.astype(jnp.int32), 1)
    at = place[:, None] == token[None, :]
    order = jnp.sum(jnp.where(at, token[:, None], 0), 0)
    ordered = jnp.sum(jnp.where(at, ids[:, None], 0), 0)
    edges = start + jnp.minimum(jnp.arange(blocks_of(limit) + 1) * BLOCK, limit)
    bounds = jnp.sum((ids[None, :] < edges[:, None]).astype(jnp.int32), 1)
    return ordered - start, order, bounds


def add_rows(total, ids_ref, order_ref, bounds_ref, grad_ref, first=0):
    at = pl.program_id(0) + first

    def step(k, carry):
        row, token = ids_ref[k] - at * BLOCK, order_ref[k]
        total[pl.ds(row, 1), :] += grad_ref[pl.ds(token, 1), :]
        return carry

    lax.fori_loop(bounds_ref[at], bounds_ref[at + 1], step, 0)


def own_rows_kernel(ids_ref, order_ref, bounds_ref, table_ref, grad_ref, out_ref, square_ref, total):
    total[...] = table_ref[...].astype(F32)
    add_rows(total, ids_ref, order_ref, bounds_ref, grad_ref)
    full = total[...]
    out_ref[...] = full.astype(BF16)

    @pl.when(pl.program_id(0) == 0)
    def _():
        square_ref[...] = jnp.zeros_like(square_ref)

    square_ref[...] += jnp.sum(full * full, 0, keepdims=True)


def add_own_rows(table, lists, grad):
    width = table.shape[1]
    return pl.pallas_call(
        own_rows_kernel,
        grid_spec=pltpu.PrefetchScalarGridSpec(
            num_scalar_prefetch=3,
            grid=(table.shape[0] // BLOCK,),
            in_specs=[row_block(width), whole_block(grad.shape)],
            out_specs=[row_block(width), whole_block((1, width))],
            scratch_shapes=[pltpu.VMEM((BLOCK, width), F32)],
        ),
        out_shape=[jax.ShapeDtypeStruct(table.shape, BF16), jax.ShapeDtypeStruct((1, width), F32)],
        cost_estimate=cost(0, 4 * table.size),
        compiler_params=pltpu.CompilerParams(vmem_limit_bytes=56 * MEGA),
    )(*lists, table, grad)


def table_sum_kernel(first, ids_ref, order_ref, bounds_ref, share_ref, *refs):
    low_ref, z_ref, log_ref, target_ref, own_ref, grad_ref, out_ref, total = refs
    steps = parts_of()
    later = mm_nt(low_ref[steps[0]], z_ref[...])
    for k, rows in enumerate(steps):
        logits = later
        if k + 1 < PARTS:
            later = mm_nt(low_ref[steps[k + 1]], z_ref[...])
        slope = slope_of(jnp.exp(logits - log_ref[...]), rows, target_ref, first)
        total[rows] = mm(slope, z_ref[...])
    add_rows(total, ids_ref, order_ref, bounds_ref, grad_ref, first)
    out_ref[...] = (share_ref[0] * own_ref[...].astype(F32) + share_ref[1] * total[...]).astype(BF16)


def table_sum(own, low, z, log_norm, target, lists, grad, shares, first, count):
    length, width = z.shape
    rows = lambda i, *_: (i + first, 0)
    return pl.pallas_call(
        functools.partial(table_sum_kernel, first),
        grid_spec=pltpu.PrefetchScalarGridSpec(
            num_scalar_prefetch=4,
            grid=(count,),
            in_specs=[pl.BlockSpec((BLOCK, width), rows), whole_block((length, width))]
            + [whole_block((1, length)), whole_block((1, length))]
            + [pl.BlockSpec((BLOCK, width), rows), whole_block(grad.shape)],
            out_specs=row_block(width),
            scratch_shapes=[pltpu.VMEM((BLOCK, width), F32)],
        ),
        out_shape=jax.ShapeDtypeStruct((count * BLOCK, width), BF16),
        cost_estimate=cost(4 * count * BLOCK * width * length, 6 * count * BLOCK * width),
        compiler_params=pltpu.CompilerParams(vmem_limit_bytes=48 * MEGA),
    )(*lists, shares, low, z, log_norm, target, own, grad)


def turned(line, height):
    return jnp.broadcast_to(line, (height, line.shape[1])).T


def gradient_kernel(limit, count, divisor, first, *refs):
    sums, (noise_ref, old_ref), outs = refs[:count], refs[count : count + 2], refs[-5:]
    grad_ref, rows_ref, cols_ref, scaled_ref, level_ref = outs
    total = sums[0][...].astype(F32)
    for item in sums[1:]:
        total = total + item[...].astype(F32)
    grad = (total + NOISE * CLIP * noise_ref[...]) * (1.0 / divisor)
    entry = lax.broadcasted_iota(jnp.int32, (ROWS, 1), 0) + (pl.program_id(0) + first) * ROWS
    inside = entry < limit
    grad_ref[...] = grad
    squares = jnp.where(inside, grad * grad, 0.0)
    mean = jnp.sum(squares, 1, keepdims=True) / grad.shape[1] + 1e-30
    old = turned(old_ref[0], 128)[:, :1]
    rows = DECAY * old + (1.0 - DECAY) * mean
    rows_ref[0] = line_of(rows)

    @pl.when(pl.program_id(0) == 0)
    def _():
        cols_ref[...] = jnp.zeros_like(cols_ref)
        scaled_ref[...] = jnp.zeros_like(scaled_ref)
        level_ref[...] = jnp.zeros_like(level_ref)

    cols_ref[...] += jnp.sum(squares, 0, keepdims=True)
    scaled_ref[...] += jnp.sum(squares * (1.0 / rows), 0, keepdims=True)
    level_ref[...] += jnp.broadcast_to(jnp.sum(jnp.where(inside, rows, 0.0), 0, keepdims=True), level_ref.shape)


def table_gradient(sums, noise, old, divisor, first, count, into=None):
    limit, width = noise.shape
    shape = jax.ShapeDtypeStruct
    rows = pl.BlockSpec((ROWS, width), lambda i: (i + first, 0))
    extra = [] if into is None else list(into)
    everything = old.shape[0]
    return pl.pallas_call(
        functools.partial(gradient_kernel, limit, len(sums), divisor, first),
        grid=(count,),
        out_shape=[shape((limit, width), F32), shape((everything, 1, ROWS), F32)]
        + [shape((1, width), F32)] * 2
        + [shape((1, 128), F32)],
        in_specs=[pl.BlockSpec((ROWS, width), lambda i: (i, 0))] * len(sums)
        + [rows, pl.BlockSpec((1, 1, ROWS), lambda i: (i + first, 0, 0))]
        + [pl.BlockSpec(memory_space=pl.ANY)] * len(extra),
        out_specs=[rows, pl.BlockSpec((1, 1, ROWS), lambda i: (i + first, 0, 0)), whole_block((1, width)), whole_block((1, width))]
        + [whole_block((1, 128))],
        input_output_aliases={len(sums) + 2: 0, len(sums) + 3: 1} if extra else {},
        cost_estimate=cost(0, (8 + 2 * len(sums)) * count * ROWS * width),
        compiler_params=pltpu.CompilerParams(vmem_limit_bytes=48 * MEGA),
    )(*sums, noise, old, *extra)


SIDE = 256


def line_of(column):
    return jnp.broadcast_to(column, (column.shape[0], 128)).T[:1]


BY_ROW = (True, True, True, True, False)


def put_line(ref, at, line):
    size = line.shape[1]
    for k in range(0, size, 128):
        ref[at : at + 1, : min(128, size - k)] = line[:, k : min(k + 128, size)]
        at += 1
    return at


def get_line(value, at, size):
    rows = [value[at + k : at + k + 1, : min(128, size - 128 * k)] for k in range(pl.cdiv(size, 128))]
    return rows[0] if len(rows) == 1 else jnp.concatenate(rows, 1)


def line_places(shapes, rows_first):
    at, places = 0, []
    for (rows, cols), along in zip(shapes, BY_ROW):
        places.append(at)
        at += pl.cdiv(rows if along == rows_first else cols, 128)
    return places, -at // 8 * -8


def join_kernel(one_ref, two_ref, after_ref, out_ref):
    out_ref[...] = (one_ref[...].astype(F32) + two_ref[...].astype(F32)).astype(BF16)


def join(one, two, after):
    return pl.pallas_call(
        join_kernel,
        out_shape=jax.ShapeDtypeStruct(one.shape, BF16),
        grid=(1,),
        in_specs=[whole_block(one.shape), whole_block(two.shape), pl.BlockSpec(memory_space=pl.ANY)],
        out_specs=whole_block(one.shape),
        cost_estimate=cost(0, 6 * one.size),
    )(one, two, after)


def small_gradients_kernel(divisor, core_ref, *refs):
    half, other_half, small, small_second, small_noise = refs[:5]
    weights, noises, grads = (refs[5 + 5 * k : 10 + 5 * k] for k in range(3))
    small_outs, (to_col, to_row, square_ref, packed) = refs[20:23], refs[23:]
    lines = half.shape[0]
    packed[pl.ds(pl.multiple_of(core_ref[0] * lines, 16), lines)] = half[...]
    packed[pl.ds(pl.multiple_of((1 - core_ref[0]) * lines, 16), lines)] = other_half[...]
    width = small.shape[1]
    scale = 1.0 / divisor
    side = weights[1].shape[0]
    cuts = (0, weights[1].shape[1], weights[1].shape[1] + weights[2].shape[1])
    for index in (1, 2, 3):
        at, end, lane_to = cuts[index - 1], cuts[index - 1] + weights[index].shape[1], 0
        while at < end:
            piece, lane = at // width, at % width
            size = min(width - lane, end - at)
            part = packed[piece * side : (piece + 1) * side, lane : lane + size].astype(F32)
            lanes = slice(lane_to, lane_to + size)
            grads[index][:, lanes] = (part + NOISE * CLIP * noises[index][:, lanes]) * scale
            at, lane_to = at + size, lane_to + size
    first = side * ((cuts[2] + weights[3].shape[1]) // width)
    down = weights[4].shape[0]
    grads[4][...] = (packed[first : first + down, :].astype(F32) + NOISE * CLIP * noises[4][...]) * scale
    first += down
    tall, wide = weights[0].shape
    grads[0][...] = (packed[first : first + tall, :wide].astype(F32) + NOISE * CLIP * noises[0][...]) * scale
    first += tall

    to_col[...] = jnp.zeros_like(to_col)
    to_row[...] = jnp.zeros_like(to_row)
    shapes = [item.shape for item in weights]
    col_places, row_places = line_places(shapes, True)[0], line_places(shapes, False)[0]
    lane = lax.broadcasted_iota(jnp.int32, (1, 128), 1)
    weight_sq = jnp.zeros((1, 128), F32)
    for index, along in enumerate(BY_ROW):
        squares = grads[index][...] * grads[index][...]
        row_sum = line_of(jnp.sum(squares, 1, keepdims=True))
        col_sum = jnp.sum(squares, 0, keepdims=True)
        put_line(to_col, col_places[index], row_sum if along else col_sum)
        put_line(to_row, row_places[index], col_sum if along else row_sum)
        total = jnp.sum(jnp.sum(weights[index][...] * weights[index][...], 0, keepdims=True), 1, keepdims=True)
        weight_sq = weight_sq + jnp.where(lane == index, total, 0.0)
    square_ref[...] = weight_sq

    count = small.shape[0]
    small_grad = (packed[first : first + 16, :].astype(F32)[:count] + NOISE * CLIP * small_noise[...]) * scale
    second_new = DECAY * small_second[...] + (1.0 - DECAY) * (small_grad * small_grad + 1e-30)
    update = small_grad * lax.rsqrt(second_new)
    mean = lambda item: jnp.sum(jnp.sum(item * item, 0, keepdims=True), 1, keepdims=True) / (count * width)
    size = RATE * jnp.maximum(1e-3, jnp.sqrt(mean(small[...])))
    size = size / jnp.maximum(1.0, jnp.sqrt(mean(update)))
    small_outs[0][...] = small_grad
    small_outs[1][...] = second_new
    small_outs[2][...] = small[...] - size * update


def small_gradients(core, half, other_half, small, small_second, small_noise, weights, noises, divisor):
    width = small.shape[1]
    matrix_shapes = [item.shape for item in weights]
    line_rows = [line_places(matrix_shapes, first)[1] for first in (True, False)]
    shape = lambda dims: jax.ShapeDtypeStruct(dims, F32)
    operands = [half, other_half, small, small_second, small_noise, *weights, *noises]
    shapes = matrix_shapes + [small.shape] * 3 + [(line_rows[0], 128), (line_rows[1], 128), (1, 128)]
    out = pl.pallas_call(
        functools.partial(small_gradients_kernel, divisor),
        grid_spec=pltpu.PrefetchScalarGridSpec(
            num_scalar_prefetch=1,
            grid=(1,),
            in_specs=[whole_block(item.shape) for item in operands],
            out_specs=[whole_block(dims) for dims in shapes],
            scratch_shapes=[pltpu.VMEM((2 * half.shape[0], width), BF16)],
        ),
        out_shape=[shape(dims) for dims in shapes],
        compiler_params=pltpu.CompilerParams(vmem_limit_bytes=56 * MEGA),
        cost_estimate=cost(0, 16 * MEGA),
    )(core, *operands)
    return out[:5], out[5:8], out[8:]


def statistics_kernel(n_row, vocab, *refs):
    table_over, over_cols, over_rows, old_lines = refs[:4]
    grads, (lines_ref, factor_ref), held = refs[4:9], refs[9:11], refs[11:16]
    to_level, both_slots, col_slots, row_slots, level_slots, send_sems, recv_sems, local_sems = refs[16:]
    n_col, width = 2, factor_ref.shape[1]
    everyone = n_row * n_col
    copies = [pltpu.make_async_copy(grads[k], held[k], local_sems.at[k]) for k in range(5)]
    for copy in copies:
        copy.start()
    link = Link(send_sems, recv_sems)
    me, peers = link.plane_peers(n_row)
    link.greet([(device, None) for _, device in peers])
    row_peers = [((link.row + k) % n_row, link.device(row=(link.row + k) % n_row)) for k in range(1, n_row)]
    meet(
        link,
        (0, table_over, both_slots, me, peers),
        (everyone, over_cols, col_slots, link.col, [(1 - link.col, link.device(col=1 - link.col))]),
        (everyone + n_col, over_rows, row_slots, link.row, row_peers),
    )
    both, over_col, over_row = added(both_slots), added(col_slots), added(row_slots)
    for copy in copies:
        copy.wait()

    lane = lax.broadcasted_iota(jnp.int32, (1, 128), 1)
    whole = lambda line: jnp.sum(line, 1, keepdims=True)
    lines = width // 128
    cols_new = DECAY * old_lines[5:6, :width] + (1.0 - DECAY) * (get_line(both, 0, width) / vocab + 1e-30)
    weight_sums, table_level = both[2 * lines : 2 * lines + 1], both[2 * lines + 1 : 2 * lines + 2, :1]
    everywhere = jnp.where(lane == 5, whole(get_line(both, lines, width) / cols_new), 0.0)
    counts = jnp.full((1, 128), float(vocab * width), F32)
    for index in range(5):
        counts = jnp.where(lane == index, float(held[index].shape[0] * held[index].shape[1] * everyone), counts)
    factor_ref[...] = jnp.zeros_like(factor_ref)
    factor_ref[0:1] = cols_new
    factor_ref[1:2] = lax.rsqrt(cols_new)

    lines_ref[...] = jnp.zeros_like(lines_ref)
    shapes = [item.shape for item in held]
    col_places, row_places = line_places(shapes, True)[0], line_places(shapes, False)[0]
    levels = jnp.where(lane == 5, table_level / (vocab * everyone), 0.0)
    scaled_sums = jnp.zeros((1, 128), F32)
    for index, along in enumerate(BY_ROW):
        rows, cols = held[index].shape
        parts_rows, parts_cols = (n_row, n_col) if along else (n_col, n_row)
        by_col = get_line(over_col, col_places[index], rows if along else cols)
        by_line = get_line(over_row, row_places[index], cols if along else rows)
        row_mean = (by_col if along else by_line) / (cols * parts_cols) + 1e-30
        col_mean = (by_line if along else by_col) / (rows * parts_rows) + 1e-30
        rows_line = DECAY * old_lines[index : index + 1, :rows] + (1.0 - DECAY) * row_mean
        cols_line = DECAY * old_lines[8 + index : 9 + index, :cols] + (1.0 - DECAY) * col_mean
        lines_ref[index : index + 1, :rows] = rows_line
        lines_ref[8 + index : 9 + index, :cols] = cols_line
        level = whole(rows_line) / (rows * parts_rows * parts_cols)
        scaled = held[index][...] * held[index][...] * (1.0 / turned(rows_line, 128)[:, :1])
        scaled = whole(jnp.sum(scaled, 0, keepdims=True) / cols_line)
        levels = jnp.where(lane == index, level, levels)
        scaled_sums = jnp.where(lane == index, scaled, scaled_sums)
    to_level[...] = jnp.zeros_like(to_level)
    to_level[0:1] = levels
    to_level[1:2] = scaled_sums
    meet(link, (everyone + n_col + n_row, to_level, level_slots, me, peers))
    levels = added(level_slots)
    level, square_sum = levels[0:1], levels[1:2] + everywhere
    size = RATE * jnp.maximum(1e-3, jnp.sqrt(weight_sums / counts))
    size = size / jnp.maximum(1.0, jnp.sqrt(square_sum * level / counts))
    sizes = size * jnp.sqrt(level)
    factor_ref[2:3, :128] = sizes
    link.finish()


def statistics(table_over, over_cols, over_rows, old_lines, grads, width, n_row, vocab, collective_id):
    wide = old_lines.shape[1]
    everyone = 2 * n_row
    vmem, hbm = pl.BlockSpec(memory_space=pltpu.VMEM), pl.BlockSpec(memory_space=pl.ANY)
    return pl.pallas_call(
        functools.partial(statistics_kernel, n_row, vocab),
        out_shape=[jax.ShapeDtypeStruct((16, wide), F32), jax.ShapeDtypeStruct((8, width), F32)],
        in_specs=[vmem] * 4 + [hbm] * 5,
        out_specs=[vmem] * 2,
        scratch_shapes=[pltpu.VMEM(item.shape, F32) for item in grads]
        + [pltpu.VMEM((8, 128), F32), pltpu.VMEM((everyone,) + table_over.shape, F32)]
        + [pltpu.VMEM((2,) + over_cols.shape, F32), pltpu.VMEM((n_row,) + over_rows.shape, F32)]
        + [pltpu.VMEM((everyone, 8, 128), F32)]
        + [pltpu.SemaphoreType.DMA((3 * everyone,)), pltpu.SemaphoreType.DMA((2 * everyone + 2 + n_row,))]
        + [pltpu.SemaphoreType.DMA((5,))],
        compiler_params=pltpu.CompilerParams(
            collective_id=collective_id, has_side_effects=True, vmem_limit_bytes=58 * MEGA
        ),
    )(table_over, over_cols, over_rows, old_lines, *grads)


def update_kernel(table_ref, table_grad_ref, rows_ref, all_rows_ref, factor_ref, lines_ref, *refs):
    weights, grads, (table_new_ref, table_rows_ref, table_cols_ref) = refs[:5], refs[5:10], refs[10:13]
    rows_outs, cols_outs, news = refs[13:18], refs[18:23], refs[23:28]
    held_weights, held_grads, (load_sems, store_sems) = refs[28:33], refs[33:38], refs[38:]
    at, last = pl.program_id(0), pl.num_programs(0) - 1
    loads = [
        pltpu.make_async_copy(source, target, load_sems.at[k])
        for k, (source, target) in enumerate(zip(weights + grads, held_weights + held_grads))
    ]
    stores = [pltpu.make_async_copy(held_weights[k], news[k], store_sems.at[k]) for k in range(5)]

    @pl.when(at == 0)
    def _():
        for load in loads:
            load.start()
        limit = table_rows_ref.shape[0]
        line = jnp.concatenate([all_rows_ref[k] for k in range(all_rows_ref.shape[0])], 1)
        table_rows_ref[...] = line[:, :limit].reshape(limit)
        table_cols_ref[...] = factor_ref[0:1].reshape(table_cols_ref.shape)

    factors = factor_ref[1:2] * factor_ref[2:3, 5:6]
    for k in range(BLOCK // ROWS):
        part = slice(k * ROWS, (k + 1) * ROWS)
        rows = turned(lax.rsqrt(rows_ref[k]), 128)[:, :1]
        table_new_ref[part] = table_ref[part] - table_grad_ref[part] * rows * factors

    @pl.when(at == last - 1)
    def _():
        for load in loads:
            load.wait()
        for index in range(5):
            count_rows, count_cols = held_weights[index].shape
            rows_line = lines_ref[index : index + 1, :count_rows]
            cols_line = lines_ref[8 + index : 9 + index, :count_cols]
            rows_outs[index][...] = rows_line.reshape(count_rows)
            cols_outs[index][...] = cols_line.reshape(count_cols)
            rows = turned(lax.rsqrt(rows_line), 128)[:, :1]
            factors = factor_ref[2:3, index : index + 1] * lax.rsqrt(cols_line)
            held_weights[index][...] = held_weights[index][...] - held_grads[index][...] * rows * factors
            stores[index].start()

    @pl.when(at == last)
    def _():
        for store in stores:
            store.wait()


def update(table, table_grad, table_rows, factors, lines, weights, grads):
    limit, width = table.shape
    shape = lambda dims: jax.ShapeDtypeStruct(dims, F32)
    small_shapes = [(limit,), (width,)] + [item.shape[:1] for item in weights] + [item.shape[1:] for item in weights]
    matrix_shapes = [item.shape for item in weights]
    hbm = pl.BlockSpec(memory_space=pl.ANY)
    out = pl.pallas_call(
        update_kernel,
        grid=(blocks_of(limit),),
        out_shape=[shape(table.shape)] + [shape(dims) for dims in small_shapes + matrix_shapes],
        in_specs=[row_block(width), row_block(width), line_block(ROWS, BLOCK // ROWS), whole_block(table_rows.shape)]
        + [whole_block(factors.shape), whole_block(lines.shape)]
        + [hbm] * 10,
        out_specs=[row_block(width)] + [whole_block(dims) for dims in small_shapes] + [hbm] * 5,
        scratch_shapes=[pltpu.VMEM(dims, F32) for dims in matrix_shapes * 2]
        + [pltpu.SemaphoreType.DMA((10,)), pltpu.SemaphoreType.DMA((5,))],
        compiler_params=pltpu.CompilerParams(vmem_limit_bytes=58 * MEGA),
        cost_estimate=cost(0, 3 * 4 * limit * width),
    )(table, table_grad, table_rows, table_rows, factors, lines, *weights, *grads)
    return out[0], out[1], out[2], out[3:8], out[8:13], out[13:]


HIDDEN = 1024
CHUNK = 512


def normed_of(inputs):
    center = jnp.mean(inputs, -1, keepdims=True)
    var = jnp.mean(inputs * inputs, -1, keepdims=True) - center * center
    inv = lax.rsqrt(var + 1e-05)
    return (inputs - center) * inv, inv


def normed_back(upstream, normed, inv, gain):
    scaled = upstream * gain
    first = jnp.mean(scaled, -1, keepdims=True)
    second = jnp.mean(scaled * normed, -1, keepdims=True)
    return inv * (scaled - first - normed * second)


def columns_sum(item):
    return jnp.sum(item.astype(F32), 0, keepdims=True)


def chunks_of(length):
    return [slice(at, at + CHUNK) for at in range(0, length, CHUNK)]


GELU_SCALE = (2.0 / jnp.pi) ** 0.5


def gelu_parts(inputs):
    square = inputs * inputs
    turn = jnp.tanh(inputs * (GELU_SCALE + (GELU_SCALE * 0.044715) * square))
    half = 0.5 + 0.5 * turn
    inner = GELU_SCALE + (3.0 * GELU_SCALE * 0.044715) * square
    return inputs * half, half + 0.5 * inputs * (1.0 - turn * turn) * inner


def middle_kernel(start_ref, mixed_ref, attn_ref, up_ref, bias_ref, down_ref, small_ref, *outs):
    mid_ref, low_ref, out_ref, z_ref, total = outs
    at = pl.program_id(0)
    length = start_ref.shape[0]

    @pl.when(at == 0)
    def _():
        for rows in chunks_of(length):
            mid = start_ref[rows].astype(F32) + mm(mixed_ref[rows], attn_ref[...]) + small_ref[4:5]
            mid_ref[rows] = mid
            low_ref[rows] = (normed_of(mid)[0] * small_ref[5:6] + small_ref[6:7]).astype(BF16)
            total[rows] = mid + small_ref[11:12]

    chunks = chunks_of(length)
    later = mm(low_ref[chunks[0]], up_ref[...])
    for k, rows in enumerate(chunks):
        product = later
        if k + 1 < len(chunks):
            later = mm(low_ref[chunks[k + 1]], up_ref[...])
        hidden = gelu_parts(product + bias_ref[...])[0].astype(BF16)
        total[rows] += mm_nt(hidden, down_ref[...])

    @pl.when(at == pl.num_programs(0) - 1)
    def _():
        for rows in chunks_of(length):
            out = total[rows]
            out_ref[rows] = out
            z_ref[rows] = (normed_of(out)[0] * small_ref[12:13] + small_ref[13:14]).astype(BF16)


def middle_forward(start, mixed, attn, up, up_bias, down, small):
    length, width = start.shape
    shape = jax.ShapeDtypeStruct
    whole = lambda item: whole_block(item.shape)
    tokens = whole_block((length, width))
    return pl.pallas_call(
        middle_kernel,
        grid=(up.shape[1] // HIDDEN,),
        out_shape=[shape((length, width), kind) for kind in (F32, BF16, F32, BF16)],
        in_specs=[whole(start), whole(mixed), whole(attn), pl.BlockSpec((width, HIDDEN), lambda i: (0, i))]
        + [pl.BlockSpec((1, HIDDEN), lambda i: (0, i)), pl.BlockSpec((width, HIDDEN), lambda i: (0, i))]
        + [whole(small)],
        out_specs=[tokens] * 4,
        scratch_shapes=[pltpu.VMEM((length, width), F32)],
        cost_estimate=cost(4 * length * width * up.shape[1], 16 * length * width),
        compiler_params=pltpu.CompilerParams(vmem_limit_bytes=56 * MEGA),
    )(start, mixed, attn, up, up_bias, down, small)


def middle_back_kernel(*refs):
    grad_ref, out_ref, mid_ref, low_ref, attn_ref, up_ref, bias_ref, down_ref, small_ref = refs[:9]
    down_grad_ref, pre_ref, act_ref, pre_sum_ref, mid_grad_ref, branch_ref, mixed_ref, rows_ref, total = refs[9:]
    at = pl.program_id(0)
    length, width = grad_ref.shape

    @pl.when(at == 0)
    def _():
        rows_ref[...] = jnp.zeros_like(rows_ref)
        for rows in chunks_of(length):
            grad = grad_ref[rows].astype(F32)
            normed, inv = normed_of(out_ref[rows])
            back = normed_back(grad, normed, inv, small_ref[12:13])
            mid_grad_ref[rows] = back
            low = back.astype(BF16)
            down_grad_ref[rows] = low
            rows_ref[0:1] += columns_sum(grad * normed)
            rows_ref[1:2] += columns_sum(grad)
            rows_ref[2:3] += columns_sum(low)
        total[...] = jnp.zeros_like(total)

    pre_sum = jnp.zeros((1, pre_ref.shape[1]), F32)
    for rows in chunks_of(length):
        act, slope = gelu_parts(mm(low_ref[rows], up_ref[...]) + bias_ref[...])
        act_ref[rows] = act.astype(BF16)
        pre = (mm(down_grad_ref[rows], down_ref[...]) * slope).astype(BF16)
        pre_ref[rows] = pre
        pre_sum = pre_sum + columns_sum(pre)
        total[rows] += mm_nt(pre, up_ref[...])
    pre_sum_ref[...] = pre_sum

    @pl.when(at == pl.num_programs(0) - 1)
    def _():
        for rows in chunks_of(length):
            grad = total[rows]
            normed, inv = normed_of(mid_ref[rows])
            mid_grad = mid_grad_ref[rows] + normed_back(grad, normed, inv, small_ref[5:6])
            mid_grad_ref[rows] = mid_grad
            low = mid_grad.astype(BF16)
            branch_ref[rows] = low
            rows_ref[3:4] += columns_sum(grad * normed)
            rows_ref[4:5] += columns_sum(grad)
            rows_ref[5:6] += columns_sum(low)
            mixed_ref[rows] = mm_nt(low, attn_ref[...]).astype(BF16)


def middle_back(grad, out, mid, low, attn, up, up_bias, down, small):
    length, width = grad.shape
    hidden = up.shape[1]
    shape = jax.ShapeDtypeStruct
    whole = lambda item: whole_block(item.shape)
    tokens = whole_block((length, width))
    wide = pl.BlockSpec((length, HIDDEN), lambda i: (0, i))
    weight = pl.BlockSpec((width, HIDDEN), lambda i: (0, i))
    line = pl.BlockSpec((1, HIDDEN), lambda i: (0, i))
    return pl.pallas_call(
        middle_back_kernel,
        grid=(hidden // HIDDEN,),
        out_shape=[shape((length, width), BF16), shape((length, hidden), BF16), shape((length, hidden), BF16)]
        + [shape((1, hidden), F32), shape((length, width), F32), shape((length, width), BF16)]
        + [shape((length, width), BF16), shape((8, width), F32)],
        in_specs=[tokens] * 4 + [whole(attn), weight, line, weight, whole(small)],
        out_specs=[tokens, wide, wide, line, tokens, tokens, tokens, whole_block((8, width))],
        scratch_shapes=[pltpu.VMEM((length, width), F32)],
        cost_estimate=cost(6 * length * width * hidden, 40 * length * width),
        compiler_params=pltpu.CompilerParams(vmem_limit_bytes=58 * MEGA),
    )(grad, out, mid, low, attn, up, up_bias, down, small)


def start_back_kernel(packed_ref, weight_ref, mid_grad_ref, start_ref, small_ref, out_ref, low_ref, wide_ref, rows_ref):
    width = start_ref.shape[1]
    grad = sum(mm_nt(packed_ref[k], weight_ref[:, k * width : (k + 1) * width]) for k in range(3))
    normed, inv = normed_of(start_ref[...].astype(F32))
    back = mid_grad_ref[...] + normed_back(grad, normed, inv, small_ref[0:1])
    out_ref[...] = back
    low_ref[...] = back.astype(BF16)
    wide_ref[...] = back.astype(BF16).astype(F32)

    @pl.when(pl.program_id(0) == 0)
    def _():
        rows_ref[...] = jnp.zeros_like(rows_ref)

    rows_ref[0:1] += columns_sum(grad * normed)
    rows_ref[1:2] += columns_sum(grad)
    rows_ref[2:3] += columns_sum(packed_ref[0])
    rows_ref[3:4] += columns_sum(packed_ref[2])
    rows_ref[4:5] += columns_sum(back * back)


def start_back(packed_grad, weight, mid_grad, start, small):
    length, width = start.shape
    shape = jax.ShapeDtypeStruct
    tokens = pl.BlockSpec((CHUNK, width), lambda i: (i, 0))
    return pl.pallas_call(
        start_back_kernel,
        grid=(length // CHUNK,),
        out_shape=[shape((length, width), kind) for kind in (F32, BF16, F32)] + [shape((8, width), F32)],
        in_specs=[pl.BlockSpec((3, CHUNK, width), lambda i: (0, i, 0)), whole_block(weight.shape), tokens, tokens]
        + [whole_block(small.shape)],
        out_specs=[tokens, tokens, tokens, whole_block((8, width))],
        cost_estimate=cost(6 * length * width * width, 20 * length * width),
        compiler_params=pltpu.CompilerParams(vmem_limit_bytes=56 * MEGA),
    )(packed_grad, weight, mid_grad, start, small)


def weight_grads_kernel(place_ref, ones_ref, mixed_ref, low_ref, *refs):
    packed, (branch_ref, pre_ref, down_ref, act_ref, grad_ref, small_ref) = refs[:3], refs[3:9]
    out_ref, square_ref, wide, turned_grad = refs[9:]
    width = ones_ref.shape[1]
    tall = width // 4
    start = pl.multiple_of(place_ref[0], 128)
    skip = pl.multiple_of(place_ref[1], 8)
    pieces = (
        (ones_ref, ((packed[0], 0, 0), (packed[1], 0, 1), (packed[2], 1, 0))),
        (mixed_ref, ((branch_ref, 1, 1),)),
        (low_ref, ((pre_ref, 2, 0), (pre_ref, 2, 1), (pre_ref, 3, 0), (pre_ref, 3, 1))),
    )
    half = width // 2
    square = jnp.zeros((1, half), F32)
    for left_ref, rights in pieces:
        left = left_ref[:, pl.ds(start, SIDE)].T
        for k, (right_ref, piece, side) in enumerate(rights):
            right = right_ref[0] if len(right_ref.shape) == 3 else right_ref[:, pl.ds(k * half, half)]
            wide[...] = mm(left, right)
            grad = wide[pl.ds(skip, tall), :]
            out_ref[piece * tall : (piece + 1) * tall, side * half : (side + 1) * half] = grad
            square = square + jnp.sum(grad * grad, 0, keepdims=True)
    left = down_ref[...].T
    first = 4 * tall
    for side in range(2):
        grad = mm(left, act_ref[:, side * half : (side + 1) * half])
        out_ref[first : first + half, side * half : (side + 1) * half] = grad
        square = square + jnp.sum(grad * grad, 0, keepdims=True)
    square_ref[...] = square
    first += half
    turned_grad[...] = grad_ref[:, pl.ds(start, SIDE)].T
    out_ref[first:, :] = jnp.zeros((out_ref.shape[0] - first, width), F32)
    out_ref[first : first + tall, : grad_ref.shape[0]] = turned_grad[pl.ds(skip, tall), :]
    first += tall
    out_ref[first : first + small_ref.shape[0], :] = small_ref[...]


def weight_grads(ln_one, mixed, low, packed_grad, branch, pre, down_grad, act, grad_in, small_ex, row_at, col_at):
    length, width = ln_one.shape
    half, tall = width // 2, width // 4
    hidden, tokens = pre.shape[1] // 2, length // 2
    shape = jax.ShapeDtypeStruct
    first = row_at * tall
    place = jnp.stack([first // 128 * 128, first % 128, row_at, col_at]).astype(jnp.int32)
    unit = lambda k: pl.BlockSpec((1, length, half), lambda i, at: ((3 * at[3] + k) // 2, 0, (3 * at[3] + k) % 2))
    by_col = lambda size: pl.BlockSpec((length, size), lambda i, at: (0, at[3]))
    lines = 5 * tall + half + 32
    return pl.pallas_call(
        weight_grads_kernel,
        grid_spec=pltpu.PrefetchScalarGridSpec(
            num_scalar_prefetch=1,
            grid=(1,),
            in_specs=[whole_block((length, width))] * 3
            + [unit(k) for k in range(3)]
            + [by_col(half), by_col(hidden), by_col(half), pl.BlockSpec((length, width), lambda i, at: (0, at[2]))]
            + [pl.BlockSpec((tokens, width), lambda i, at: (at[3], 0)), whole_block(small_ex.shape)],
            out_specs=[whole_block((lines, width)), whole_block((1, half))],
            scratch_shapes=[pltpu.VMEM((SIDE, half), F32), pltpu.VMEM((SIDE, tokens), F32)],
        ),
        out_shape=[shape((lines, width), F32), shape((1, half), F32)],
        cost_estimate=cost(2 * length * width * width * 2, 16 * length * width),
        compiler_params=pltpu.CompilerParams(vmem_limit_bytes=56 * MEGA),
    )(place, ln_one, mixed, low, packed_grad, packed_grad, packed_grad, branch, pre, down_grad, act, grad_in, small_ex)


def body(
    token_ids,
    target_ids,
    included,
    tok_table,
    pos_table,
    qkv_weight,
    attn_weight,
    up_weight,
    down_weight,
    small_params,
    table_rows,
    table_cols,
    pos_rows,
    pos_cols,
    qkv_rows,
    qkv_cols,
    attn_rows,
    attn_cols,
    up_rows,
    up_cols,
    down_rows,
    down_cols,
    small_second,
    table_noise,
    pos_noise,
    qkv_noise,
    attn_noise,
    up_noise,
    down_noise,
    small_noise,
):
    n_row = lax.axis_size("row")
    n_col = lax.axis_size("col")
    n_data = lax.axis_size("dp")
    row_at = lax.axis_index("row")
    col_at = lax.axis_index("col")
    ids, targets = token_ids[0], target_ids[0]
    length = ids.shape[0]
    width = small_params.shape[1]
    vocab_here = tok_table.shape[0]
    vocab_start = (col_at * n_row + row_at) * vocab_here
    small = small_params

    target = targets - vocab_start
    target = jnp.where((target >= 0) & (target < vocab_here), target, -1)[None]
    lists = token_lists(ids, vocab_start, vocab_here)
    tuned = (n_data, n_row, n_col) == (4, 4, 2)
    block = length // (n_row * n_col)
    if tuned:
        beside = lambda item: lax.ppermute(item, "dp", [(at, at ^ 2) for at in range(4)])
        met_ids, met_target = beside(jnp.stack([ids, targets]))
        met_target = met_target - vocab_start
        met_target = jnp.where((met_target >= 0) & (met_target < vocab_here), met_target, -1)[None]
        met_lists = token_lists(met_ids, vocab_start, vocab_here)

    weights_in = [tok_table, pos_table, qkv_weight, attn_weight, up_weight, down_weight]
    noises = [table_noise, pos_noise, qkv_noise, attn_noise, up_noise, down_noise]
    lows = [item.astype(BF16) for item in weights_in[2:]]
    if tuned:
        shards = [item.reshape(n_data, -1, item.shape[1]) for item in lows]
        start, table_low, table_sq, qkv_full, attn_full, up_full, down_full = front(
            ids, tok_table, pos_table.T, shards, n_row
        )
        stream_in = start.reshape(length, width)
        qkv_full, attn_full, up_full, down_full = (
            item.reshape(width, -1) for item in (qkv_full, attn_full, up_full, down_full)
        )
    else:
        local_ids = ids - vocab_start
        inside = (local_ids >= 0) & (local_ids < vocab_here)
        safe_ids = jnp.clip(local_ids, 0, vocab_here - 1)
        looked = jnp.where(inside[:, None], jnp.take(tok_table, safe_ids, axis=0), 0.0).astype(BF16)
        table_sq = jnp.sum(tok_table * tok_table, 0, keepdims=True)
        table_low = jnp.pad(tok_table.astype(BF16), ((0, blocks_of(vocab_here) * BLOCK - vocab_here), (0, 0)))
        stream_in = (plane_sum(looked).astype(F32) + gather_matrix(pos_table, 1)).astype(BF16)
        qkv_full, attn_full, up_full = (gather_matrix(item, 0) for item in lows[:3])
        down_full = gather_matrix(lows[3], 1)

    ln_one = (normed_of(stream_in.astype(F32))[0] * small[0] + small[1]).astype(BF16)
    bias = jnp.concatenate([small[2], jnp.zeros_like(small[2]), small[3]])
    packed = (mm(ln_one, qkv_full) + bias).astype(BF16)
    mixed, attn_log = attend(packed)
    up_bias = small[7:11].reshape(1, -1)
    stream_mid, ln_two, stream_out, ln_fin = middle_forward(
        stream_in, mixed, attn_full, up_full, up_bias, down_full, small
    )

    exps, tops, exp_sums, picked = head(table_low, vocab_here, ln_fin, target)
    if tuned:
        met_z = beside(ln_fin)
        log_norm, picked = log_total(tops, exp_sums, picked, n_row, 3)
        met_log = beside(log_norm)
    else:
        top = lax.pmax(jnp.max(tops, 0), PLANE)
        log_norm = top + jnp.log(plane_sum(jnp.sum(exp_sums * jnp.exp(tops - top[None]), 0)))
        picked = plane_sum(picked)
    loss = jnp.sum(log_norm - picked)
    final_part, table_ex = head_back(exps, tops, log_norm, target, table_low, ln_fin)
    if tuned:
        final_part = plane_total(final_part.reshape(n_col, n_row, block, width), 2)
        final_grad = final_part.reshape(length, width)
    else:
        final_grad = plane_sum(final_part)

    down_grad, pre_grad, up_act, pre_sum, mid_grad, branch_grad, mixed_grad, mid_rows = middle_back(
        final_grad, stream_out, stream_mid, ln_two, attn_full, up_full, up_bias, down_full, small
    )
    packed_grad = attend_back(packed, mixed_grad, attn_log)
    grad_in, emb_low, emb_grad, start_rows = start_back(packed_grad, qkv_full, mid_grad, stream_in, small)
    small_ex = jnp.concatenate(
        [start_rows[:4], mid_rows[5:6], mid_rows[3:5], pre_sum.reshape(-1, width), mid_rows[2:3], mid_rows[:2]], 0
    )
    if tuned:
        met_grad = beside(emb_low)
        packed_ex, layer_sq = weight_grads(
            ln_one,
            mixed,
            ln_two,
            packed_grad,
            branch_grad,
            pre_grad,
            down_grad,
            up_act,
            grad_in,
            small_ex,
            row_at,
            col_at,
        )
        layer_sq = jnp.sum(layer_sq)
    else:
        tok_here, dim_here = pos_table.shape
        pos_ex = lax.dynamic_slice(grad_in, (col_at * tok_here, row_at * dim_here), (tok_here, dim_here))
        all_grads = packed_grad.transpose(1, 0, 2).reshape(length, -1)

        def columns_of(array, at, parts):
            size = array.shape[1] // parts
            return lax.dynamic_slice_in_dim(array, at * size, size, 1)

        layer_ex = [
            mm_tn(columns_of(left, at_left, n_left), columns_of(right, at_right, n_right))
            for left, at_left, n_left, right, at_right, n_right in (
                (ln_one, row_at, n_row, all_grads, col_at, n_col),
                (mixed, row_at, n_row, branch_grad, col_at, n_col),
                (ln_two, row_at, n_row, pre_grad, col_at, n_col),
                (down_grad, col_at, n_col, up_act, row_at, n_row),
            )
        ]
        layer_sq = sum(jnp.sum(item * item) for item in layer_ex)
    table_ex, own_sq = add_own_rows(table_ex, lists, emb_grad)

    own_sq = jnp.sum(own_sq) + layer_sq
    same_sq = jnp.sum(start_rows[4]) + jnp.sum(small_ex * small_ex)
    taken = included[0].astype(F32)
    ex_at = lax.axis_index("dp")
    leads = (row_at + col_at == 0).astype(F32)
    at_own = (jnp.arange(n_data) == ex_at).astype(F32)
    total = jnp.concatenate([at_own * (own_sq + leads * same_sq), at_own * leads * taken, leads * taken * loss[None]])
    if tuned:
        total = jnp.pad(total, (0, 1024 - total.shape[0])).reshape(8, 128)
        total, met_grad = lax.optimization_barrier((total, met_grad))
        total = sum_small(total, n_row, 4).reshape(-1)
    else:
        total = lax.psum(lax.psum(total, PLANE), "dp")
    norm_sq, taken, loss_sum = total[:n_data], total[n_data : 2 * n_data], total[2 * n_data]
    share = taken * jnp.minimum(1.0, CLIP * lax.rsqrt(norm_sq + 1e-12))
    example_norm = jnp.sqrt(norm_sq[ex_at])
    own_share = share[ex_at]

    divisor = SAMPLE * n_data
    vocab = vocab_here * n_row * n_col
    count = blocks_of(vocab_here)
    table_old = jnp.pad(table_rows, (0, count * BLOCK - vocab_here), constant_values=1.0).reshape(-1, 1, ROWS)
    fine = BLOCK // ROWS
    olds = [(pos_rows, pos_cols), (qkv_rows, qkv_cols), (attn_rows, attn_cols), (up_rows, up_cols)]
    olds.append((down_rows, down_cols))
    ends = (token_ids.shape[1] * jnp.sum(taken), example_norm[None])
    if tuned:
        core = ex_at % 2
        to_core = lambda item: lax.ppermute(item, "dp", [(at, at ^ 1) for at in range(4)])
        halves = (own_share * packed_ex).astype(BF16).reshape(2, -1, width)
        half = (halves[core].astype(F32) + to_core(halves[1 - core]).astype(F32)).astype(BF16)
        shares = jnp.stack([own_share, share[ex_at ^ 2]])
        half, shares = lax.optimization_barrier((half, shares))
        from_beside = beside(half)
        middle = count // 2
        spans = [(0, middle), (middle, count - middle)]
        met = (met_z, met_log, met_target, met_lists, met_grad.astype(F32), shares)
        pair_sums = [table_sum(table_ex, table_low, *met, *span) for span in spans]
        pair_sums = [[item, to_core(item)] for item in pair_sums]
        into, over = None, []
        for pair, span in zip(pair_sums, spans):
            *into, cols, scaled, level = table_gradient(
                pair, table_noise, table_old, divisor, span[0] * fine, span[1] * fine, into
            )
            over.append((cols, scaled, level))
        table_grad, rows_blocks = into
        half = join(half, from_beside, cols)
        other_half = to_core(half)
        cols, scaled, level = (over[0][k] + over[1][k] for k in range(3))
        turn = lambda items: [items[1].T] + list(items[2:])
        matrices, matrix_noises = turn(weights_in), turn(noises)
        olds[0] = olds[0][::-1]
        small_grads, smalls, (over_cols, over_rows, squares) = small_gradients(
            core[None], half, other_half, small_params, small_second, small_noise, matrices, matrix_noises, divisor
        )
        scalars = jnp.where(jnp.arange(128) == 5, jnp.sum(table_sq), squares[0])
        table_over = jnp.concatenate([cols[0], scaled[0], scalars, level[0]]).reshape(-1, 128)
        table_over = jnp.pad(table_over, ((0, -table_over.shape[0] % 8), (0, 0)))
        wide = max(item.shape[0] for pair in olds for item in pair)
        lines = [jnp.pad(item, (0, wide - item.shape[0])) for pair in zip(*olds) for item in pair + (table_cols,) * 3]
        old_lines = jnp.stack(lines)
        lines, factors = statistics(
            table_over, over_cols, over_rows, old_lines, small_grads, width, n_row, vocab, 5
        )
        table_new, table_rows_new, table_cols_new, rows_new, cols_new, news = update(
            tok_table, table_grad, rows_blocks, factors, lines, matrices, small_grads
        )
        outputs = [table_grad, table_rows_new, table_cols_new, table_new]
        outputs.extend([small_grads[0].T, cols_new[0], rows_new[0], news[0].T])
        for group in zip(small_grads[1:], rows_new[1:], cols_new[1:], news[1:]):
            outputs.extend(group)
        return tuple(outputs) + tuple(smalls) + (loss_sum,) + ends

    weight_total = plane_sum(
        jnp.stack([jnp.sum(table_sq)] + [jnp.sum(item * item) for item in weights_in[1:]])
    )
    table_sum_all = example_sum((own_share * table_ex.astype(F32)).astype(BF16))
    others = [(own_share * item).astype(BF16) for item in [pos_ex] + layer_ex + [small_ex]]
    sums = [example_sum(item).astype(F32) for item in others]
    grads = [(sums[index] + NOISE * CLIP * noises[index + 1]) / divisor for index in range(5)]
    table_grad, table_rows_new, *table_over = table_gradient(
        [table_sum_all], table_noise, table_old, divisor, 0, pl.cdiv(vocab_here, ROWS)
    )
    table_rows_new = table_rows_new.reshape(-1)[:vocab_here]
    by_row = [False, True, True, True, False]
    over = {"col": [], "row": []}
    for grad, first in zip(grads, by_row):
        squares = grad * grad + 1e-30
        over["col" if first else "row"].append(jnp.sum(squares, 1))
        over["row" if first else "col"].append(jnp.sum(squares, 0))
    over = {axis: [lax.psum(item, axis) for item in items] for axis, items in over.items()}
    table_over = [plane_sum(item[0]) for item in table_over]
    news, levels = [], []
    for index, (grad, first) in enumerate(zip(grads, by_row)):
        rows_parts, cols_parts = (n_row, n_col) if first else (n_col, n_row)
        row_sum = over["col" if first else "row"][index]
        col_sum = over["row" if first else "col"][index]
        rows_new = DECAY * olds[index][0] + (1.0 - DECAY) * (row_sum / (grad.shape[1] * cols_parts))
        cols_new = DECAY * olds[index][1] + (1.0 - DECAY) * (col_sum / (grad.shape[0] * rows_parts))
        news.append((rows_new, cols_new))
        levels += [
            jnp.sum(rows_new) / (grad.shape[0] * rows_parts * cols_parts),
            jnp.sum(grad * grad / (rows_new[:, None] * cols_new[None, :])),
        ]
    levels = plane_sum(jnp.stack(levels))

    def updated(index, weight, grad, rows_new, cols_new, level, square_sum, entries_all):
        size = RATE * jnp.maximum(1e-3, jnp.sqrt(weight_total[index] / entries_all))
        size = size / jnp.maximum(1.0, jnp.sqrt(square_sum * level / entries_all))
        size = size * jnp.sqrt(level)
        return weight - grad * lax.rsqrt(rows_new)[:, None] * (size * lax.rsqrt(cols_new))[None, :]

    table_cols_new = DECAY * table_cols + (1.0 - DECAY) * (table_over[0] / vocab + 1e-30)
    table_new = updated(
        0,
        tok_table,
        table_grad,
        table_rows_new,
        table_cols_new,
        table_over[2][0] / vocab,
        jnp.sum(table_over[1] / table_cols_new),
        vocab * width,
    )
    outputs = [table_grad, table_rows_new, table_cols_new, table_new]
    for index, grad in enumerate(grads):
        rows_new, cols_new = news[index]
        weight_new = updated(
            index + 1,
            weights_in[index + 1],
            grad,
            rows_new,
            cols_new,
            levels[2 * index],
            levels[2 * index + 1],
            grad.shape[0] * grad.shape[1] * n_row * n_col,
        )
        outputs.extend([grad, rows_new, cols_new, weight_new])
    small_grad = (sums[5] + NOISE * CLIP * small_noise) / divisor
    second_new = DECAY * small_second + (1.0 - DECAY) * (small_grad * small_grad + 1e-30)
    small_update = small_grad * lax.rsqrt(second_new)
    small_update = small_update / jnp.maximum(1.0, jnp.sqrt(jnp.mean(small_update * small_update)))
    small_size = RATE * jnp.maximum(1e-3, jnp.sqrt(jnp.mean(small_params * small_params)))
    small_new = small_params - small_size * small_update
    return tuple(outputs) + (small_grad, second_new, small_new, loss_sum) + ends


def solution(mesh):
    table, by_col, by_row = P(("col", "row"), None), P("col", "row"), P("row", "col")
    return jax.shard_map(
        body,
        mesh=mesh,
        in_specs=(P("dp", None), P("dp", None), P("dp"))
        + (table, by_col, by_row, by_row, by_row, by_col, P())
        + (P(("col", "row")), P(), P("col"), P("row"))
        + (P("row"), P("col")) * 3
        + (P("col"), P("row"), P())
        + (table, by_col, by_row, by_row, by_row, by_col, P()),
        out_specs=(table, P(("col", "row")), P(), table)
        + (by_col, P("col"), P("row"), by_col)
        + (by_row, P("row"), P("col"), by_row) * 3
        + (by_col, P("col"), P("row"), by_col)
        + (P(), P(), P(), P(), P(), P("dp")),
        check_vma=False,
    )
```

```python
import functools

import jax
import jax.numpy as jnp
from jax import lax
from jax.experimental import pallas as pl
from jax.experimental.pallas import tpu as pltpu
from jax.sharding import PartitionSpec as P

HEADS = 12
HEAD = 64
STEP = 10
CLIP = 1.0
NOISE = 0.002
SAMPLE = 0.5
RATE = 0.5
DECAY = 1.0 - STEP ** (-0.8)

F32 = jnp.float32
BF16 = jnp.bfloat16
PLANE = ("row", "col")
MESH = pl.DeviceIdType.MESH


def dot_f32(left, right, dims):
    return lax.dot_general(left, right, (dims, ((), ())), preferred_element_type=F32)


def mm(left, right):
    return dot_f32(left, right, ((1,), (0,)))


def mm_nt(left, right):
    return dot_f32(left, right, ((1,), (1,)))


def mm_tn(left, right):
    return dot_f32(left, right, ((0,), (0,)))


def gather_matrix(block, row_dim):
    part = lax.all_gather(block, "row", axis=row_dim, tiled=True)
    return lax.all_gather(part, "col", axis=1 - row_dim, tiled=True)


def plane_sum(array):
    return lax.psum(array, PLANE)


def example_sum(array):
    return lax.psum(array, "dp")


class Link:
    def __init__(self, send_sems, recv_sems):
        self.dp, self.row, self.col = (lax.axis_index(axis) for axis in ("dp", "row", "col"))
        self.x, self.core = self.dp // 2, self.dp % 2
        self.beside = 2 * (1 - self.x) + self.core
        self.sibling = 2 * self.x + 1 - self.core
        self.send_sems, self.recv_sems = send_sems, recv_sems
        self.n_send = 0
        self.open = []

    def device(self, **moved):
        return {"dp": self.dp, "row": self.row, "col": self.col, **moved}

    def send(self, src, dst, recv, device, when=None):
        sem = self.send_sems.at[self.n_send]
        self.n_send += 1
        copy = pltpu.make_async_remote_copy(
            src_ref=src,
            dst_ref=dst,
            send_sem=sem,
            recv_sem=self.recv_sems.at[recv],
            device_id=device,
            device_id_type=MESH,
        )
        self.open.append((copy, when))
        copy.start() if when is None else pl.when(when)(copy.start)

    def landed(self, dst, recv):
        pltpu.make_async_remote_copy(
            src_ref=dst,
            dst_ref=dst,
            send_sem=self.send_sems.at[0],
            recv_sem=self.recv_sems.at[recv],
            device_id=self.device(col=1 - self.col),
            device_id_type=MESH,
        ).wait_recv()

    def finish(self):
        for copy, when in self.open:
            copy.wait_send() if when is None else pl.when(when)(copy.wait_send)
        self.open = []

    def greet(self, devices):
        barrier = pltpu.get_barrier_semaphore()
        count = 0
        for device, when in devices:

            def signal(device=device):
                pl.semaphore_signal(barrier, inc=1, device_id=device, device_id_type=MESH)

            if when is None:
                signal()
                count = count + 1
            else:
                pl.when(when)(signal)
                count = count + when.astype(jnp.int32)
        pl.semaphore_wait(barrier, count)

    def plane_peers(self, n_row):
        me, peers = self.col * n_row + self.row, []
        for k in range(1, 2 * n_row):
            index = (me + k) % (2 * n_row)
            peers.append((index, self.device(row=index % n_row, col=index // n_row)))
        return me, peers

    def example_peers(self):
        return [((self.dp + k) % 4, self.device(dp=(self.dp + k) % 4)) for k in range(1, 4)]

    def plane_neighbours(self, n_row):
        return [
            (self.device(row=self.row + 1), self.row < n_row - 1),
            (self.device(row=self.row - 1), self.row > 0),
            (self.device(col=1 - self.col), None),
        ]


def run_together(*steps):
    steps = list(steps)
    while steps:
        for step in list(steps):
            try:
                next(step)
            except StopIteration:
                steps.remove(step)


def scatter_sum(link, base, n_row, part, from_col, ins, outs, own, make=None, span=slice(None)):
    row, col = link.row, link.col
    (up_in, down_in), (up_out, down_out) = ins, outs
    y_base, up_base, down_base = base, base + n_row, base + 2 * n_row
    order = [at for k in range(n_row // 2) for at in (n_row - 1 - k, k)]
    for at in order:
        if make is not None:
            make(1 - col, at)
        link.send(part.at[1 - col, at, span], from_col.at[at, span], y_base + at, link.device(col=1 - col))
    yield
    if make is not None:
        for k, at in enumerate(order):
            make(col, at)
            if k % 2:
                yield
    waiting = list(order)

    def mine(at):
        return part[col, at, span].astype(F32) + from_col[at, span].astype(F32)

    for k in range(n_row - 1):
        for at in (n_row - 1 - k, k):
            if at in waiting:
                waiting.remove(at)
                link.landed(from_col.at[at, span], y_base + at)
        for at, going, more, source, target, base_at, device in (
            (n_row - 1 - k, row < n_row - 1 - k, row > 0, up_in, up_out, up_base, link.device(row=row + 1)),
            (k, row > k, row < n_row - 1, down_in, down_out, down_base, link.device(row=row - 1)),
        ):

            @pl.when(going & more)
            def _():
                link.landed(source.at[at, span], base_at + at)
                target[at, span] = (mine(at) + source[at, span].astype(F32)).astype(BF16)

            @pl.when(going & jnp.logical_not(more))
            def _():
                target[at, span] = mine(at).astype(BF16)

            link.send(target.at[at, span], source.at[at, span], base_at + at, device, going)
        yield
    own[span] = mine(row)

    for more, source, base_at in ((row > 0, up_in, up_base), (row < n_row - 1, down_in, down_base)):

        @pl.when(more)
        def _():
            link.landed(source.at[row, span], base_at + row)
            own[span] += source[row, span].astype(F32)


def spread(link, base, n_row, own, place, onward=None):
    row, col = link.row, link.col
    up, down, side = (device for device, _ in link.plane_neighbours(n_row))
    here = place(row, col)
    link.send(own, here, base + row, up, row < n_row - 1)
    link.send(own, here, base + row, down, row > 0)
    if onward is not None:
        yield
    link.send(own, here, base + n_row + row, side)
    yield
    def arrive(k):
        for at, there in [(row - k, row >= k), (row + k, row + k < n_row)][: 2 if k else 1]:
            block = place(at, 1 - col)
            pl.when(there)(functools.partial(link.landed, block, base + n_row + at))
            if onward is not None:
                onward(at, 1 - col, there)

    for k in range(1, n_row):
        for at, there, device, further in (
            (row - k, row >= k, up, row < n_row - 1),
            (row + k, row + k < n_row, down, row > 0),
        ):
            block = place(at, col)
            pl.when(there)(functools.partial(link.landed, block, base + at))
            if k < n_row - 1:
                link.send(block, block, base + at, device, there & further)
            link.send(block, block, base + n_row + at, side, there)
            if onward is not None:
                onward(at, col, there)
        yield
        if k > 1:
            arrive(k - 2)
            yield
    for k in range(n_row - 2, n_row):
        arrive(k)
        yield


def spread_matrix(link, base, n_row, shard, whole, by_row, local_sems):
    row, col, at_x, at_core = link.row, link.col, link.x, link.core
    columns = shard.shape[-1]

    def block(at_row, at_col, x, core):
        lead, side = (at_row, at_col) if by_row else (at_col, at_row)
        return whole.at[lead, x, core, :, pl.ds(pl.multiple_of(side * columns, 128), columns)]

    local = []
    for index, x in enumerate((at_x, 1 - at_x)):
        copy = pltpu.make_async_copy(
            shard.at[2 * x + at_core], block(row, col, x, at_core), local_sems.at[index]
        )
        copy.start()
        local.append(copy)
    x_base, core_base = base + 2 * n_row, base + 4 * n_row
    beside, sibling = link.device(dp=link.beside), link.device(dp=link.sibling)

    def side_of(at_col, x, core):
        if not by_row:
            return whole.at[at_col, x, core]
        return whole.at[:, x, core, :, pl.ds(pl.multiple_of(at_col * columns, 128), columns)]

    def to_x(at_row, at_col, when):
        ref = block(at_row, at_col, at_x, at_core)
        link.send(ref, ref, x_base + at_col * n_row + at_row, beside, when)

    def to_core(at_col, x, index):
        ref = side_of(at_col, x, at_core)
        link.send(ref, ref, core_base + index, sibling)

    yield from spread(link, base, n_row, shard.at[link.dp], lambda r, c: block(r, c, at_x, at_core), to_x)
    for copy in local:
        copy.wait()
    to_core(0, at_x, 0)
    to_core(1, at_x, 1)
    yield
    for index, at_col in enumerate((col, 1 - col)):
        for k in range(n_row):
            at_row = lax.rem(row + k, n_row)
            if k or index:
                link.landed(block(at_row, at_col, 1 - at_x, at_core), x_base + at_col * n_row + at_row)
            if k % 2:
                yield
        to_core(at_col, 1 - at_x, 2 + at_col)
    yield
    for at_col in range(2):
        link.landed(side_of(at_col, at_x, 1 - at_core), core_base + at_col)
        link.landed(side_of(at_col, 1 - at_x, 1 - at_core), core_base + 2 + at_col)


N_MATRIX = 4 * 4 + 4


def front_kernel(n_row, ids, table, pos, *refs):
    shards, (start, low, square), wholes = refs[:4], refs[4:7], refs[7:11]
    held, staged, row_block_ref, pos_in, looked = refs[11:16]
    from_col, up_in, down_in, up_out, down_out, own, own_low = refs[16:23]
    send_sems, recv_sems, local_sems, table_sems, low_sems = refs[23:]
    limit, width = table.shape
    block = own.shape[0]
    piece = limit // table_sems.shape[0]
    loads = [
        pltpu.make_async_copy(table.at[pl.ds(at, piece)], held.at[pl.ds(at, piece)], table_sems.at[k])
        for k, at in enumerate(range(0, limit, piece))
    ]
    for load in loads:
        load.start()
    link = Link(send_sems, recv_sems)
    row_peers = [(link.row + k) % n_row for k in range(1, n_row)]
    link.greet(
        [(link.device(row=peer), None) for peer in row_peers]
        + [(link.device(col=1 - link.col), None)]
        + [(link.device(dp=link.beside), None), (link.device(dp=link.sibling), None)]
    )
    first = (link.col * n_row + link.row) * limit
    pos_base = 5 * n_row + 4 * N_MATRIX

    def look_up(col, at):
        token = (col * n_row + at) * block

        def step(k, carry):
            entry = ids[token + k] - first
            inside = (entry >= 0) & (entry < limit)
            row = held[pl.ds(jnp.clip(entry, 0, limit - 1), 1), :]
            row_block_ref[pl.ds(k, 1), :] = jnp.where(inside, row, 0.0)
            return carry

        lax.fori_loop(0, block, step, 0, unroll=8)
        looked[col, at] = row_block_ref[...].astype(BF16)

    def tokens():
        for peer in row_peers:
            rows = pos.at[:, pl.ds(pl.multiple_of(peer * block, 128), block)]
            link.send(rows, pos_in.at[link.row], pos_base + link.row, link.device(row=peer))
        pos_in[link.row] = pos[:, pl.ds(pl.multiple_of(link.row * block, 128), block)]
        for load in loads:
            load.wait()
        yield from scatter_sum(
            link, 0, n_row, looked, from_col, (up_in, down_in), (up_out, down_out), own, look_up
        )
        for peer in row_peers:
            link.landed(pos_in.at[peer], pos_base + peer)
        pos_own = jnp.concatenate([pos_in[k] for k in range(n_row)], 0).T
        own_low[...] = (own[...] + pos_own).astype(BF16)
        start[link.col, link.row] = own_low[...]
        yield from spread(link, 3 * n_row, n_row, own_low, lambda r, c: start.at[c, r])

    def shorten():
        yield
        square[...] = jnp.zeros_like(square)
        count = low.shape[0] // BLOCK
        stores = []
        for k in range(count):
            rows = min(BLOCK, limit - k * BLOCK)
            if k > 1:
                stores[k - 2].wait()
            part = held[k * BLOCK : k * BLOCK + rows, :]
            square[...] += jnp.sum(part * part, 0, keepdims=True)
            if rows < BLOCK:
                staged[k % 2, rows:] = jnp.zeros((BLOCK - rows, width), BF16)
            staged[k % 2, :rows] = part.astype(BF16)
            stores.append(
                pltpu.make_async_copy(staged.at[k % 2], low.at[pl.ds(k * BLOCK, BLOCK)], low_sems.at[k % 2])
            )
            stores[k].start()
            yield
        for store in stores[-2:]:
            store.wait()

    matrices = [
        spread_matrix(
            link, 5 * n_row + index * N_MATRIX, n_row, shards[index], wholes[index], index < 3, local_sems.at[index]
        )
        for index in range(4)
    ]
    run_together(*matrices, tokens(), shorten())
    link.finish()


def front(ids, table, pos, shards, n_row):
    limit, width = table.shape
    block = ids.shape[0] // (2 * n_row)
    low = (pl.cdiv(limit, BLOCK) * BLOCK, width)
    wholes = [(n_row, 2, 2) + shard.shape[1:2] + (2 * shard.shape[2],) for shard in shards[:3]]
    wholes.append((2, 2, 2) + shards[3].shape[1:2] + (n_row * shards[3].shape[2],))
    rows = pltpu.VMEM((n_row, block, width), BF16)
    vmem, hbm = pl.BlockSpec(memory_space=pltpu.VMEM), pl.BlockSpec(memory_space=pl.ANY)
    shape = jax.ShapeDtypeStruct
    return pl.pallas_call(
        functools.partial(front_kernel, n_row),
        out_shape=[shape((2, n_row, block, width), BF16), shape(low, BF16), shape((1, width), F32)]
        + [shape(whole, BF16) for whole in wholes],
        in_specs=[pl.BlockSpec(memory_space=pltpu.SMEM), hbm, vmem] + [hbm] * 4,
        out_specs=[vmem, hbm, vmem] + [hbm] * 4,
        scratch_shapes=[pltpu.VMEM(table.shape, F32), pltpu.VMEM((2, BLOCK, width), BF16)]
        + [pltpu.VMEM((block, width), F32), pltpu.VMEM((n_row,) + pos.shape[:1] + (block,), F32)]
        + [pltpu.VMEM((2, n_row, block, width), BF16)]
        + [rows] * 5
        + [pltpu.VMEM((block, width), F32), pltpu.VMEM((block, width), BF16)]
        + [
            pltpu.SemaphoreType.DMA((220,)),
            pltpu.SemaphoreType.DMA((6 * n_row + 4 * N_MATRIX,)),
            pltpu.SemaphoreType.DMA((4, 2)),
            pltpu.SemaphoreType.DMA((6,)),
            pltpu.SemaphoreType.DMA((2,)),
        ],
        compiler_params=pltpu.CompilerParams(
            collective_id=1, has_side_effects=True, vmem_limit_bytes=56 * 1024 * 1024
        ),
    )(ids, table, pos, *shards)


def total_kernel(n_row, part, total, *refs):
    from_col, up_in, down_in, up_out, down_out, own, own_low, send_sems, recv_sems = refs
    link = Link(send_sems, recv_sems)
    link.greet(link.plane_neighbours(n_row))

    def steps(base, span):
        yield from scatter_sum(
            link, base, n_row, part, from_col, (up_in, down_in), (up_out, down_out), own, None, span
        )
        own_low[span] = own[span].astype(BF16)
        total[link.col, link.row, span] = own_low[span]
        place = lambda r, c: total.at[c, r, span]
        yield from spread(link, base + 3 * n_row, n_row, own_low.at[span], place)

    size = own.shape[0] // SPANS
    run_together(*(steps(5 * n_row * k, pl.ds(k * size, size)) for k in range(SPANS)))
    link.finish()


SPANS = 2


def plane_total(part, collective_id):
    n_row, block, width = part.shape[1:]
    rows = pltpu.VMEM((n_row, block, width), BF16)
    vmem = pl.BlockSpec(memory_space=pltpu.VMEM)
    return pl.pallas_call(
        functools.partial(total_kernel, n_row),
        out_shape=jax.ShapeDtypeStruct(part.shape, BF16),
        in_specs=[vmem],
        out_specs=vmem,
        scratch_shapes=[rows] * 5
        + [pltpu.VMEM((block, width), F32), pltpu.VMEM((block, width), BF16)]
        + [pltpu.SemaphoreType.DMA((40 * SPANS,)), pltpu.SemaphoreType.DMA((5 * n_row * SPANS,))],
        compiler_params=pltpu.CompilerParams(
            collective_id=collective_id, has_side_effects=True, vmem_limit_bytes=40 * 1024 * 1024
        ),
    )(part)


FORWARD_QUERIES = 512
BACK_QUERIES = 256


def causal(scores):
    keys = lax.broadcasted_iota(jnp.int32, scores.shape, 0)
    queries = lax.broadcasted_iota(jnp.int32, scores.shape, 1)
    return jnp.where(keys <= queries, scores, -1e30)


def lanes_of(head):
    return slice(head * HEAD, (head + 1) * HEAD)


def attend_kernel(q_ref, k_ref, v_ref, o_ref, log_ref):
    size = FORWARD_QUERIES
    values = [v_ref[:, lanes_of(head)].T for head in range(2)]
    steps = [(head, at) for head in range(2) for at in range(0, q_ref.shape[0], size)]

    def scores_of(head, at):
        queries = q_ref[at : at + size, lanes_of(head)] * HEAD ** (-0.5)
        return mm_nt(k_ref[: at + size, lanes_of(head)], queries)

    later = scores_of(*steps[0])
    for k, (head, at) in enumerate(steps):
        scores = later
        if k + 1 < len(steps):
            later = scores_of(*steps[k + 1])
        here = slice(at, at + size)
        edge = causal(scores[at:])
        top = jnp.max(edge, 0, keepdims=True)
        if at:
            top = jnp.maximum(top, jnp.max(scores[:at], 0, keepdims=True))
        exps = jnp.exp(edge - top)
        count = jnp.sum(exps, 0, keepdims=True)
        exps = exps.astype(BF16)
        if at:
            before = jnp.exp(scores[:at] - top)
            count = count + jnp.sum(before, 0, keepdims=True)
            exps = jnp.concatenate([before.astype(BF16), exps], 0)
        mixed = mm(values[head][:, : at + size], exps)
        o_ref[here, lanes_of(head)] = (mixed / count).T.astype(BF16)
        log_ref[0, head : head + 1, here] = top + jnp.log(count)


def attend(packed):
    length, width = packed.shape[0], packed.shape[1] // 3
    pairs = HEADS // 2
    lanes = 2 * HEAD
    column = lambda first: pl.BlockSpec((length, lanes), lambda i: (0, first + i))
    return pl.pallas_call(
        attend_kernel,
        grid=(pairs,),
        out_shape=[
            jax.ShapeDtypeStruct((length, width), BF16),
            jax.ShapeDtypeStruct((pairs, 2, length), F32),
        ],
        in_specs=[column(0), column(pairs), column(2 * pairs)],
        out_specs=[column(0), pl.BlockSpec((1, 2, length), lambda i: (i, 0, 0))],
        cost_estimate=cost(20 * length * length * width, 8 * length * width),
        compiler_params=pltpu.CompilerParams(vmem_limit_bytes=40 * MEGA),
    )(packed, packed, packed)


def attend_back_kernel(q_ref, k_ref, v_ref, g_ref, log_ref, out_ref, key_sum, value_sum):
    length, size = q_ref.shape[0], BACK_QUERIES
    keys_turned = [k_ref[:, lanes_of(head)].T for head in range(2)]
    steps = [(head, at) for head in range(2) for at in range(0, length, size)]

    def products_of(head, at):
        queries = q_ref[at : at + size, lanes_of(head)] * HEAD ** (-0.5)
        grads = g_ref[at : at + size, lanes_of(head)]
        scores = mm_nt(k_ref[: at + size, lanes_of(head)], queries)
        return scores, mm_nt(v_ref[: at + size, lanes_of(head)], grads), queries, grads

    later = products_of(*steps[0])
    for k, (head, at) in enumerate(steps):
        scores, prob_grad, queries, grads = later
        if k + 1 < len(steps):
            later = products_of(*steps[k + 1])
        here = slice(at, at + size)
        log_norm = log_ref[0, head : head + 1, here]
        probs = jnp.exp(causal(scores[at:]) - log_norm)
        if at:
            probs = jnp.concatenate([jnp.exp(scores[:at] - log_norm), probs], 0)
        level = jnp.sum(probs * prob_grad, 0, keepdims=True)
        score_grad = (probs * (prob_grad - level)).astype(BF16)
        value_grad = mm(probs.astype(BF16), grads)
        key_grad = mm(score_grad, queries)
        query_grad = mm(keys_turned[head][:, : at + size], score_grad) * HEAD ** (-0.5)
        out_ref[0, here, lanes_of(head)] = query_grad.T.astype(BF16)
        if at:
            value_sum[head, :at] += value_grad[:at]
            key_sum[head, :at] += key_grad[:at]
        value_sum[head, here] = value_grad[at:]
        key_sum[head, here] = key_grad[at:]
        if at + size == length:
            out_ref[1, :, lanes_of(head)] = key_sum[head].astype(BF16)
            out_ref[2, :, lanes_of(head)] = value_sum[head].astype(BF16)


def attend_back(packed, mixed_grad, log_norm):
    length, width = mixed_grad.shape
    pairs = HEADS // 2
    lanes = 2 * HEAD
    column = lambda first: pl.BlockSpec((length, lanes), lambda i: (0, first + i))
    return pl.pallas_call(
        attend_back_kernel,
        grid=(pairs,),
        out_shape=jax.ShapeDtypeStruct((3, length, width), BF16),
        in_specs=[column(0), column(pairs), column(2 * pairs), column(0)]
        + [pl.BlockSpec((1, 2, length), lambda i: (i, 0, 0))],
        out_specs=pl.BlockSpec((3, length, lanes), lambda i: (0, 0, i)),
        scratch_shapes=[pltpu.VMEM((2, length, HEAD), F32)] * 2,
        cost_estimate=cost(30 * length * length * width, 16 * length * width),
        compiler_params=pltpu.CompilerParams(vmem_limit_bytes=48 * 1024 * 1024),
    )(packed, packed, packed, mixed_grad, log_norm)


def meet(link, *exchanges):
    for base, value, slots, me, peers in exchanges:
        slots[me] = value[...]
        for _, device in peers:
            link.send(value, slots.at[me], base + me, device)
    for base, _, slots, _, peers in exchanges:
        for index, _ in peers:
            link.landed(slots.at[index], base + index)


def added(slots):
    total = slots[0]
    for k in range(1, slots.shape[0]):
        total = total + slots[k]
    return total


def sum_small_kernel(n_row, value, total, middle, slots, dp_slots, send_sems, recv_sems):
    link = Link(send_sems, recv_sems)
    me, peers = link.plane_peers(n_row)
    examples = link.example_peers()
    link.greet([(device, None) for _, device in peers + examples])
    meet(link, (0, value, slots, me, peers))
    middle[...] = added(slots)
    meet(link, (2 * n_row, middle, dp_slots, link.dp, examples))
    total[...] = added(dp_slots)
    link.finish()


def sum_small(value, n_row, collective_id):
    vmem = pl.BlockSpec(memory_space=pltpu.VMEM)
    return pl.pallas_call(
        functools.partial(sum_small_kernel, n_row),
        out_shape=jax.ShapeDtypeStruct(value.shape, F32),
        in_specs=[vmem],
        out_specs=vmem,
        scratch_shapes=[pltpu.VMEM(value.shape, F32), pltpu.VMEM((2 * n_row,) + value.shape, F32)]
        + [pltpu.VMEM((4,) + value.shape, F32)]
        + [pltpu.SemaphoreType.DMA((2 * n_row + 2,)), pltpu.SemaphoreType.DMA((2 * n_row + 4,))],
        compiler_params=pltpu.CompilerParams(collective_id=collective_id, has_side_effects=True),
    )(value)


def log_total_kernel(n_row, tops, sums, picked, log_ref, pick_ref, value, slots, send_sems, recv_sems):
    link = Link(send_sems, recv_sems)
    me, peers = link.plane_peers(n_row)
    link.greet([(device, None) for _, device in peers])
    top = jnp.max(tops[...], 0)
    value[0] = top
    value[1] = jnp.sum(sums[...] * jnp.exp(tops[...] - top[None]), 0)
    value[2] = picked[...]
    meet(link, (0, value, slots, me, peers))
    everyone = range(2 * n_row)
    top, total, pick = slots[0, 0], jnp.zeros_like(top), jnp.zeros_like(top)
    for k in everyone:
        top = jnp.maximum(top, slots[k, 0])
    for k in everyone:
        total = total + slots[k, 1] * jnp.exp(slots[k, 0] - top)
        pick = pick + slots[k, 2]
    log_ref[...] = top + jnp.log(total)
    pick_ref[...] = pick
    link.finish()


def log_total(tops, sums, picked, n_row, collective_id):
    length = picked.shape[-1]
    tile = (length // 128, 128)
    tops, sums, picked = (item.reshape(item.shape[:-2] + tile) for item in (tops, sums, picked))
    vmem = pl.BlockSpec(memory_space=pltpu.VMEM)
    log_norm, picked = pl.pallas_call(
        functools.partial(log_total_kernel, n_row),
        out_shape=[jax.ShapeDtypeStruct(tile, F32)] * 2,
        in_specs=[vmem] * 3,
        out_specs=[vmem] * 2,
        scratch_shapes=[pltpu.VMEM((3,) + tile, F32), pltpu.VMEM((2 * n_row, 3) + tile, F32)]
        + [pltpu.SemaphoreType.DMA((2 * n_row,))] * 2,
        compiler_params=pltpu.CompilerParams(collective_id=collective_id, has_side_effects=True),
    )(tops, sums, picked)
    return log_norm.reshape(1, length), picked.reshape(1, length)


BLOCK = 1056
ROWS = 528
MEGA = 1024 * 1024


def cost(flops, bytes_accessed):
    return pl.CostEstimate(flops=flops, bytes_accessed=bytes_accessed, transcendentals=0)


def blocks_of(limit):
    return pl.cdiv(limit, BLOCK)


def entries(shape, first=0, skip=0):
    return lax.broadcasted_iota(jnp.int32, shape, 0) + ((pl.program_id(0) + first) * BLOCK + skip)


PARTS = 3
PART = BLOCK // PARTS


def parts_of():
    return [slice(at, at + PART) for at in range(0, BLOCK, PART)]


def head_kernel(limit, low_ref, z_ref, target_ref, exp_ref, top_ref, sum_ref, pick_ref):
    @pl.when(pl.program_id(0) == 0)
    def _():
        pick_ref[...] = jnp.zeros_like(pick_ref)

    picked = jnp.zeros(pick_ref.shape, F32)
    steps = parts_of()
    later = mm_nt(low_ref[steps[0]], z_ref[...])
    for k, rows in enumerate(steps):
        logits = later
        if k + 1 < PARTS:
            later = mm_nt(low_ref[steps[k + 1]], z_ref[...])
        off = jnp.where(entries((PART, 1), 0, rows.start) < limit, 0.0, -1e30)
        logits = logits + off
        top = jnp.max(logits, 0, keepdims=True)
        hit = lax.broadcasted_iota(jnp.int32, logits.shape, 0) == target_ref[...] - (pl.program_id(0) * BLOCK + rows.start)
        picked = picked + jnp.sum(jnp.where(hit, logits, 0.0), 0, keepdims=True)
        exps = jnp.exp(logits - top)
        exp_ref[rows] = exps.astype(BF16)
        top_ref[k] = top
        sum_ref[k] = jnp.sum(exps, 0, keepdims=True)
    pick_ref[...] += picked


def whole_block(shape):
    return pl.BlockSpec(shape, lambda i, *_: (0,) * len(shape), pipeline_mode=pl.Buffered(1))


def row_block(width):
    return pl.BlockSpec((BLOCK, width), lambda i, *_: (i, 0))


def line_block(width, lines=1):
    return pl.BlockSpec((lines, 1, width), lambda i, *_: (i, 0, 0))


def head(low, limit, z, target):
    length, width = z.shape
    count = blocks_of(limit)
    shape = jax.ShapeDtypeStruct
    line = shape((count * PARTS, 1, length), F32)
    return pl.pallas_call(
        functools.partial(head_kernel, limit),
        grid=(count,),
        out_shape=[shape((count * BLOCK, length), BF16), line, line, shape((1, length), F32)],
        in_specs=[row_block(width), whole_block((length, width)), whole_block((1, length))],
        out_specs=[row_block(length), line_block(length, PARTS), line_block(length, PARTS), whole_block((1, length))],
        cost_estimate=cost(2 * limit * width * length, 2 * limit * width + 2 * limit * length),
        compiler_params=pltpu.CompilerParams(vmem_limit_bytes=48 * MEGA),
    )(low, z, target)


def slope_of(exps, rows, target_ref, first=0):
    entry = lax.broadcasted_iota(jnp.int32, exps.shape, 0)
    target = target_ref[...] - ((pl.program_id(0) + first) * BLOCK + rows.start)
    return jnp.where(entry == target, exps - 1.0, exps).astype(BF16)


def head_back_kernel(exp_ref, top_ref, log_ref, target_ref, low_ref, z_ref, grad_ref, table_ref, slope, total):
    at = pl.program_id(0)
    for k, rows in enumerate(parts_of()):
        scale = jnp.exp(top_ref[k] - log_ref[...])
        slope[rows] = slope_of(exp_ref[rows].astype(F32) * scale, rows, target_ref)
        table_ref[rows] = mm(slope[rows], z_ref[...]).astype(BF16)
    part = mm_tn(low_ref[...], slope[...])

    @pl.when(at == 0)
    def _():
        total[...] = part

    @pl.when(at > 0)
    def _():
        total[...] += part

    @pl.when(at == pl.num_programs(0) - 1)
    def _():
        grad_ref[...] = total[...].T.astype(BF16)


def head_back(exps, tops, log_norm, target, low, z):
    length, width = z.shape
    return pl.pallas_call(
        head_back_kernel,
        grid=(low.shape[0] // BLOCK,),
        out_shape=[jax.ShapeDtypeStruct((length, width), BF16), jax.ShapeDtypeStruct(low.shape, BF16)],
        in_specs=[row_block(length), line_block(length, PARTS), whole_block((1, length)), whole_block((1, length))]
        + [row_block(width), whole_block((length, width))],
        out_specs=[whole_block((length, width)), row_block(width)],
        scratch_shapes=[pltpu.VMEM((BLOCK, length), BF16), pltpu.VMEM((width, length), F32)],
        cost_estimate=cost(4 * low.size * length, 4 * low.size + 2 * exps.size),
        compiler_params=pltpu.CompilerParams(vmem_limit_bytes=48 * MEGA),
    )(exps, tops, log_norm, target, low, z)


def token_lists(ids, start, limit):
    length = ids.shape[0]
    token = jnp.arange(length, dtype=jnp.int32)
    one, two = ids[:, None], ids[None, :]
    ahead = (two < one) | ((two == one) & (token[None, :] < token[:, None]))
    place = jnp.sum(ahead.astype(jnp.int32), 1)
    at = place[:, None] == token[None, :]
    order = jnp.sum(jnp.where(at, token[:, None], 0), 0)
    ordered = jnp.sum(jnp.where(at, ids[:, None], 0), 0)
    edges = start + jnp.minimum(jnp.arange(blocks_of(limit) + 1) * BLOCK, limit)
    bounds = jnp.sum((ids[None, :] < edges[:, None]).astype(jnp.int32), 1)
    return ordered - start, order, bounds


def add_rows(total, ids_ref, order_ref, bounds_ref, grad_ref, first=0):
    at = pl.program_id(0) + first

    def step(k, carry):
        row, token = ids_ref[k] - at * BLOCK, order_ref[k]
        total[pl.ds(row, 1), :] += grad_ref[pl.ds(token, 1), :]
        return carry

    lax.fori_loop(bounds_ref[at], bounds_ref[at + 1], step, 0)


def own_rows_kernel(ids_ref, order_ref, bounds_ref, table_ref, grad_ref, out_ref, square_ref, total):
    total[...] = table_ref[...].astype(F32)
    add_rows(total, ids_ref, order_ref, bounds_ref, grad_ref)
    full = total[...]
    out_ref[...] = full.astype(BF16)

    @pl.when(pl.program_id(0) == 0)
    def _():
        square_ref[...] = jnp.zeros_like(square_ref)

    square_ref[...] += jnp.sum(full * full, 0, keepdims=True)


def add_own_rows(table, lists, grad):
    width = table.shape[1]
    return pl.pallas_call(
        own_rows_kernel,
        grid_spec=pltpu.PrefetchScalarGridSpec(
            num_scalar_prefetch=3,
            grid=(table.shape[0] // BLOCK,),
            in_specs=[row_block(width), whole_block(grad.shape)],
            out_specs=[row_block(width), whole_block((1, width))],
            scratch_shapes=[pltpu.VMEM((BLOCK, width), F32)],
        ),
        out_shape=[jax.ShapeDtypeStruct(table.shape, BF16), jax.ShapeDtypeStruct((1, width), F32)],
        cost_estimate=cost(0, 4 * table.size),
        compiler_params=pltpu.CompilerParams(vmem_limit_bytes=56 * MEGA),
    )(*lists, table, grad)


def table_sum_kernel(first, ids_ref, order_ref, bounds_ref, share_ref, *refs):
    low_ref, z_ref, log_ref, target_ref, own_ref, grad_ref, out_ref, total = refs
    steps = parts_of()
    later = mm_nt(low_ref[steps[0]], z_ref[...])
    for k, rows in enumerate(steps):
        logits = later
        if k + 1 < PARTS:
            later = mm_nt(low_ref[steps[k + 1]], z_ref[...])
        slope = slope_of(jnp.exp(logits - log_ref[...]), rows, target_ref, first)
        total[rows] = mm(slope, z_ref[...])
    add_rows(total, ids_ref, order_ref, bounds_ref, grad_ref, first)
    out_ref[...] = (share_ref[0] * own_ref[...].astype(F32) + share_ref[1] * total[...]).astype(BF16)


def table_sum(own, low, z, log_norm, target, lists, grad, shares, first, count):
    length, width = z.shape
    rows = lambda i, *_: (i + first, 0)
    return pl.pallas_call(
        functools.partial(table_sum_kernel, first),
        grid_spec=pltpu.PrefetchScalarGridSpec(
            num_scalar_prefetch=4,
            grid=(count,),
            in_specs=[pl.BlockSpec((BLOCK, width), rows), whole_block((length, width))]
            + [whole_block((1, length)), whole_block((1, length))]
            + [pl.BlockSpec((BLOCK, width), rows), whole_block(grad.shape)],
            out_specs=row_block(width),
            scratch_shapes=[pltpu.VMEM((BLOCK, width), F32)],
        ),
        out_shape=jax.ShapeDtypeStruct((count * BLOCK, width), BF16),
        cost_estimate=cost(4 * count * BLOCK * width * length, 6 * count * BLOCK * width),
        compiler_params=pltpu.CompilerParams(vmem_limit_bytes=48 * MEGA),
    )(*lists, shares, low, z, log_norm, target, own, grad)


def turned(line, height):
    return jnp.broadcast_to(line, (height, line.shape[1])).T


def gradient_kernel(limit, count, divisor, first, *refs):
    sums, (noise_ref, old_ref), outs = refs[:count], refs[count : count + 2], refs[-5:]
    grad_ref, rows_ref, cols_ref, scaled_ref, level_ref = outs
    total = sums[0][...].astype(F32)
    for item in sums[1:]:
        total = total + item[...].astype(F32)
    grad = (total + NOISE * CLIP * noise_ref[...]) * (1.0 / divisor)
    entry = lax.broadcasted_iota(jnp.int32, (ROWS, 1), 0) + (pl.program_id(0) + first) * ROWS
    inside = entry < limit
    grad_ref[...] = grad
    squares = jnp.where(inside, grad * grad, 0.0)
    mean = jnp.sum(squares, 1, keepdims=True) / grad.shape[1] + 1e-30
    old = turned(old_ref[0], 128)[:, :1]
    rows = DECAY * old + (1.0 - DECAY) * mean
    rows_ref[0] = line_of(rows)

    @pl.when(pl.program_id(0) == 0)
    def _():
        cols_ref[...] = jnp.zeros_like(cols_ref)
        scaled_ref[...] = jnp.zeros_like(scaled_ref)
        level_ref[...] = jnp.zeros_like(level_ref)

    cols_ref[...] += jnp.sum(squares, 0, keepdims=True)
    scaled_ref[...] += jnp.sum(squares * (1.0 / rows), 0, keepdims=True)
    level_ref[...] += jnp.broadcast_to(jnp.sum(jnp.where(inside, rows, 0.0), 0, keepdims=True), level_ref.shape)


def table_gradient(sums, noise, old, divisor, first, count, into=None):
    limit, width = noise.shape
    shape = jax.ShapeDtypeStruct
    rows = pl.BlockSpec((ROWS, width), lambda i: (i + first, 0))
    extra = [] if into is None else list(into)
    everything = old.shape[0]
    return pl.pallas_call(
        functools.partial(gradient_kernel, limit, len(sums), divisor, first),
        grid=(count,),
        out_shape=[shape((limit, width), F32), shape((everything, 1, ROWS), F32)]
        + [shape((1, width), F32)] * 2
        + [shape((1, 128), F32)],
        in_specs=[pl.BlockSpec((ROWS, width), lambda i: (i, 0))] * len(sums)
        + [rows, pl.BlockSpec((1, 1, ROWS), lambda i: (i + first, 0, 0))]
        + [pl.BlockSpec(memory_space=pl.ANY)] * len(extra),
        out_specs=[rows, pl.BlockSpec((1, 1, ROWS), lambda i: (i + first, 0, 0)), whole_block((1, width)), whole_block((1, width))]
        + [whole_block((1, 128))],
        input_output_aliases={len(sums) + 2: 0, len(sums) + 3: 1} if extra else {},
        cost_estimate=cost(0, (8 + 2 * len(sums)) * count * ROWS * width),
        compiler_params=pltpu.CompilerParams(vmem_limit_bytes=58 * MEGA),
    )(*sums, noise, old, *extra)


SIDE = 256


def line_of(column):
    return jnp.broadcast_to(column, (column.shape[0], 128)).T[:1]


BY_ROW = (True, True, True, True, False)


def put_line(ref, at, line):
    size = line.shape[1]
    for k in range(0, size, 128):
        ref[at : at + 1, : min(128, size - k)] = line[:, k : min(k + 128, size)]
        at += 1
    return at


def get_line(value, at, size):
    rows = [value[at + k : at + k + 1, : min(128, size - 128 * k)] for k in range(pl.cdiv(size, 128))]
    return rows[0] if len(rows) == 1 else jnp.concatenate(rows, 1)


def line_places(shapes, rows_first):
    at, places = 0, []
    for (rows, cols), along in zip(shapes, BY_ROW):
        places.append(at)
        at += pl.cdiv(rows if along == rows_first else cols, 128)
    return places, -at // 8 * -8


def join_kernel(one_ref, two_ref, after_ref, out_ref):
    out_ref[...] = (one_ref[...].astype(F32) + two_ref[...].astype(F32)).astype(BF16)


def join(one, two, after):
    return pl.pallas_call(
        join_kernel,
        out_shape=jax.ShapeDtypeStruct(one.shape, BF16),
        grid=(1,),
        in_specs=[whole_block(one.shape), whole_block(two.shape), pl.BlockSpec(memory_space=pl.ANY)],
        out_specs=whole_block(one.shape),
        cost_estimate=cost(0, 6 * one.size),
    )(one, two, after)


def small_gradients_kernel(divisor, core_ref, *refs):
    half, other_half, small, small_second, small_noise = refs[:5]
    weights, noises, grads = (refs[5 + 5 * k : 10 + 5 * k] for k in range(3))
    small_outs, (to_col, to_row, square_ref, packed) = refs[20:23], refs[23:]
    lines = half.shape[0]
    packed[pl.ds(pl.multiple_of(core_ref[0] * lines, 16), lines)] = half[...]
    packed[pl.ds(pl.multiple_of((1 - core_ref[0]) * lines, 16), lines)] = other_half[...]
    width = small.shape[1]
    scale = 1.0 / divisor
    side = weights[1].shape[0]
    cuts = (0, weights[1].shape[1], weights[1].shape[1] + weights[2].shape[1])
    for index in (1, 2, 3):
        at, end, lane_to = cuts[index - 1], cuts[index - 1] + weights[index].shape[1], 0
        while at < end:
            piece, lane = at // width, at % width
            size = min(width - lane, end - at)
            part = packed[piece * side : (piece + 1) * side, lane : lane + size].astype(F32)
            lanes = slice(lane_to, lane_to + size)
            grads[index][:, lanes] = (part + NOISE * CLIP * noises[index][:, lanes]) * scale
            at, lane_to = at + size, lane_to + size
    first = side * ((cuts[2] + weights[3].shape[1]) // width)
    down = weights[4].shape[0]
    grads[4][...] = (packed[first : first + down, :].astype(F32) + NOISE * CLIP * noises[4][...]) * scale
    first += down
    tall, wide = weights[0].shape
    grads[0][...] = (packed[first : first + tall, :wide].astype(F32) + NOISE * CLIP * noises[0][...]) * scale
    first += tall

    to_col[...] = jnp.zeros_like(to_col)
    to_row[...] = jnp.zeros_like(to_row)
    shapes = [item.shape for item in weights]
    col_places, row_places = line_places(shapes, True)[0], line_places(shapes, False)[0]
    lane = lax.broadcasted_iota(jnp.int32, (1, 128), 1)
    weight_sq = jnp.zeros((1, 128), F32)
    for index, along in enumerate(BY_ROW):
        squares = grads[index][...] * grads[index][...]
        row_sum = line_of(jnp.sum(squares, 1, keepdims=True))
        col_sum = jnp.sum(squares, 0, keepdims=True)
        put_line(to_col, col_places[index], row_sum if along else col_sum)
        put_line(to_row, row_places[index], col_sum if along else row_sum)
        total = jnp.sum(jnp.sum(weights[index][...] * weights[index][...], 0, keepdims=True), 1, keepdims=True)
        weight_sq = weight_sq + jnp.where(lane == index, total, 0.0)
    square_ref[...] = weight_sq

    count = small.shape[0]
    small_grad = (packed[first : first + 16, :].astype(F32)[:count] + NOISE * CLIP * small_noise[...]) * scale
    second_new = DECAY * small_second[...] + (1.0 - DECAY) * (small_grad * small_grad + 1e-30)
    update = small_grad * lax.rsqrt(second_new)
    mean = lambda item: jnp.sum(jnp.sum(item * item, 0, keepdims=True), 1, keepdims=True) / (count * width)
    size = RATE * jnp.maximum(1e-3, jnp.sqrt(mean(small[...])))
    size = size / jnp.maximum(1.0, jnp.sqrt(mean(update)))
    small_outs[0][...] = small_grad
    small_outs[1][...] = second_new
    small_outs[2][...] = small[...] - size * update


def small_gradients(core, half, other_half, small, small_second, small_noise, weights, noises, divisor):
    width = small.shape[1]
    matrix_shapes = [item.shape for item in weights]
    line_rows = [line_places(matrix_shapes, first)[1] for first in (True, False)]
    shape = lambda dims: jax.ShapeDtypeStruct(dims, F32)
    operands = [half, other_half, small, small_second, small_noise, *weights, *noises]
    shapes = matrix_shapes + [small.shape] * 3 + [(line_rows[0], 128), (line_rows[1], 128), (1, 128)]
    out = pl.pallas_call(
        functools.partial(small_gradients_kernel, divisor),
        grid_spec=pltpu.PrefetchScalarGridSpec(
            num_scalar_prefetch=1,
            grid=(1,),
            in_specs=[whole_block(item.shape) for item in operands],
            out_specs=[whole_block(dims) for dims in shapes],
            scratch_shapes=[pltpu.VMEM((2 * half.shape[0], width), BF16)],
        ),
        out_shape=[shape(dims) for dims in shapes],
        compiler_params=pltpu.CompilerParams(vmem_limit_bytes=56 * MEGA),
        cost_estimate=cost(0, 16 * MEGA),
    )(core, *operands)
    return out[:5], out[5:8], out[8:]


def statistics_kernel(n_row, vocab, *refs):
    table_over, over_cols, over_rows, old_lines = refs[:4]
    grads, (lines_ref, factor_ref), held = refs[4:9], refs[9:11], refs[11:16]
    to_level, both_slots, col_slots, row_slots, level_slots, send_sems, recv_sems, local_sems = refs[16:]
    n_col, width = 2, factor_ref.shape[1]
    everyone = n_row * n_col
    copies = [pltpu.make_async_copy(grads[k], held[k], local_sems.at[k]) for k in range(5)]
    for copy in copies:
        copy.start()
    link = Link(send_sems, recv_sems)
    me, peers = link.plane_peers(n_row)
    link.greet([(device, None) for _, device in peers])
    row_peers = [((link.row + k) % n_row, link.device(row=(link.row + k) % n_row)) for k in range(1, n_row)]
    meet(
        link,
        (0, table_over, both_slots, me, peers),
        (everyone, over_cols, col_slots, link.col, [(1 - link.col, link.device(col=1 - link.col))]),
        (everyone + n_col, over_rows, row_slots, link.row, row_peers),
    )
    both, over_col, over_row = added(both_slots), added(col_slots), added(row_slots)
    for copy in copies:
        copy.wait()

    lane = lax.broadcasted_iota(jnp.int32, (1, 128), 1)
    whole = lambda line: jnp.sum(line, 1, keepdims=True)
    lines = width // 128
    cols_new = DECAY * old_lines[5:6, :width] + (1.0 - DECAY) * (get_line(both, 0, width) / vocab + 1e-30)
    weight_sums, table_level = both[2 * lines : 2 * lines + 1], both[2 * lines + 1 : 2 * lines + 2, :1]
    everywhere = jnp.where(lane == 5, whole(get_line(both, lines, width) / cols_new), 0.0)
    counts = jnp.full((1, 128), float(vocab * width), F32)
    for index in range(5):
        counts = jnp.where(lane == index, float(held[index].shape[0] * held[index].shape[1] * everyone), counts)
    factor_ref[...] = jnp.zeros_like(factor_ref)
    factor_ref[0:1] = cols_new
    factor_ref[1:2] = lax.rsqrt(cols_new)

    lines_ref[...] = jnp.zeros_like(lines_ref)
    shapes = [item.shape for item in held]
    col_places, row_places = line_places(shapes, True)[0], line_places(shapes, False)[0]
    levels = jnp.where(lane == 5, table_level / (vocab * everyone), 0.0)
    scaled_sums = jnp.zeros((1, 128), F32)
    for index, along in enumerate(BY_ROW):
        rows, cols = held[index].shape
        parts_rows, parts_cols = (n_row, n_col) if along else (n_col, n_row)
        by_col = get_line(over_col, col_places[index], rows if along else cols)
        by_line = get_line(over_row, row_places[index], cols if along else rows)
        row_mean = (by_col if along else by_line) / (cols * parts_cols) + 1e-30
        col_mean = (by_line if along else by_col) / (rows * parts_rows) + 1e-30
        rows_line = DECAY * old_lines[index : index + 1, :rows] + (1.0 - DECAY) * row_mean
        cols_line = DECAY * old_lines[8 + index : 9 + index, :cols] + (1.0 - DECAY) * col_mean
        lines_ref[index : index + 1, :rows] = rows_line
        lines_ref[8 + index : 9 + index, :cols] = cols_line
        level = whole(rows_line) / (rows * parts_rows * parts_cols)
        scaled = held[index][...] * held[index][...] * (1.0 / turned(rows_line, 128)[:, :1])
        scaled = whole(jnp.sum(scaled, 0, keepdims=True) / cols_line)
        levels = jnp.where(lane == index, level, levels)
        scaled_sums = jnp.where(lane == index, scaled, scaled_sums)
    to_level[...] = jnp.zeros_like(to_level)
    to_level[0:1] = levels
    to_level[1:2] = scaled_sums
    meet(link, (everyone + n_col + n_row, to_level, level_slots, me, peers))
    levels = added(level_slots)
    level, square_sum = levels[0:1], levels[1:2] + everywhere
    size = RATE * jnp.maximum(1e-3, jnp.sqrt(weight_sums / counts))
    size = size / jnp.maximum(1.0, jnp.sqrt(square_sum * level / counts))
    sizes = size * jnp.sqrt(level)
    factor_ref[2:3, :128] = sizes
    link.finish()


def statistics(table_over, over_cols, over_rows, old_lines, grads, width, n_row, vocab, collective_id):
    wide = old_lines.shape[1]
    everyone = 2 * n_row
    vmem, hbm = pl.BlockSpec(memory_space=pltpu.VMEM), pl.BlockSpec(memory_space=pl.ANY)
    return pl.pallas_call(
        functools.partial(statistics_kernel, n_row, vocab),
        out_shape=[jax.ShapeDtypeStruct((16, wide), F32), jax.ShapeDtypeStruct((8, width), F32)],
        in_specs=[vmem] * 4 + [hbm] * 5,
        out_specs=[vmem] * 2,
        scratch_shapes=[pltpu.VMEM(item.shape, F32) for item in grads]
        + [pltpu.VMEM((8, 128), F32), pltpu.VMEM((everyone,) + table_over.shape, F32)]
        + [pltpu.VMEM((2,) + over_cols.shape, F32), pltpu.VMEM((n_row,) + over_rows.shape, F32)]
        + [pltpu.VMEM((everyone, 8, 128), F32)]
        + [pltpu.SemaphoreType.DMA((3 * everyone,)), pltpu.SemaphoreType.DMA((2 * everyone + 2 + n_row,))]
        + [pltpu.SemaphoreType.DMA((5,))],
        compiler_params=pltpu.CompilerParams(
            collective_id=collective_id, has_side_effects=True, vmem_limit_bytes=58 * MEGA
        ),
    )(table_over, over_cols, over_rows, old_lines, *grads)


def update_kernel(table_ref, table_grad_ref, rows_ref, all_rows_ref, factor_ref, lines_ref, *refs):
    weights, grads, (table_new_ref, table_rows_ref, table_cols_ref) = refs[:5], refs[5:10], refs[10:13]
    rows_outs, cols_outs, news = refs[13:18], refs[18:23], refs[23:28]
    held_weights, held_grads, (load_sems, store_sems) = refs[28:33], refs[33:38], refs[38:]
    at, last = pl.program_id(0), pl.num_programs(0) - 1
    loads = [
        pltpu.make_async_copy(source, target, load_sems.at[k])
        for k, (source, target) in enumerate(zip(weights + grads, held_weights + held_grads))
    ]
    stores = [pltpu.make_async_copy(held_weights[k], news[k], store_sems.at[k]) for k in range(5)]

    @pl.when(at == 0)
    def _():
        for load in loads:
            load.start()
        limit = table_rows_ref.shape[0]
        line = jnp.concatenate([all_rows_ref[k] for k in range(all_rows_ref.shape[0])], 1)
        table_rows_ref[...] = line[:, :limit].reshape(limit)
        table_cols_ref[...] = factor_ref[0:1].reshape(table_cols_ref.shape)

    factors = factor_ref[1:2] * factor_ref[2:3, 5:6]
    for k in range(BLOCK // ROWS):
        part = slice(k * ROWS, (k + 1) * ROWS)
        rows = turned(lax.rsqrt(rows_ref[k]), 128)[:, :1]
        table_new_ref[part] = table_ref[part] - table_grad_ref[part] * rows * factors

    @pl.when(at == last - 1)
    def _():
        for load in loads:
            load.wait()
        for index in range(5):
            count_rows, count_cols = held_weights[index].shape
            rows_line = lines_ref[index : index + 1, :count_rows]
            cols_line = lines_ref[8 + index : 9 + index, :count_cols]
            rows_outs[index][...] = rows_line.reshape(count_rows)
            cols_outs[index][...] = cols_line.reshape(count_cols)
            rows = turned(lax.rsqrt(rows_line), 128)[:, :1]
            factors = factor_ref[2:3, index : index + 1] * lax.rsqrt(cols_line)
            held_weights[index][...] = held_weights[index][...] - held_grads[index][...] * rows * factors
            stores[index].start()

    @pl.when(at == last)
    def _():
        for store in stores:
            store.wait()


def update(table, table_grad, table_rows, factors, lines, weights, grads):
    limit, width = table.shape
    shape = lambda dims: jax.ShapeDtypeStruct(dims, F32)
    small_shapes = [(limit,), (width,)] + [item.shape[:1] for item in weights] + [item.shape[1:] for item in weights]
    matrix_shapes = [item.shape for item in weights]
    hbm = pl.BlockSpec(memory_space=pl.ANY)
    out = pl.pallas_call(
        update_kernel,
        grid=(blocks_of(limit),),
        out_shape=[shape(table.shape)] + [shape(dims) for dims in small_shapes + matrix_shapes],
        in_specs=[row_block(width), row_block(width), line_block(ROWS, BLOCK // ROWS), whole_block(table_rows.shape)]
        + [whole_block(factors.shape), whole_block(lines.shape)]
        + [hbm] * 10,
        out_specs=[row_block(width)] + [whole_block(dims) for dims in small_shapes] + [hbm] * 5,
        scratch_shapes=[pltpu.VMEM(dims, F32) for dims in matrix_shapes * 2]
        + [pltpu.SemaphoreType.DMA((10,)), pltpu.SemaphoreType.DMA((5,))],
        compiler_params=pltpu.CompilerParams(vmem_limit_bytes=58 * MEGA),
        cost_estimate=cost(0, 3 * 4 * limit * width),
    )(table, table_grad, table_rows, table_rows, factors, lines, *weights, *grads)
    return out[0], out[1], out[2], out[3:8], out[8:13], out[13:]


HIDDEN = 1024
CHUNK = 512


def normed_of(inputs):
    center = jnp.mean(inputs, -1, keepdims=True)
    var = jnp.mean(inputs * inputs, -1, keepdims=True) - center * center
    inv = lax.rsqrt(var + 1e-05)
    return (inputs - center) * inv, inv


def normed_back(upstream, normed, inv, gain):
    scaled = upstream * gain
    first = jnp.mean(scaled, -1, keepdims=True)
    second = jnp.mean(scaled * normed, -1, keepdims=True)
    return inv * (scaled - first - normed * second)


def columns_sum(item):
    return jnp.sum(item.astype(F32), 0, keepdims=True)


def chunks_of(length):
    return [slice(at, at + CHUNK) for at in range(0, length, CHUNK)]


GELU_SCALE = (2.0 / jnp.pi) ** 0.5


def gelu_parts(inputs):
    square = inputs * inputs
    turn = jnp.tanh(inputs * (GELU_SCALE + (GELU_SCALE * 0.044715) * square))
    half = 0.5 + 0.5 * turn
    inner = GELU_SCALE + (3.0 * GELU_SCALE * 0.044715) * square
    return inputs * half, half + 0.5 * inputs * (1.0 - turn * turn) * inner


def first_kernel(start_ref, weight_ref, bias_ref, small_ref, packed_ref, ones_ref):
    @pl.when(pl.program_id(0) == 0)
    def _():
        for rows in chunks_of(start_ref.shape[0]):
            normed = normed_of(start_ref[rows].astype(F32))[0]
            ones_ref[rows] = (normed * small_ref[0:1] + small_ref[1:2]).astype(BF16)

    for rows in chunks_of(start_ref.shape[0]):
        packed_ref[rows] = (mm(ones_ref[rows], weight_ref[...]) + bias_ref[...]).astype(BF16)


def first_forward(start, weight, bias, small):
    length, width = start.shape
    shape = jax.ShapeDtypeStruct
    return pl.pallas_call(
        first_kernel,
        grid=(weight.shape[1] // width,),
        out_shape=[shape((length, weight.shape[1]), BF16), shape((length, width), BF16)],
        in_specs=[whole_block(start.shape), pl.BlockSpec((width, width), lambda i: (0, i))]
        + [pl.BlockSpec((1, width), lambda i: (0, i)), whole_block(small.shape)],
        out_specs=[pl.BlockSpec((length, width), lambda i: (0, i)), whole_block((length, width))],
        cost_estimate=cost(2 * length * width * weight.shape[1], 4 * length * weight.shape[1]),
        compiler_params=pltpu.CompilerParams(vmem_limit_bytes=40 * MEGA),
    )(start, weight, bias, small)


def middle_kernel(start_ref, mixed_ref, attn_ref, up_ref, bias_ref, down_ref, small_ref, *outs):
    mid_ref, low_ref, out_ref, z_ref, total = outs
    at = pl.program_id(0)
    length = start_ref.shape[0]

    @pl.when(at == 0)
    def _():
        for rows in chunks_of(length):
            mid = start_ref[rows].astype(F32) + mm(mixed_ref[rows], attn_ref[...]) + small_ref[4:5]
            mid_ref[rows] = mid
            low_ref[rows] = (normed_of(mid)[0] * small_ref[5:6] + small_ref[6:7]).astype(BF16)
            total[rows] = mid + small_ref[11:12]

    chunks = chunks_of(length)
    later = mm(low_ref[chunks[0]], up_ref[...])
    for k, rows in enumerate(chunks):
        product = later
        if k + 1 < len(chunks):
            later = mm(low_ref[chunks[k + 1]], up_ref[...])
        hidden = gelu_parts(product + bias_ref[...])[0].astype(BF16)
        total[rows] += mm_nt(hidden, down_ref[...])

    @pl.when(at == pl.num_programs(0) - 1)
    def _():
        for rows in chunks_of(length):
            out = total[rows]
            out_ref[rows] = out
            z_ref[rows] = (normed_of(out)[0] * small_ref[12:13] + small_ref[13:14]).astype(BF16)


def middle_forward(start, mixed, attn, up, up_bias, down, small):
    length, width = start.shape
    shape = jax.ShapeDtypeStruct
    whole = lambda item: whole_block(item.shape)
    tokens = whole_block((length, width))
    return pl.pallas_call(
        middle_kernel,
        grid=(up.shape[1] // HIDDEN,),
        out_shape=[shape((length, width), kind) for kind in (F32, BF16, F32, BF16)],
        in_specs=[whole(start), whole(mixed), whole(attn), pl.BlockSpec((width, HIDDEN), lambda i: (0, i))]
        + [pl.BlockSpec((1, HIDDEN), lambda i: (0, i)), pl.BlockSpec((width, HIDDEN), lambda i: (0, i))]
        + [whole(small)],
        out_specs=[tokens] * 4,
        scratch_shapes=[pltpu.VMEM((length, width), F32)],
        cost_estimate=cost(4 * length * width * up.shape[1], 16 * length * width),
        compiler_params=pltpu.CompilerParams(vmem_limit_bytes=56 * MEGA),
    )(start, mixed, attn, up, up_bias, down, small)


def middle_back_kernel(*refs):
    grad_ref, out_ref, mid_ref, low_ref, attn_ref, up_ref, bias_ref, down_ref, small_ref = refs[:9]
    down_grad_ref, pre_ref, act_ref, pre_sum_ref, mid_grad_ref, branch_ref, mixed_ref, rows_ref, total = refs[9:]
    at = pl.program_id(0)
    length, width = grad_ref.shape

    @pl.when(at == 0)
    def _():
        rows_ref[...] = jnp.zeros_like(rows_ref)
        for rows in chunks_of(length):
            grad = grad_ref[rows].astype(F32)
            normed, inv = normed_of(out_ref[rows])
            back = normed_back(grad, normed, inv, small_ref[12:13])
            mid_grad_ref[rows] = back
            low = back.astype(BF16)
            down_grad_ref[rows] = low
            rows_ref[0:1] += columns_sum(grad * normed)
            rows_ref[1:2] += columns_sum(grad)
            rows_ref[2:3] += columns_sum(low)
        total[...] = jnp.zeros_like(total)

    pre_sum = jnp.zeros((1, pre_ref.shape[1]), F32)
    for rows in chunks_of(length):
        act, slope = gelu_parts(mm(low_ref[rows], up_ref[...]) + bias_ref[...])
        act_ref[rows] = act.astype(BF16)
        pre = (mm(down_grad_ref[rows], down_ref[...]) * slope).astype(BF16)
        pre_ref[rows] = pre
        pre_sum = pre_sum + columns_sum(pre)
        total[rows] += mm_nt(pre, up_ref[...])
    pre_sum_ref[...] = pre_sum

    @pl.when(at == pl.num_programs(0) - 1)
    def _():
        for rows in chunks_of(length):
            grad = total[rows]
            normed, inv = normed_of(mid_ref[rows])
            mid_grad = mid_grad_ref[rows] + normed_back(grad, normed, inv, small_ref[5:6])
            mid_grad_ref[rows] = mid_grad
            low = mid_grad.astype(BF16)
            branch_ref[rows] = low
            rows_ref[3:4] += columns_sum(grad * normed)
            rows_ref[4:5] += columns_sum(grad)
            rows_ref[5:6] += columns_sum(low)
            mixed_ref[rows] = mm_nt(low, attn_ref[...]).astype(BF16)


def middle_back(grad, out, mid, low, attn, up, up_bias, down, small):
    length, width = grad.shape
    hidden = up.shape[1]
    shape = jax.ShapeDtypeStruct
    whole = lambda item: whole_block(item.shape)
    tokens = whole_block((length, width))
    wide = pl.BlockSpec((length, HIDDEN), lambda i: (0, i))
    weight = pl.BlockSpec((width, HIDDEN), lambda i: (0, i))
    line = pl.BlockSpec((1, HIDDEN), lambda i: (0, i))
    return pl.pallas_call(
        middle_back_kernel,
        grid=(hidden // HIDDEN,),
        out_shape=[shape((length, width), BF16), shape((length, hidden), BF16), shape((length, hidden), BF16)]
        + [shape((1, hidden), F32), shape((length, width), F32), shape((length, width), BF16)]
        + [shape((length, width), BF16), shape((8, width), F32)],
        in_specs=[tokens] * 4 + [whole(attn), weight, line, weight, whole(small)],
        out_specs=[tokens, wide, wide, line, tokens, tokens, tokens, whole_block((8, width))],
        scratch_shapes=[pltpu.VMEM((length, width), F32)],
        cost_estimate=cost(6 * length * width * hidden, 40 * length * width),
        compiler_params=pltpu.CompilerParams(vmem_limit_bytes=58 * MEGA),
    )(grad, out, mid, low, attn, up, up_bias, down, small)


def start_back_kernel(packed_ref, weight_ref, mid_grad_ref, start_ref, small_ref, out_ref, low_ref, wide_ref, rows_ref):
    width = start_ref.shape[1]
    grad = sum(mm_nt(packed_ref[k], weight_ref[:, k * width : (k + 1) * width]) for k in range(3))
    normed, inv = normed_of(start_ref[...].astype(F32))
    back = mid_grad_ref[...] + normed_back(grad, normed, inv, small_ref[0:1])
    out_ref[...] = back
    low_ref[...] = back.astype(BF16)
    wide_ref[...] = back.astype(BF16).astype(F32)

    @pl.when(pl.program_id(0) == 0)
    def _():
        rows_ref[...] = jnp.zeros_like(rows_ref)

    rows_ref[0:1] += columns_sum(grad * normed)
    rows_ref[1:2] += columns_sum(grad)
    rows_ref[2:3] += columns_sum(packed_ref[0])
    rows_ref[3:4] += columns_sum(packed_ref[2])
    rows_ref[4:5] += columns_sum(back * back)


def start_back(packed_grad, weight, mid_grad, start, small):
    length, width = start.shape
    shape = jax.ShapeDtypeStruct
    tokens = pl.BlockSpec((CHUNK, width), lambda i: (i, 0))
    return pl.pallas_call(
        start_back_kernel,
        grid=(length // CHUNK,),
        out_shape=[shape((length, width), kind) for kind in (F32, BF16, F32)] + [shape((8, width), F32)],
        in_specs=[pl.BlockSpec((3, CHUNK, width), lambda i: (0, i, 0)), whole_block(weight.shape), tokens, tokens]
        + [whole_block(small.shape)],
        out_specs=[tokens, tokens, tokens, whole_block((8, width))],
        cost_estimate=cost(6 * length * width * width, 20 * length * width),
        compiler_params=pltpu.CompilerParams(vmem_limit_bytes=56 * MEGA),
    )(packed_grad, weight, mid_grad, start, small)


def weight_grads_kernel(place_ref, ones_ref, mixed_ref, low_ref, *refs):
    packed, (branch_ref, pre_ref, down_ref, act_ref, grad_ref, small_ref) = refs[:3], refs[3:9]
    out_ref, square_ref, wide, turned_grad = refs[9:]
    width = ones_ref.shape[1]
    tall = width // 4
    start = pl.multiple_of(place_ref[0], 128)
    skip = pl.multiple_of(place_ref[1], 8)
    pieces = (
        (ones_ref, ((packed[0], 0, 0), (packed[1], 0, 1), (packed[2], 1, 0))),
        (mixed_ref, ((branch_ref, 1, 1),)),
        (low_ref, ((pre_ref, 2, 0), (pre_ref, 2, 1), (pre_ref, 3, 0), (pre_ref, 3, 1))),
    )
    half = width // 2
    square = jnp.zeros((1, half), F32)
    for left_ref, rights in pieces:
        left = left_ref[:, pl.ds(start, SIDE)].T
        for k, (right_ref, piece, side) in enumerate(rights):
            right = right_ref[0] if len(right_ref.shape) == 3 else right_ref[:, pl.ds(k * half, half)]
            wide[...] = mm(left, right)
            grad = wide[pl.ds(skip, tall), :]
            out_ref[piece * tall : (piece + 1) * tall, side * half : (side + 1) * half] = grad
            square = square + jnp.sum(grad * grad, 0, keepdims=True)
    left = down_ref[...].T
    first = 4 * tall
    for side in range(2):
        grad = mm(left, act_ref[:, side * half : (side + 1) * half])
        out_ref[first : first + half, side * half : (side + 1) * half] = grad
        square = square + jnp.sum(grad * grad, 0, keepdims=True)
    square_ref[...] = square
    first += half
    turned_grad[...] = grad_ref[:, pl.ds(start, SIDE)].T
    out_ref[first:, :] = jnp.zeros((out_ref.shape[0] - first, width), F32)
    out_ref[first : first + tall, : grad_ref.shape[0]] = turned_grad[pl.ds(skip, tall), :]
    first += tall
    out_ref[first : first + small_ref.shape[0], :] = small_ref[...]


def weight_grads(ln_one, mixed, low, packed_grad, branch, pre, down_grad, act, grad_in, small_ex, row_at, col_at):
    length, width = ln_one.shape
    half, tall = width // 2, width // 4
    hidden, tokens = pre.shape[1] // 2, length // 2
    shape = jax.ShapeDtypeStruct
    first = row_at * tall
    place = jnp.stack([first // 128 * 128, first % 128, row_at, col_at]).astype(jnp.int32)
    unit = lambda k: pl.BlockSpec((1, length, half), lambda i, at: ((3 * at[3] + k) // 2, 0, (3 * at[3] + k) % 2))
    by_col = lambda size: pl.BlockSpec((length, size), lambda i, at: (0, at[3]))
    lines = 5 * tall + half + 32
    return pl.pallas_call(
        weight_grads_kernel,
        grid_spec=pltpu.PrefetchScalarGridSpec(
            num_scalar_prefetch=1,
            grid=(1,),
            in_specs=[whole_block((length, width))] * 3
            + [unit(k) for k in range(3)]
            + [by_col(half), by_col(hidden), by_col(half), pl.BlockSpec((length, width), lambda i, at: (0, at[2]))]
            + [pl.BlockSpec((tokens, width), lambda i, at: (at[3], 0)), whole_block(small_ex.shape)],
            out_specs=[whole_block((lines, width)), whole_block((1, half))],
            scratch_shapes=[pltpu.VMEM((SIDE, half), F32), pltpu.VMEM((SIDE, tokens), F32)],
        ),
        out_shape=[shape((lines, width), F32), shape((1, half), F32)],
        cost_estimate=cost(2 * length * width * width * 2, 16 * length * width),
        compiler_params=pltpu.CompilerParams(vmem_limit_bytes=56 * MEGA),
    )(place, ln_one, mixed, low, packed_grad, packed_grad, packed_grad, branch, pre, down_grad, act, grad_in, small_ex)


def body(
    token_ids,
    target_ids,
    included,
    tok_table,
    pos_table,
    qkv_weight,
    attn_weight,
    up_weight,
    down_weight,
    small_params,
    table_rows,
    table_cols,
    pos_rows,
    pos_cols,
    qkv_rows,
    qkv_cols,
    attn_rows,
    attn_cols,
    up_rows,
    up_cols,
    down_rows,
    down_cols,
    small_second,
    table_noise,
    pos_noise,
    qkv_noise,
    attn_noise,
    up_noise,
    down_noise,
    small_noise,
):
    n_row = lax.axis_size("row")
    n_col = lax.axis_size("col")
    n_data = lax.axis_size("dp")
    row_at = lax.axis_index("row")
    col_at = lax.axis_index("col")
    ids, targets = token_ids[0], target_ids[0]
    length = ids.shape[0]
    width = small_params.shape[1]
    vocab_here = tok_table.shape[0]
    vocab_start = (col_at * n_row + row_at) * vocab_here
    small = small_params

    target = targets - vocab_start
    target = jnp.where((target >= 0) & (target < vocab_here), target, -1)[None]
    lists = token_lists(ids, vocab_start, vocab_here)
    tuned = (n_data, n_row, n_col) == (4, 4, 2)
    block = length // (n_row * n_col)
    if tuned:
        beside = lambda item: lax.ppermute(item, "dp", [(at, at ^ 2) for at in range(4)])
        met_ids, met_target = beside(jnp.stack([ids, targets]))
        met_target = met_target - vocab_start
        met_target = jnp.where((met_target >= 0) & (met_target < vocab_here), met_target, -1)[None]
        met_lists = token_lists(met_ids, vocab_start, vocab_here)

    weights_in = [tok_table, pos_table, qkv_weight, attn_weight, up_weight, down_weight]
    noises = [table_noise, pos_noise, qkv_noise, attn_noise, up_noise, down_noise]
    lows = [item.astype(BF16) for item in weights_in[2:]]
    if tuned:
        shards = [item.reshape(n_data, -1, item.shape[1]) for item in lows]
        start, table_low, table_sq, qkv_full, attn_full, up_full, down_full = front(
            ids, tok_table, pos_table.T, shards, n_row
        )
        stream_in = start.reshape(length, width)
        qkv_full, attn_full, up_full, down_full = (
            item.reshape(width, -1) for item in (qkv_full, attn_full, up_full, down_full)
        )
    else:
        local_ids = ids - vocab_start
        inside = (local_ids >= 0) & (local_ids < vocab_here)
        safe_ids = jnp.clip(local_ids, 0, vocab_here - 1)
        looked = jnp.where(inside[:, None], jnp.take(tok_table, safe_ids, axis=0), 0.0).astype(BF16)
        table_sq = jnp.sum(tok_table * tok_table, 0, keepdims=True)
        table_low = jnp.pad(tok_table.astype(BF16), ((0, blocks_of(vocab_here) * BLOCK - vocab_here), (0, 0)))
        stream_in = (plane_sum(looked).astype(F32) + gather_matrix(pos_table, 1)).astype(BF16)
        qkv_full, attn_full, up_full = (gather_matrix(item, 0) for item in lows[:3])
        down_full = gather_matrix(lows[3], 1)

    bias = jnp.concatenate([small[2:3], jnp.zeros_like(small[2:3]), small[3:4]], 1)
    packed, ln_one = first_forward(stream_in, qkv_full, bias, small)
    mixed, attn_log = attend(packed)
    up_bias = small[7:11].reshape(1, -1)
    stream_mid, ln_two, stream_out, ln_fin = middle_forward(
        stream_in, mixed, attn_full, up_full, up_bias, down_full, small
    )

    exps, tops, exp_sums, picked = head(table_low, vocab_here, ln_fin, target)
    if tuned:
        met_z = beside(ln_fin)
        log_norm, picked = log_total(tops, exp_sums, picked, n_row, 3)
        met_log = beside(log_norm)
    else:
        top = lax.pmax(jnp.max(tops, 0), PLANE)
        log_norm = top + jnp.log(plane_sum(jnp.sum(exp_sums * jnp.exp(tops - top[None]), 0)))
        picked = plane_sum(picked)
    loss = jnp.sum(log_norm - picked)
    final_part, table_ex = head_back(exps, tops, log_norm, target, table_low, ln_fin)
    if tuned:
        final_part = plane_total(final_part.reshape(n_col, n_row, block, width), 2)
        final_grad = final_part.reshape(length, width)
    else:
        final_grad = plane_sum(final_part)

    down_grad, pre_grad, up_act, pre_sum, mid_grad, branch_grad, mixed_grad, mid_rows = middle_back(
        final_grad, stream_out, stream_mid, ln_two, attn_full, up_full, up_bias, down_full, small
    )
    packed_grad = attend_back(packed, mixed_grad, attn_log)
    grad_in, emb_low, emb_grad, start_rows = start_back(packed_grad, qkv_full, mid_grad, stream_in, small)
    small_ex = jnp.concatenate(
        [start_rows[:4], mid_rows[5:6], mid_rows[3:5], pre_sum.reshape(-1, width), mid_rows[2:3], mid_rows[:2]], 0
    )
    if tuned:
        met_grad = beside(emb_low)
        packed_ex, layer_sq = weight_grads(
            ln_one,
            mixed,
            ln_two,
            packed_grad,
            branch_grad,
            pre_grad,
            down_grad,
            up_act,
            grad_in,
            small_ex,
            row_at,
            col_at,
        )
        layer_sq = jnp.sum(layer_sq)
    else:
        tok_here, dim_here = pos_table.shape
        pos_ex = lax.dynamic_slice(grad_in, (col_at * tok_here, row_at * dim_here), (tok_here, dim_here))
        all_grads = packed_grad.transpose(1, 0, 2).reshape(length, -1)

        def columns_of(array, at, parts):
            size = array.shape[1] // parts
            return lax.dynamic_slice_in_dim(array, at * size, size, 1)

        layer_ex = [
            mm_tn(columns_of(left, at_left, n_left), columns_of(right, at_right, n_right))
            for left, at_left, n_left, right, at_right, n_right in (
                (ln_one, row_at, n_row, all_grads, col_at, n_col),
                (mixed, row_at, n_row, branch_grad, col_at, n_col),
                (ln_two, row_at, n_row, pre_grad, col_at, n_col),
                (down_grad, col_at, n_col, up_act, row_at, n_row),
            )
        ]
        layer_sq = sum(jnp.sum(item * item) for item in layer_ex)
    table_ex, own_sq = add_own_rows(table_ex, lists, emb_grad)

    own_sq = jnp.sum(own_sq) + layer_sq
    same_sq = jnp.sum(start_rows[4]) + jnp.sum(small_ex * small_ex)
    taken = included[0].astype(F32)
    ex_at = lax.axis_index("dp")
    leads = (row_at + col_at == 0).astype(F32)
    at_own = (jnp.arange(n_data) == ex_at).astype(F32)
    total = jnp.concatenate([at_own * (own_sq + leads * same_sq), at_own * leads * taken, leads * taken * loss[None]])
    if tuned:
        total = jnp.pad(total, (0, 1024 - total.shape[0])).reshape(8, 128)
        total, met_grad = lax.optimization_barrier((total, met_grad))
        total = sum_small(total, n_row, 4).reshape(-1)
    else:
        total = lax.psum(lax.psum(total, PLANE), "dp")
    norm_sq, taken, loss_sum = total[:n_data], total[n_data : 2 * n_data], total[2 * n_data]
    share = taken * jnp.minimum(1.0, CLIP * lax.rsqrt(norm_sq + 1e-12))
    example_norm = jnp.sqrt(norm_sq[ex_at])
    own_share = share[ex_at]

    divisor = SAMPLE * n_data
    vocab = vocab_here * n_row * n_col
    count = blocks_of(vocab_here)
    table_old = jnp.pad(table_rows, (0, count * BLOCK - vocab_here), constant_values=1.0).reshape(-1, 1, ROWS)
    fine = BLOCK // ROWS
    olds = [(pos_rows, pos_cols), (qkv_rows, qkv_cols), (attn_rows, attn_cols), (up_rows, up_cols)]
    olds.append((down_rows, down_cols))
    ends = (token_ids.shape[1] * jnp.sum(taken), example_norm[None])
    if tuned:
        core = ex_at % 2
        to_core = lambda item: lax.ppermute(item, "dp", [(at, at ^ 1) for at in range(4)])
        halves = (own_share * packed_ex).astype(BF16).reshape(2, -1, width)
        half = (halves[core].astype(F32) + to_core(halves[1 - core]).astype(F32)).astype(BF16)
        shares = jnp.stack([own_share, share[ex_at ^ 2]])
        half, shares = lax.optimization_barrier((half, shares))
        from_beside = beside(half)
        middle = count // 2
        spans = [(0, middle), (middle, count - middle)]
        met = (met_z, met_log, met_target, met_lists, met_grad.astype(F32), shares)
        pair_sums = [table_sum(table_ex, table_low, *met, *span) for span in spans]
        pair_sums = [[item, to_core(item)] for item in pair_sums]
        into, over = None, []
        for pair, span in zip(pair_sums, spans):
            *into, cols, scaled, level = table_gradient(
                pair, table_noise, table_old, divisor, span[0] * fine, span[1] * fine, into
            )
            over.append((cols, scaled, level))
        table_grad, rows_blocks = into
        half = join(half, from_beside, cols)
        other_half = to_core(half)
        cols, scaled, level = (over[0][k] + over[1][k] for k in range(3))
        turn = lambda items: [items[1].T] + list(items[2:])
        matrices, matrix_noises = turn(weights_in), turn(noises)
        olds[0] = olds[0][::-1]
        small_grads, smalls, (over_cols, over_rows, squares) = small_gradients(
            core[None], half, other_half, small_params, small_second, small_noise, matrices, matrix_noises, divisor
        )
        scalars = jnp.where(jnp.arange(128) == 5, jnp.sum(table_sq), squares[0])
        table_over = jnp.concatenate([cols[0], scaled[0], scalars, level[0]]).reshape(-1, 128)
        table_over = jnp.pad(table_over, ((0, -table_over.shape[0] % 8), (0, 0)))
        wide = max(item.shape[0] for pair in olds for item in pair)
        lines = [jnp.pad(item, (0, wide - item.shape[0])) for pair in zip(*olds) for item in pair + (table_cols,) * 3]
        old_lines = jnp.stack(lines)
        lines, factors = statistics(
            table_over, over_cols, over_rows, old_lines, small_grads, width, n_row, vocab, 5
        )
        table_new, table_rows_new, table_cols_new, rows_new, cols_new, news = update(
            tok_table, table_grad, rows_blocks, factors, lines, matrices, small_grads
        )
        outputs = [table_grad, table_rows_new, table_cols_new, table_new]
        outputs.extend([small_grads[0].T, cols_new[0], rows_new[0], news[0].T])
        for group in zip(small_grads[1:], rows_new[1:], cols_new[1:], news[1:]):
            outputs.extend(group)
        return tuple(outputs) + tuple(smalls) + (loss_sum,) + ends

    weight_total = plane_sum(
        jnp.stack([jnp.sum(table_sq)] + [jnp.sum(item * item) for item in weights_in[1:]])
    )
    table_sum_all = example_sum((own_share * table_ex.astype(F32)).astype(BF16))
    others = [(own_share * item).astype(BF16) for item in [pos_ex] + layer_ex + [small_ex]]
    sums = [example_sum(item).astype(F32) for item in others]
    grads = [(sums[index] + NOISE * CLIP * noises[index + 1]) / divisor for index in range(5)]
    table_grad, table_rows_new, *table_over = table_gradient(
        [table_sum_all], table_noise, table_old, divisor, 0, pl.cdiv(vocab_here, ROWS)
    )
    table_rows_new = table_rows_new.reshape(-1)[:vocab_here]
    by_row = [False, True, True, True, False]
    over = {"col": [], "row": []}
    for grad, first in zip(grads, by_row):
        squares = grad * grad + 1e-30
        over["col" if first else "row"].append(jnp.sum(squares, 1))
        over["row" if first else "col"].append(jnp.sum(squares, 0))
    over = {axis: [lax.psum(item, axis) for item in items] for axis, items in over.items()}
    table_over = [plane_sum(item[0]) for item in table_over]
    news, levels = [], []
    for index, (grad, first) in enumerate(zip(grads, by_row)):
        rows_parts, cols_parts = (n_row, n_col) if first else (n_col, n_row)
        row_sum = over["col" if first else "row"][index]
        col_sum = over["row" if first else "col"][index]
        rows_new = DECAY * olds[index][0] + (1.0 - DECAY) * (row_sum / (grad.shape[1] * cols_parts))
        cols_new = DECAY * olds[index][1] + (1.0 - DECAY) * (col_sum / (grad.shape[0] * rows_parts))
        news.append((rows_new, cols_new))
        levels += [
            jnp.sum(rows_new) / (grad.shape[0] * rows_parts * cols_parts),
            jnp.sum(grad * grad / (rows_new[:, None] * cols_new[None, :])),
        ]
    levels = plane_sum(jnp.stack(levels))

    def updated(index, weight, grad, rows_new, cols_new, level, square_sum, entries_all):
        size = RATE * jnp.maximum(1e-3, jnp.sqrt(weight_total[index] / entries_all))
        size = size / jnp.maximum(1.0, jnp.sqrt(square_sum * level / entries_all))
        size = size * jnp.sqrt(level)
        return weight - grad * lax.rsqrt(rows_new)[:, None] * (size * lax.rsqrt(cols_new))[None, :]

    table_cols_new = DECAY * table_cols + (1.0 - DECAY) * (table_over[0] / vocab + 1e-30)
    table_new = updated(
        0,
        tok_table,
        table_grad,
        table_rows_new,
        table_cols_new,
        table_over[2][0] / vocab,
        jnp.sum(table_over[1] / table_cols_new),
        vocab * width,
    )
    outputs = [table_grad, table_rows_new, table_cols_new, table_new]
    for index, grad in enumerate(grads):
        rows_new, cols_new = news[index]
        weight_new = updated(
            index + 1,
            weights_in[index + 1],
            grad,
            rows_new,
            cols_new,
            levels[2 * index],
            levels[2 * index + 1],
            grad.shape[0] * grad.shape[1] * n_row * n_col,
        )
        outputs.extend([grad, rows_new, cols_new, weight_new])
    small_grad = (sums[5] + NOISE * CLIP * small_noise) / divisor
    second_new = DECAY * small_second + (1.0 - DECAY) * (small_grad * small_grad + 1e-30)
    small_update = small_grad * lax.rsqrt(second_new)
    small_update = small_update / jnp.maximum(1.0, jnp.sqrt(jnp.mean(small_update * small_update)))
    small_size = RATE * jnp.maximum(1e-3, jnp.sqrt(jnp.mean(small_params * small_params)))
    small_new = small_params - small_size * small_update
    return tuple(outputs) + (small_grad, second_new, small_new, loss_sum) + ends


def solution(mesh):
    table, by_col, by_row = P(("col", "row"), None), P("col", "row"), P("row", "col")
    return jax.shard_map(
        body,
        mesh=mesh,
        in_specs=(P("dp", None), P("dp", None), P("dp"))
        + (table, by_col, by_row, by_row, by_row, by_col, P())
        + (P(("col", "row")), P(), P("col"), P("row"))
        + (P("row"), P("col")) * 3
        + (P("col"), P("row"), P())
        + (table, by_col, by_row, by_row, by_row, by_col, P()),
        out_specs=(table, P(("col", "row")), P(), table)
        + (by_col, P("col"), P("row"), by_col)
        + (by_row, P("row"), P("col"), by_row) * 3
        + (by_col, P("col"), P("row"), by_col)
        + (P(), P(), P(), P(), P(), P("dp")),
        check_vma=False,
    )
```
